512 devices in a mesh: event: 32 (over z, core), mesh: 16 (over x, y).
Axes of the slice: x: 4, y: 4, z: 16, core: 2. Of those that a mesh axis runs over, the one named last changes fastest.
Arguments:
- forward_start: float32 [32, 3, 125, 2048], P('event', None, None, 'mesh'), may hold values from -6 to 6
- adjoint_start: float32 [32, 3, 125, 2048], P('event', None, None, 'mesh'), may hold values from -6 to 6
- stiffness: float32 [125, 125], replicated
- projection: float32 [125, 64], replicated, may hold values from -0.5 to 0.5
- material: float32 [32, 2048], P('event', 'mesh'), may hold values from 0.5 to 2
- neighbours: int32 [32, 6, 2048], P('event', None, 'mesh'), may hold values from 0 to 2047, as said below
- destinations: int32 [32, 2048], P('event', 'mesh'), may hold values from 0 to 2047
- counts: int32 [32, 16], P('event', 'mesh'), may hold values from 32 to 128, as said below
- smoothing: float32 [4, 2048], P(None, ('event', 'mesh')), may hold values from 0.02 to 0.12
Outputs:
- forward_final: float32 [32, 3, 125, 2048], P('event', None, None, 'mesh')
- tiles: float32 [64, 2048], P(None, ('event', 'mesh'))
The draws below stay inside these ranges and needn't reach their ends.
Inputs may be any that keep to these rules, and one draw needn't show every extreme that they name: `counts`: in every event one partition holds exactly 128 live elements and another exactly 32; live elements fill a partition's first slots. `neighbours`: A neighbour slot lies in the element's own partition, or in the previous or next partition of the same event (wrapping around), and then among that partition's first 32 slots.
All inputs are finite; a program needn't handle non-finite values.
Results may differ from the reference program's by a relative error of at most 0.0003.
Values sent between devices are 32-bit elements; how exact they have to be, the bound alone decides.
No kernel may reach another device: no remote copies, remote signals or barrier semaphores. Data moves between devices by JAX's collectives and lax.ppermute only.
A program may use at most 64 MiB of HBM per device.

```python
import math
import jax
import jax.numpy as jnp
from jax import lax

NODES = 125
KNODES = 64
COMP = 3
ECAP = 128
TILE_DEV = 4
STEPS = 2
BND = 32
EVENTS = 32
PARTITIONS = 16
ELEM = 2048
NTILE = 2048


def draw_stiffness(key, part):
    sample_key = jax.random.fold_in(key, 37)
    factor = jax.random.normal(sample_key, (NODES, NODES), jnp.float32)
    gram_matrix = jnp.dot(factor, factor.T, precision=lax.Precision.HIGHEST) / NODES
    return 0.25 * gram_matrix + 0.1 * jnp.eye(NODES, dtype=jnp.float32)


def draw_counts(key, part):
    first_key, second_key = jax.random.split(jax.random.fold_in(key, 11))
    drawn = jax.random.randint(first_key, (EVENTS, PARTITIONS), ECAP // 4, ECAP + 1)
    fullest = jax.random.randint(second_key, (EVENTS, 1), 0, PARTITIONS)
    columns = jnp.arange(PARTITIONS)[None, :]
    drawn = jnp.where(columns == fullest, ECAP, drawn)
    drawn = jnp.where(columns == (fullest + 1) % PARTITIONS, ECAP // 4, drawn)
    return drawn.astype(jnp.int32)


def draw_neighbours(key, part):
    side_key, near_key, far_key = jax.random.split(jax.random.fold_in(key, 23), 3)
    grid_shape = (EVENTS, 6, ELEM)
    which_side = jax.random.randint(side_key, grid_shape, 0, 4)
    near_slot = jax.random.randint(near_key, grid_shape, 0, ECAP)
    far_slot = jax.random.randint(far_key, grid_shape, 0, BND)
    partition = jnp.arange(ELEM)[None, None, :] // ECAP
    offset = jnp.where(which_side == 2, -1, jnp.where(which_side == 3, 1, 0))
    target = (partition + offset + PARTITIONS) % PARTITIONS
    local_slot = jnp.where(which_side >= 2, far_slot, near_slot)
    result = target * ECAP + local_slot
    result = result.at[:, 0, ELEM - 1].set(ELEM - 1)
    result = result.at[:, 1, 1].set(0)
    return result.astype(jnp.int32)


def with_ends(values, key, least, high):
    shape = values.shape
    place = [jax.random.randint(jax.random.fold_in(key, axis), (), 0, shape[axis]) for axis in range(len(shape))]
    values = values.at[tuple(place)].set(least)
    longest = shape.index(max(shape))
    place[longest] = (place[longest] + 1) % shape[longest]
    return values.at[tuple(place)].set(high)


def block_levels(own_key, dims, pieces, least, high):
    level, own = 1.0, jax.random.fold_in(own_key, 6)
    for axis_at, shards_of in pieces:
        steps = jnp.exp(jax.random.uniform(jax.random.fold_in(own, axis_at), (shards_of,), jnp.float32, least / len(pieces), high / len(pieces)))
        level = level * jnp.repeat(steps, dims[axis_at] // shards_of).reshape([-1 if axis == axis_at else 1 for axis in range(len(dims))])
    return level


def normal_values(stream_key, dims, spread, reach, pieces=(), held_as=jnp.bfloat16):
    level = block_levels(stream_key, dims, pieces, -0.22, 0.18) if pieces else 1.0
    values = jax.random.normal(stream_key, dims, jnp.float32) * spread * level
    return jnp.minimum(jnp.maximum(values, -reach), reach).astype(held_as)


def setup_inputs(seed: int = 0) -> dict:
    key_of = jax.random.split(jax.random.key(seed), 10)
    return {
        "forward_start": normal_values(key_of[0], (EVENTS, COMP, NODES, ELEM), 1.0, 6.0, ((0, 32), (3, 16)), jnp.float32),
        "adjoint_start": normal_values(key_of[1], (EVENTS, COMP, NODES, ELEM), 1.0, 6.0, ((0, 32), (3, 16)), jnp.float32),
        "stiffness": draw_stiffness(jax.random.fold_in(key_of[9], 71), 0),
        "projection": normal_values(key_of[3], (NODES, KNODES), NODES ** -0.5, 0.5, (), jnp.float32),
        "material": jnp.clip(jnp.exp(math.log(2.0) - 1.3862944 * jax.random.uniform(key_of[4], (EVENTS, ELEM), jnp.float32) ** block_levels(key_of[4], (EVENTS, ELEM), ((0, 32), (1, 16)), -0.2, 0.2)), 0.5, 2.0),
        "neighbours": draw_neighbours(jax.random.fold_in(key_of[9], 71), 0),
        "destinations": with_ends(jax.random.randint(key_of[6], (EVENTS, ELEM), 0, NTILE), jax.random.fold_in(key_of[6], 1), 0, NTILE - 1).astype(jnp.int32),
        "counts": draw_counts(jax.random.fold_in(key_of[9], 71), 0),
        "smoothing": jnp.clip(jnp.exp(math.log(0.12) - 1.7917595 * jax.random.uniform(key_of[8], (4, NTILE), jnp.float32) ** block_levels(key_of[8], (4, NTILE), ((1, 512),), -0.2, 0.2)), 0.02, 0.12),
    }


time_square = 0.4
penalty = 0.5
partner_face = (1, 0, 3, 2, 5, 4)

def element_faces(field):
    elements = field.shape[-1]
    cube = field.reshape(3, 5, 5, 5, elements)
    sheets = [cube[:, 0], cube[:, 4], cube[:, :, 0], cube[:, :, 4], cube[:, :, :, 0], cube[:, :, :, 4]]
    return jnp.stack(sheets).reshape(6, 3, 25, elements)

def lift_faces(jumps):
    elements = jumps.shape[-1]
    sheets = jumps.reshape(6, 3, 5, 5, elements)
    keep = (0, 0)
    lifted = jnp.pad(sheets[0][:, None], (keep, (0, 4), keep, keep, keep))
    lifted = lifted + jnp.pad(sheets[1][:, None], (keep, (4, 0), keep, keep, keep))
    lifted = lifted + jnp.pad(sheets[2][:, :, None], (keep, keep, (0, 4), keep, keep))
    lifted = lifted + jnp.pad(sheets[3][:, :, None], (keep, keep, (4, 0), keep, keep))
    lifted = lifted + jnp.pad(sheets[4][:, :, :, None], (keep, keep, keep, (0, 4), keep))
    lifted = lifted + jnp.pad(sheets[5][:, :, :, None], (keep, keep, keep, (4, 0), keep))
    return lifted.reshape(3, 125, elements)

def apply_stiffness(stiffness, field):
    return jnp.einsum('nm,cme->cne', stiffness, field, precision=lax.Precision.HIGHEST)

def pick_faces(faces, neighbour_rows):
    return jnp.stack([jnp.take(faces[partner_face[face]], neighbour_rows[face], axis=2) for face in range(6)])

def advance(field, previous, strain, across, own_faces, material_row, live):
    force = -material_row[None, None, :] * strain + penalty * lift_faces(across - own_faces)
    return live[None, None, :] * (2.0 * field - previous + time_square * force)

def node_laplace(values, coefs):
    width = values.shape[-1]
    cube = values.reshape(4, 4, 4, width)
    padded = jnp.pad(cube, ((1, 1), (1, 1), (1, 1), (0, 0)))
    first_dir = padded[2:, 1:-1, 1:-1] + padded[:-2, 1:-1, 1:-1] - 2.0 * cube
    second_dir = padded[1:-1, 2:, 1:-1] + padded[1:-1, :-2, 1:-1] - 2.0 * cube
    third_dir = padded[1:-1, 1:-1, 2:] + padded[1:-1, 1:-1, :-2] - 2.0 * cube
    summed = coefs[0] * first_dir + coefs[1] * second_dir + coefs[2] * third_dir
    return summed.reshape(64, width)

def smooth_columns(values, coefs):
    middle = values[:, 1:-1]
    chain = values[:, :-2] + values[:, 2:] - 2.0 * middle
    return middle + coefs[0] * chain + node_laplace(middle, coefs[1:])

def reference(forward_start, adjoint_start, stiffness, projection, material, neighbours, destinations, counts, smoothing):
    scale = math.sqrt(TILE_DEV / ECAP) / STEPS

    def one_event(summed, inputs):
        forward_row, adjoint_row, material_row, neighbour_rows, destination_row, count_row = inputs
        slots = jnp.arange(ECAP, dtype=jnp.int32)
        live = (slots[None, :] < count_row[:, None]).reshape(ELEM).astype(jnp.float32)
        forward = forward_row * live[None, None, :]
        adjoint = adjoint_row * live[None, None, :]
        forward_prev, adjoint_prev = (forward, adjoint)
        kernel = jnp.zeros((NODES, ELEM), jnp.float32)
        for step_index in range(STEPS):
            strain_forward = apply_stiffness(stiffness, forward)
            strain_adjoint = apply_stiffness(stiffness, adjoint)
            kernel = kernel + lax.optimization_barrier(jnp.sum(forward * strain_adjoint, axis=0))
            faces_forward = element_faces(forward)
            faces_adjoint = element_faces(adjoint)
            across_forward = pick_faces(faces_forward, neighbour_rows)
            across_adjoint = pick_faces(faces_adjoint, neighbour_rows)
            next_forward = advance(forward, forward_prev, strain_forward, across_forward, faces_forward, material_row, live)
            next_adjoint = advance(adjoint, adjoint_prev, strain_adjoint, across_adjoint, faces_adjoint, material_row, live)
            forward_prev, forward = (forward, next_forward)
            adjoint_prev, adjoint = (adjoint, next_adjoint)
        blocks = jnp.dot(projection.T, kernel, precision=lax.Precision.HIGHEST) * scale
        summed = summed.at[:, destination_row].add(blocks)
        return (summed, forward)
    summed, finals = lax.scan(one_event, jnp.zeros((KNODES, NTILE), jnp.float32), (forward_start, adjoint_start, material, neighbours, destinations, counts))
    tiles = summed
    for pass_index in range(2):
        padded = jnp.pad(tiles, ((0, 0), (1, 1)))
        tiles = smooth_columns(padded, smoothing)
    return (finals, tiles)
```

```python
import math

import jax
import jax.numpy as jnp
from jax import lax
from jax.experimental import pallas as pl
from jax.experimental.pallas import tpu as pltpu
from jax.sharding import PartitionSpec as P

STEPS = 2
NODES = 125
RIM = 32
SHEET = 32
FACES = 6
F32, BF16, I32 = jnp.float32, jnp.bfloat16, jnp.int32
partner_face = (1, 0, 3, 2, 5, 4)

VMEM = pl.BlockSpec(memory_space=pltpu.VMEM)
SMEM = pl.BlockSpec(memory_space=pltpu.SMEM)
PARAMS = pltpu.CompilerParams(vmem_limit_bytes=40 * 2**20)


def shape(*dims):
    return jax.ShapeDtypeStruct(dims, F32)


def iota(dims, axis):
    return lax.broadcasted_iota(I32, dims, axis)


def halves(x):
    high = x.astype(BF16)
    return high, (x - high.astype(F32)).astype(BF16)


def dot(a, b):
    return lax.dot_general(a, b, (((1,), (0,)), ((), ())), preferred_element_type=F32)


def face_nodes(dims, axis):
    row = iota(dims, axis)
    face, q = row // SHEET, row % SHEET
    a = sum((q >= 5 * i).astype(I32) for i in range(1, 5))
    b = q - 5 * a
    node = jnp.where(face == 0, q, q + 100)
    node = jnp.where(face == 2, 25 * a + b, node)
    node = jnp.where(face == 3, 25 * a + 20 + b, node)
    node = jnp.where(face == 4, 5 * q, node)
    node = jnp.where(face == 5, 5 * q + 4, node)
    return jnp.where(q < 25, node, -1)


def picker():
    dims = (FACES * SHEET, 128)
    return jnp.where(face_nodes(dims, 0) == iota(dims, 1), 1.0, 0.0).astype(BF16)


def lifter():
    dims = (128, FACES * SHEET)
    return jnp.where(face_nodes(dims, 1) == iota(dims, 0), 1.0, 0.0).astype(BF16)


def padded(ref, index):
    return jnp.concatenate([ref[index], jnp.zeros((128 - NODES, 128), F32)], axis=0)


def stacked(fields):
    high, low = halves(jnp.concatenate(fields, axis=1))
    return jnp.concatenate([high, low], axis=0)


def pack_rim(fields):
    lane = iota((128, 128), 1)
    out = fields[0]
    for k in range(1, 4):
        if k < len(fields):
            out = jnp.where(lane < RIM * k, out, pltpu.roll(fields[k], RIM * k, 1))
    return jnp.where(lane < RIM * len(fields), out, 0.0)


def pack_kernel(count_ref, forward_ref, adjoint_ref, rim_ref):
    live = (iota((128, 128), 1) < count_ref[0, 0]).astype(F32)
    fields = [padded(ref, c) * live for ref in (forward_ref, adjoint_ref) for c in range(3)]
    rim_ref[0] = pack_rim(fields[:4])
    rim_ref[1] = pack_rim(fields[4:])


def own_kernel(count_ref, forward_ref, adjoint_ref, stiff_ref, strain_ref, face_ref, kernel_ref):
    live = (iota((128, 128), 1) < count_ref[0, 0]).astype(F32)
    fields = [padded(ref, c) * live for ref in (forward_ref, adjoint_ref) for c in range(3)]
    strain, faces = products(stiff_ref, fields, fields)
    for k in range(6):
        strain_ref[k] = strain[k]
        face_ref[k] = faces[k]
    kernel_ref[...] = sum(fields[c] * strain[3 + c] for c in range(3))


def padded_stiffness(stiff_ref):
    wide = jnp.concatenate([stiff_ref[...], jnp.zeros((NODES, 128 - NODES), F32)], axis=1)
    return jnp.concatenate([wide, jnp.zeros((128 - NODES, 128), F32)], axis=0)


def products(stiff_ref, fields, faced):
    n, m = len(fields), len(faced)
    high, low = halves(padded_stiffness(stiff_ref))
    x = stacked(fields)
    both = dot(jnp.concatenate([high, high], axis=1), x)
    strain = both + dot(low, x[:128])
    pick = picker()
    faces = dot(jnp.concatenate([pick, pick], axis=1), x[:, : 128 * m])
    return (
        [strain[:, 128 * k : 128 * (k + 1)] for k in range(n)],
        [faces[:, 128 * k : 128 * (k + 1)] for k in range(m)],
    )


def rim_faces(groups):
    x = stacked(groups)
    pick = picker()
    faces = dot(jnp.concatenate([pick, pick], axis=1), x)
    return [faces[:, 128 * k : 128 * (k + 1)] for k in range(len(groups))]


def lifted(place_ref, near_ref, own, before, after):
    mine, parts = place_ref[0], place_ref[1]
    jumps = [[] for _ in own]
    for face in range(FACES):
        p = partner_face[face]
        near = jnp.broadcast_to(near_ref[face : face + 1, :], (SHEET, 128))
        target, slot = near // 128, near % 128
        relative = target - mine
        relative = jnp.where(relative < 0, relative + parts, relative)
        at_home, is_next = relative == 0, relative == 1
        rim_slot = slot % RIM
        for k in range(len(own)):
            group, q = k // 4, k % 4
            rows = slice(SHEET * p, SHEET * (p + 1))
            here = jnp.take_along_axis(own[k][rows], slot, axis=1, mode="promise_in_bounds")
            prev = jnp.take_along_axis(before[group][rows], rim_slot + RIM * q, axis=1, mode="promise_in_bounds")
            foll = jnp.take_along_axis(after[group][rows], rim_slot + RIM * q, axis=1, mode="promise_in_bounds")
            across = jnp.where(at_home, here, jnp.where(is_next, foll, prev))
            jumps[k].append(across - own[k][SHEET * face : SHEET * (face + 1)])
    high, low = halves(jnp.concatenate([jnp.concatenate(j, axis=0) for j in jumps], axis=1))
    lift = lifter()
    out = dot(lift, high) + dot(lift, low)
    return [out[:, 128 * k : 128 * (k + 1)] for k in range(len(own))]


def step_kernel(
    n_event, n_mesh, tile_width, scale,
    count_ref, place_ref, forward_ref, adjoint_ref, strain_ref, face_ref, kernel_ref, before_ref, after_ref,
    near_ref, material_ref, stiff_ref, project_ref, destination_ref,
    forward_one_ref, strain_one_ref, face_one_ref, rim_ref, dense_ref,
):
    live = (iota((128, 128), 1) < count_ref[0, 0]).astype(F32)
    material = jnp.broadcast_to(material_ref[...], (128, 128))
    before = rim_faces([before_ref[0], before_ref[1]])
    after = rim_faces([after_ref[0], after_ref[1]])
    lift = lifted(place_ref, near_ref, [face_ref[k] for k in range(6)], before, after)
    fields = []
    for k in range(6):
        start = padded(forward_ref if k < 3 else adjoint_ref, k % 3) * live
        force = 0.5 * lift[k] - material * strain_ref[k]
        fields.append(live * (start + 0.4 * force))
    rim_ref[...] = pack_rim(fields[:3])
    strain, faces = products(stiff_ref, fields, fields[:3])
    for c in range(3):
        forward_one_ref[c] = fields[c]
        strain_one_ref[c] = strain[c]
        face_one_ref[c] = faces[c]
    kernel = kernel_ref[...] + sum(fields[c] * strain[3 + c] for c in range(3))
    k_high, k_low = halves(kernel.T)
    project = jnp.concatenate([project_ref[...], jnp.zeros((128 - NODES, 64), F32)], axis=0)
    p_high, p_low = halves(project)
    blocks = (dot(k_high, p_high) + (dot(k_high, p_low) + dot(k_low, p_high))) * scale
    b_high, b_low = halves(blocks)
    none = jnp.zeros((128, 64), BF16)
    right = jnp.concatenate(
        [
            jnp.concatenate([b_high, none, b_low, none], axis=1),
            jnp.concatenate([none, b_high, none, b_low], axis=1),
        ],
        axis=0,
    )
    rows = 4 * n_event
    row = iota((rows, 128), 0)
    tile = (row // 4) * (n_mesh * tile_width) - 2 + row % 4
    wanted = jnp.broadcast_to(destination_ref[...], (rows, 128))
    offset = wanted - tile
    for m in range(n_mesh):
        hit = [jnp.where(offset == m * tile_width + 4 * h, 1.0, 0.0).astype(BF16) for h in range(2)]
        out = dot(jnp.concatenate(hit, axis=1), right)
        dense_ref[m] = out[:, :128] + out[:, 128:]


def last_kernel(
    count_ref, place_ref, forward_ref, one_ref, strain_ref, face_ref, before_ref, after_ref, near_ref, material_ref,
    final_ref,
):
    live = (iota((128, 128), 1) < count_ref[0, 0]).astype(F32)
    material = jnp.broadcast_to(material_ref[...], (128, 128))
    before = rim_faces([before_ref[...]])
    after = rim_faces([after_ref[...]])
    lift = lifted(place_ref, near_ref, [face_ref[k] for k in range(3)], before, after)
    for c in range(3):
        force = 0.5 * lift[c] - material * strain_ref[c]
        out = live * (2.0 * one_ref[c] - padded(forward_ref, c) * live + 0.4 * force)
        final_ref[c] = out[:NODES]


def sum_kernel(x_ref, o_ref):
    total = x_ref[0]
    for i in range(1, x_ref.shape[0]):
        total = total + x_ref[i]
    o_ref[...] = total


def smooth_kernel(x_ref, coef_ref, o_ref):
    total = x_ref[0]
    for i in range(1, x_ref.shape[0]):
        total = total + x_ref[i]
    both = jnp.concatenate([total, pltpu.roll(total, 64, 1)], axis=0)
    x = both.T[:64]
    node = iota((64, 8), 0)
    tile = iota((64, 8), 1)
    for _ in range(2):
        right = jnp.where(tile < 7, pltpu_shift(x, -1, 1), 0.0)
        left = jnp.where(tile > 0, pltpu_shift(x, 1, 1), 0.0)
        out = x + coef_ref[0:1, :] * (left + right - 2.0 * x)
        for d, stride in ((1, 16), (2, 4), (3, 1)):
            place = (node // stride) % 4
            up = jnp.where(place < 3, pltpu_shift(x, -stride, 0), 0.0)
            down = jnp.where(place > 0, pltpu_shift(x, stride, 0), 0.0)
            out = out + coef_ref[d : d + 1, :] * (up + down - 2.0 * x)
        x = out
    o_ref[...] = x[:, 2:6]


def pltpu_shift(x, by, axis):
    n = x.shape[axis]
    cut = (n - by) % n
    return jnp.concatenate([lax.slice_in_dim(x, cut, n, axis=axis), lax.slice_in_dim(x, 0, cut, axis=axis)], axis=axis)


def exchange(x, axis, wrap):
    count = lax.axis_size(axis)
    up = [(i, (i + 1) % count) for i in range(count if wrap else count - 1)]
    down = [(j, i) for i, j in up]
    return up, down


def per_device(
    forward_start, adjoint_start, stiffness, projection, material, neighbours, destinations, counts, smoothing
):
    elements = forward_start.shape[-1]
    tile_width = smoothing.shape[1]
    n_mesh, n_event = lax.axis_size("mesh"), lax.axis_size("event")
    scale = math.sqrt(tile_width / elements) / STEPS
    forward, adjoint, near = forward_start[0], adjoint_start[0], neighbours[0]
    place = jnp.stack([lax.axis_index("mesh"), jnp.int32(n_mesh)]).astype(I32)

    rim = pl.pallas_call(
        pack_kernel, out_shape=shape(2, 128, 128), in_specs=[SMEM, VMEM, VMEM], out_specs=VMEM, compiler_params=PARAMS
    )(counts, forward, adjoint)
    up, down = exchange(rim, "mesh", True)
    before, after = lax.ppermute(rim, "mesh", up), lax.ppermute(rim, "mesh", down)
    all_up, all_down = exchange(smoothing, ("event", "mesh"), False)
    coef_before = lax.ppermute(smoothing[:, tile_width - 1 :], ("event", "mesh"), all_up)
    coef_after = lax.ppermute(smoothing[:, :1], ("event", "mesh"), all_down)
    edge = jnp.zeros((4, 1), F32)
    coefs = jnp.concatenate([edge, coef_before, smoothing, coef_after, edge], axis=1)

    strain, faces, kernel = pl.pallas_call(
        own_kernel,
        out_shape=(shape(6, 128, 128), shape(6, 192, 128), shape(128, 128)),
        in_specs=[SMEM, VMEM, VMEM, VMEM],
        out_specs=(VMEM,) * 3,
        compiler_params=PARAMS,
    )(counts, forward, adjoint, stiffness)

    def one_step(*refs):
        step_kernel(n_event, n_mesh, tile_width, scale, *refs)

    one, strain_one, face_one, rim_one, dense = pl.pallas_call(
        one_step,
        out_shape=(
            shape(3, 128, 128),
            shape(3, 128, 128),
            shape(3, 192, 128),
            shape(128, 128),
            shape(n_mesh, 4 * n_event, 128),
        ),
        in_specs=[SMEM, SMEM] + [VMEM] * 12,
        out_specs=(VMEM,) * 5,
        compiler_params=PARAMS,
    )(
        counts, place, forward, adjoint, strain, faces, kernel, before, after,
        near, material, stiffness, projection, destinations,
    )
    before, after = lax.ppermute(rim_one, "mesh", up), lax.ppermute(rim_one, "mesh", down)

    parts = lax.all_to_all(dense, "mesh", 0, 0, tiled=True)
    partial = pl.pallas_call(
        sum_kernel, out_shape=shape(4 * n_event, 128), in_specs=[VMEM], out_specs=VMEM, compiler_params=PARAMS
    )(parts)
    final = pl.pallas_call(
        last_kernel,
        out_shape=shape(3, NODES, 128),
        in_specs=[SMEM, SMEM] + [VMEM] * 8,
        out_specs=VMEM,
        compiler_params=PARAMS,
    )(counts, place, forward, one, strain_one, face_one, before, after, near, material)
    pieces = lax.all_to_all(partial.reshape(n_event, 4, 128), "event", 0, 0, tiled=True)
    tiles = pl.pallas_call(
        smooth_kernel, out_shape=shape(64, tile_width), in_specs=[VMEM, VMEM], out_specs=VMEM, compiler_params=PARAMS
    )(pieces, coefs)
    return final[None], tiles


def solution(mesh):
    in_specs = (
        P("event", None, None, "mesh"),
        P("event", None, None, "mesh"),
        P(),
        P(),
        P("event", "mesh"),
        P("event", None, "mesh"),
        P("event", "mesh"),
        P("event", "mesh"),
        P(None, ("event", "mesh")),
    )
    out_specs = (P("event", None, None, "mesh"), P(None, ("event", "mesh")))
    return jax.shard_map(per_device, mesh=mesh, in_specs=in_specs, out_specs=out_specs, check_vma=False)
```

```python
import math

import jax
import jax.numpy as jnp
from jax import lax
from jax.experimental import pallas as pl
from jax.experimental.pallas import tpu as pltpu
from jax.sharding import PartitionSpec as P

STEPS = 2
NODES = 125
RIM = 32
SHEET = 32
FACES = 6
F32, BF16, I32 = jnp.float32, jnp.bfloat16, jnp.int32
partner_face = (1, 0, 3, 2, 5, 4)

VMEM = pl.BlockSpec(memory_space=pltpu.VMEM)
SMEM = pl.BlockSpec(memory_space=pltpu.SMEM)
ANY = pl.BlockSpec(memory_space=pl.ANY)
PARAMS = pltpu.CompilerParams(vmem_limit_bytes=40 * 2**20)


def shape(*dims):
    return jax.ShapeDtypeStruct(dims, F32)


def iota(dims, axis):
    return lax.broadcasted_iota(I32, dims, axis)


def halves(x):
    high = x.astype(BF16)
    return high, (x - high.astype(F32)).astype(BF16)


def dot(a, b):
    return lax.dot_general(a, b, (((1,), (0,)), ((), ())), preferred_element_type=F32)


def face_nodes(dims, axis):
    row = iota(dims, axis)
    face, q = row // SHEET, row % SHEET
    a = sum((q >= 5 * i).astype(I32) for i in range(1, 5))
    b = q - 5 * a
    node = jnp.where(face == 0, q, q + 100)
    node = jnp.where(face == 2, 25 * a + b, node)
    node = jnp.where(face == 3, 25 * a + 20 + b, node)
    node = jnp.where(face == 4, 5 * q, node)
    node = jnp.where(face == 5, 5 * q + 4, node)
    return jnp.where(q < 25, node, -1)


def picker():
    dims = (FACES * SHEET, 128)
    return jnp.where(face_nodes(dims, 0) == iota(dims, 1), 1.0, 0.0).astype(BF16)


def lifter():
    dims = (128, FACES * SHEET)
    return jnp.where(face_nodes(dims, 1) == iota(dims, 0), 1.0, 0.0).astype(BF16)


def padded(ref, index):
    return jnp.concatenate([ref[index], jnp.zeros((128 - NODES, 128), F32)], axis=0)


def stacked(fields):
    high, low = halves(jnp.concatenate(fields, axis=1))
    return jnp.concatenate([high, low], axis=0)


def pack_rim(fields):
    lane = iota((128, 128), 1)
    out = fields[0]
    for k in range(1, len(fields)):
        out = jnp.where(lane < RIM * k, out, pltpu.roll(fields[k], RIM * k, 1))
    return jnp.where(lane < RIM * len(fields), out, 0.0)


def fold(x):
    return jnp.where(iota((64, 128), 1) < 64, x[:64], pltpu.roll(x[64:], 64, 1))


def live_mask(count_ref):
    return (iota((128, 128), 1) < count_ref[0, 0]).astype(F32)


def pack_kernel(count_ref, forward_ref, adjoint_ref, rim_ref):
    live = live_mask(count_ref)
    fields = [padded(ref, c) * live for ref in (forward_ref, adjoint_ref) for c in range(3)]
    rim_ref[:128] = pack_rim(fields[:4])
    rim_ref[128:] = fold(pack_rim(fields[4:]))


def split_stiffness(stiff_ref):
    wide = jnp.concatenate([stiff_ref[...], jnp.zeros((NODES, 128 - NODES), F32)], axis=1)
    return halves(jnp.concatenate([wide, jnp.zeros((128 - NODES, 128), F32)], axis=0))


def columns(x):
    return [x[:, 128 * k : 128 * (k + 1)] for k in range(x.shape[1] // 128)]


def strains(stiffness, x):
    high, low = stiffness
    return columns(dot(jnp.concatenate([high, high], axis=1), x) + dot(low, x[:128]))


def faces_of(x):
    pick = picker()
    return columns(dot(jnp.concatenate([pick, pick], axis=1), x))


def take(x, index):
    return jnp.take_along_axis(x, index, axis=1, mode="promise_in_bounds")


def lift_of(jumps):
    high, low = halves(jnp.concatenate([jnp.concatenate(j, axis=0) for j in jumps], axis=1))
    lift = lifter()
    return columns(dot(lift, high) + dot(lift, low))


def own_jumps(place_ref, near_ref, own):
    jumps = [[] for _ in own]
    for face in range(FACES):
        p = partner_face[face]
        near = jnp.broadcast_to(near_ref[face : face + 1, :], (SHEET, 128))
        home = near // 128 == place_ref[0]
        slot = near % 128
        for k in range(len(own)):
            here = take(own[k][SHEET * p : SHEET * (p + 1)], slot)
            jumps[k].append(jnp.where(home, here, 0.0) - own[k][SHEET * face : SHEET * (face + 1)])
    return jumps


def rim_jumps(place_ref, near_ref, rims, n):
    mine, parts = place_ref[0], place_ref[1]
    follower = jnp.where(mine + 1 == parts, 0, mine + 1)
    jumps = [[] for _ in range(n)]
    for face in range(FACES):
        p = partner_face[face]
        near = jnp.broadcast_to(near_ref[face : face + 1, :], (SHEET, 128))
        target = near // 128
        away = target != mine
        index = near % RIM + jnp.where(target == follower, 64, 0)
        for k in range(n):
            across = take(rims[k // 2][SHEET * p : SHEET * (p + 1)], index + RIM * (k % 2))
            jumps[k].append(jnp.where(away, across, 0.0))
    return jumps


def merge(before, after):
    lane = iota(before.shape, 1)
    first = jnp.where(lane < 64, before, pltpu.roll(after, 64, 1))
    second = jnp.where(lane < 64, pltpu.roll(before, 64, 1), after)
    return first, second


def edges_of(smooth_ref):
    width = smooth_ref.shape[1]
    wide = jnp.concatenate([smooth_ref[...], jnp.zeros((4, 128 - width), F32)], axis=1)
    turned = jnp.concatenate([wide, jnp.zeros((124, 128), F32)], axis=0).T
    last, first = turned[width - 1 : width], turned[0:1]
    lane = iota((1, 128), 1)
    row = jnp.where(lane < 4, last, pltpu.roll(jnp.broadcast_to(first, (8, 128)), 4, 1)[0:1])
    return row, turned


def own_kernel(
    count_ref, place_ref, forward_ref, adjoint_ref, stiff_ref, near_ref, material_ref, smooth_ref,
    partial_ref, kernel_ref, edge_ref, turned_ref,
):
    live = live_mask(count_ref)
    material = jnp.broadcast_to(material_ref[...], (128, 128))
    fields = [padded(ref, c) * live for ref in (forward_ref, adjoint_ref) for c in range(3)]
    x = stacked(fields)
    strain = strains(split_stiffness(stiff_ref), x)
    lift = lift_of(own_jumps(place_ref, near_ref, faces_of(x)))
    for k in range(6):
        force = 0.5 * lift[k] - material * strain[k]
        partial_ref[k] = live * (fields[k] + 0.4 * force)
    kernel_ref[...] = sum(fields[c] * strain[3 + c] for c in range(3))
    row, turned = edges_of(smooth_ref)
    edge_ref[...] = jnp.broadcast_to(row, (8, 128))
    turned_ref[...] = turned[:8]


def step_kernel(
    scale, n_mesh,
    count_ref, place_ref, partial_ref, kernel_ref, before_ref, after_ref, near_ref, stiff_ref, project_ref,
    destination_ref, edge_ref,
    forward_ref, strain_ref, rim_ref, edge_out_ref, chunk_ref,
):
    live = live_mask(count_ref)
    first, second = merge(before_ref[:128], after_ref[:128])
    upper, lower = merge(before_ref[128:], after_ref[128:])
    rims = faces_of(stacked([first, second, jnp.concatenate([upper, lower], axis=0)]))
    lift = lift_of(rim_jumps(place_ref, near_ref, rims, 6))
    fields = [partial_ref[k] + live * (0.2 * lift[k]) for k in range(6)]
    rim = pack_rim(fields[:3])
    rim_ref[...] = jnp.where(iota((128, 128), 0) == NODES, jnp.broadcast_to(edge_ref[0:1, :], (128, 128)), rim)
    edge_out_ref[...] = edge_ref[...]
    strain = strains(split_stiffness(stiff_ref), stacked(fields))
    for c in range(3):
        forward_ref[c] = fields[c]
        strain_ref[c] = strain[c]
    kernel = kernel_ref[...] + sum(fields[c] * strain[3 + c] for c in range(3))
    k_high, k_low = halves(kernel)
    p_high, p_low = halves(jnp.concatenate([project_ref[...], jnp.zeros((64, 128 - NODES), F32)], axis=1))
    blocks = dot(jnp.concatenate([p_high, p_high], axis=1), jnp.concatenate([k_high, k_low], axis=0))
    blocks = (blocks + dot(p_low, k_high)) * scale
    turned = jnp.concatenate([blocks, pltpu.roll(blocks, 64, 1)], axis=0).T[:64]
    wanted = jnp.broadcast_to(destination_ref[...].astype(F32), (8, 128))
    for m in range(n_mesh):
        chunk_ref[m, :64] = turned
        chunk_ref[m, 64:] = wanted


def dense_kernel(n_event, n_mesh, tile_width, place_ref, parts_ref, before_ref, after_ref, wrap_ref, out_ref):
    rows = 4 * n_event
    row = iota((2 * rows, 128), 0)
    within = row % rows
    tile = (within // 4) * (n_mesh * tile_width) + within % 4 + 4 * (row // rows) - 2
    tile = tile.astype(F32) + (place_ref[0] * tile_width).astype(F32)
    lane = iota((64, 128), 1)
    left, right = [], []
    for m in range(n_mesh):
        x = parts_ref[m, :64]
        high = x.astype(BF16).astype(F32)
        low = x - high
        right.append(jnp.where(lane < 64, high, pltpu.roll(low, 64, 1)).astype(BF16))
        right.append(jnp.where(lane < 64, pltpu.roll(high, 64, 1), low).astype(BF16))
        wanted = jnp.broadcast_to(parts_ref[m, 64:65], (2 * rows, 128))
        left.append(jnp.where(wanted == tile, 1.0, 0.0).astype(BF16))
    both = dot(jnp.concatenate(left, axis=1), jnp.concatenate(right, axis=0))
    both = both + pltpu.roll(both, 64, 1)
    out_ref[...] = jnp.where(iota((rows, 128), 1) < 64, both[:rows], both[rows:])


def last_kernel(
    count_ref, place_ref, forward_ref, one_ref, strain_ref, before_ref, after_ref, near_ref, material_ref, turned_ref,
    wrap_ref,
    final_ref, coef_ref,
):
    live = live_mask(count_ref)
    material = jnp.broadcast_to(material_ref[...], (128, 128))
    fields = [one_ref[c] for c in range(3)]
    jumps = own_jumps(place_ref, near_ref, faces_of(stacked(fields)))
    row = iota((128, 128), 0)
    before = jnp.where(row < NODES, before_ref[...], 0.0)
    after = jnp.where(row < NODES, after_ref[...], 0.0)
    rims = faces_of(stacked(list(merge(before, after))))
    more = rim_jumps(place_ref, near_ref, rims, 3)
    lift = lift_of([[a + b for a, b in zip(*pair)] for pair in zip(jumps, more)])
    for c in range(3):
        force = 0.5 * lift[c] - material * strain_ref[c]
        out = live * (2.0 * fields[c] - padded(forward_ref, c) * live + 0.4 * force)
        final_ref[c] = out[:NODES]
    mine, parts = place_ref[0], place_ref[1]
    wrap = wrap_ref[0:1]
    first = jnp.where(jnp.full((1, 128), mine) == 0, wrap, before_ref[NODES : NODES + 1])
    last = jnp.where(jnp.full((1, 128), mine) == parts - 1, wrap, after_ref[NODES : NODES + 1])
    last = pltpu.roll(jnp.broadcast_to(last, (8, 128)), 124, 1)
    tile = iota((8, 128), 0)
    table = pltpu.roll(turned_ref[...], 2, 0)
    table = jnp.where((tile >= 2) & (tile < 6), table, 0.0)
    table = jnp.where(tile == 1, jnp.broadcast_to(first, (8, 128)), table)
    table = jnp.where(tile == 6, last, table)
    for d in range(4):
        coef_ref[d] = jnp.broadcast_to(table[:, d : d + 1], (8, 128))


def smooth_kernel(x_ref, coef_ref, o_ref):
    total = x_ref[0]
    for i in range(1, x_ref.shape[0]):
        total = total + x_ref[i]
    x = jnp.concatenate([total, pltpu.roll(total, 64, 1)], axis=0)
    node, tile = iota((8, 128), 1), iota((8, 128), 0)
    for _ in range(2):
        right = jnp.where(tile < 7, pltpu.roll(x, 7, 0), 0.0)
        left = jnp.where(tile > 0, pltpu.roll(x, 1, 0), 0.0)
        out = x + coef_ref[0] * (left + right - 2.0 * x)
        for d, stride in ((1, 16), (2, 4), (3, 1)):
            place = (node // stride) % 4
            up = jnp.where(place < 3, pltpu.roll(x, 128 - stride, 1), 0.0)
            down = jnp.where(place > 0, pltpu.roll(x, stride, 1), 0.0)
            out = out + coef_ref[d] * (up + down - 2.0 * x)
        x = out
    o_ref[...] = x[2:6, :64]


def call(kernel, out_shape, n_smem, n_vmem, n_any=0):
    many = isinstance(out_shape, tuple)
    return pl.pallas_call(
        kernel,
        out_shape=out_shape,
        in_specs=[SMEM] * n_smem + [VMEM] * n_vmem + [ANY] * n_any,
        out_specs=(VMEM,) * len(out_shape) if many else VMEM,
        compiler_params=PARAMS,
    )


def per_device(
    forward_start, adjoint_start, stiffness, projection, material, neighbours, destinations, counts, smoothing
):
    elements = forward_start.shape[-1]
    tile_width = smoothing.shape[1]
    n_mesh, n_event = lax.axis_size("mesh"), lax.axis_size("event")
    scale = math.sqrt(tile_width / elements) / STEPS
    forward, adjoint, near = forward_start[0], adjoint_start[0], neighbours[0]
    place = jnp.stack([lax.axis_index("mesh"), jnp.int32(n_mesh)]).astype(I32)
    up = [(i, (i + 1) % n_mesh) for i in range(n_mesh)]
    down = [(j, i) for i, j in up]
    ends = [((e + 1) * n_mesh - 1, (e + 1) * n_mesh) for e in range(n_event - 1)]
    ends = ends + [(j, i) for i, j in ends]

    rim = call(pack_kernel, shape(192, 128), 1, 2)(counts, forward, adjoint)
    before, after = lax.ppermute(rim, "mesh", up), lax.ppermute(rim, "mesh", down)
    partial, kernel, edge, turned = call(
        own_kernel, (shape(6, 128, 128), shape(128, 128), shape(8, 128), shape(8, 128)), 2, 6
    )(counts, place, forward, adjoint, stiffness, near, material, smoothing)

    def one_step(*refs):
        step_kernel(scale, n_mesh, *refs)

    one, strain, rim_one, edge, chunk = call(
        one_step,
        (shape(3, 128, 128), shape(3, 128, 128), shape(128, 128), shape(8, 128), shape(n_mesh, 72, 128)),
        2,
        9,
    )(counts, place, partial, kernel, before, after, near, stiffness, projection.T, destinations, edge)
    parts = lax.all_to_all(chunk, "mesh", 0, 0, tiled=True)
    before, after = lax.ppermute(rim_one, "mesh", up), lax.ppermute(rim_one, "mesh", down)
    wrap = lax.ppermute(edge, ("event", "mesh"), ends)

    def dense(*refs):
        dense_kernel(n_event, n_mesh, tile_width, *refs)

    partial = call(dense, shape(4 * n_event, 128), 1, 1, 3)(place, parts, before, after, wrap)
    pieces = lax.all_to_all(partial.reshape(n_event, 4, 128), "event", 0, 0, tiled=True)
    final, coefs = call(last_kernel, (shape(3, NODES, 128), shape(4, 8, 128)), 2, 9)(
        counts, place, forward, one, strain, before, after, near, material, turned, wrap
    )
    tiles = call(smooth_kernel, shape(tile_width, 64), 0, 2)(pieces, coefs)
    return final[None], tiles.T


def solution(mesh):
    in_specs = (
        P("event", None, None, "mesh"),
        P("event", None, None, "mesh"),
        P(),
        P(),
        P("event", "mesh"),
        P("event", None, "mesh"),
        P("event", "mesh"),
        P("event", "mesh"),
        P(None, ("event", "mesh")),
    )
    out_specs = (P("event", None, None, "mesh"), P(None, ("event", "mesh")))
    return jax.shard_map(per_device, mesh=mesh, in_specs=in_specs, out_specs=out_specs, check_vma=False)
```

```python
import math

import jax
import jax.numpy as jnp
from jax import lax
from jax.experimental import pallas as pl
from jax.experimental.pallas import tpu as pltpu
from jax.sharding import PartitionSpec as P

STEPS = 2
NODES = 125
RIM = 32
SHEET = 32
FACES = 6
F32, BF16, I32 = jnp.float32, jnp.bfloat16, jnp.int32
partner_face = (1, 0, 3, 2, 5, 4)

VMEM = pl.BlockSpec(memory_space=pltpu.VMEM)
SMEM = pl.BlockSpec(memory_space=pltpu.SMEM)
HBM = pl.BlockSpec(memory_space=pltpu.HBM)
PARAMS = pltpu.CompilerParams(vmem_limit_bytes=40 * 2**20)


def shape(*dims, dtype=F32):
    return jax.ShapeDtypeStruct(dims, dtype)


def iota(dims, axis):
    return lax.broadcasted_iota(I32, dims, axis)


def halves(x):
    high = x.astype(BF16)
    return high, (x - high.astype(F32)).astype(BF16)


def dot(a, b):
    return lax.dot_general(a, b, (((1,), (0,)), ((), ())), preferred_element_type=F32)


def face_nodes(dims, axis):
    row = iota(dims, axis)
    face, q = row // SHEET, row % SHEET
    a = sum((q >= 5 * i).astype(I32) for i in range(1, 5))
    b = q - 5 * a
    node = jnp.where(face == 0, q, q + 100)
    node = jnp.where(face == 2, 25 * a + b, node)
    node = jnp.where(face == 3, 25 * a + 20 + b, node)
    node = jnp.where(face == 4, 5 * q, node)
    node = jnp.where(face == 5, 5 * q + 4, node)
    return jnp.where(q < 25, node, -1)


def picker():
    dims = (FACES * SHEET, 128)
    return jnp.where(face_nodes(dims, 0) == iota(dims, 1), 1.0, 0.0).astype(BF16)


def lifter():
    dims = (128, FACES * SHEET)
    return jnp.where(face_nodes(dims, 1) == iota(dims, 0), 1.0, 0.0).astype(BF16)


def rows_of(ref):
    return ref.reshape(3 * NODES, 128)


def padded(ref, c):
    rows = rows_of(ref)[NODES * c : NODES * (c + 1)]
    return jnp.concatenate([rows, jnp.zeros((128 - NODES, 128), F32)], axis=0)


def stacked(fields):
    high, low = halves(jnp.concatenate(fields, axis=1))
    return jnp.concatenate([high, low], axis=0)


def pack_rim(fields):
    lane = iota((128, 128), 1)
    out = fields[0]
    for k in range(1, len(fields)):
        out = jnp.where(lane < RIM * k, out, pltpu.roll(fields[k], RIM * k, 1))
    return jnp.where(lane < RIM * len(fields), out, 0.0)


def fold(x):
    return jnp.where(iota((64, 128), 1) < 64, x[:64], pltpu.roll(x[64:], 64, 1))


def live_mask(count_ref):
    return (iota((128, 128), 1) < count_ref[0, 0]).astype(F32)


def pack_kernel(count_ref, forward_ref, adjoint_ref, rim_ref, field_ref, forward_in, adjoint_in, sems):
    pairs = ((forward_ref, forward_in), (adjoint_ref, adjoint_in))
    copies = [pltpu.make_async_copy(a, b, sems.at[i]) for i, (a, b) in enumerate(pairs)]
    for copy in copies:
        copy.start()
    for copy in copies:
        copy.wait()
    live = live_mask(count_ref)
    fields = [padded(ref, c) * live for ref in (forward_in, adjoint_in) for c in range(3)]
    rim_ref[:128] = pack_rim(fields[:4])
    rim_ref[128:] = fold(pack_rim(fields[4:]))
    for k in range(6):
        field_ref[k] = fields[k]


def split_stiffness(stiff_ref):
    wide = jnp.concatenate([stiff_ref[...], jnp.zeros((NODES, 128 - NODES), F32)], axis=1)
    return halves(jnp.concatenate([wide, jnp.zeros((128 - NODES, 128), F32)], axis=0))


def columns(x):
    return [x[:, 128 * k : 128 * (k + 1)] for k in range(x.shape[1] // 128)]


def strains(high, low, x):
    return columns(dot(jnp.concatenate([high, high], axis=1), x) + dot(low, x[:128]))


def faces_of(pick, x):
    return columns(dot(jnp.concatenate([pick, pick], axis=1), x))


def take(x, index):
    return jnp.take_along_axis(x, index, axis=1, mode="promise_in_bounds")


def lift_of(lift, jumps):
    high, low = halves(jnp.concatenate([jnp.concatenate(j, axis=0) for j in jumps], axis=1))
    return columns(dot(lift, high) + dot(lift, low))


def own_jumps(place_ref, near_ref, own):
    jumps = [[] for _ in own]
    for face in range(FACES):
        p = partner_face[face]
        near = jnp.broadcast_to(near_ref[face], (SHEET, 128))
        home = near // 128 == place_ref[0]
        slot = near % 128
        for k in range(len(own)):
            here = take(own[k][SHEET * p : SHEET * (p + 1)], slot)
            jumps[k].append(jnp.where(home, here, 0.0) - own[k][SHEET * face : SHEET * (face + 1)])
    return jumps


def rim_jumps(place_ref, near_ref, rims, n):
    mine, parts = place_ref[0], place_ref[1]
    follower = jnp.where(mine + 1 == parts, 0, mine + 1)
    jumps = [[] for _ in range(n)]
    for face in range(FACES):
        p = partner_face[face]
        near = jnp.broadcast_to(near_ref[face], (SHEET, 128))
        target = near // 128
        away = target != mine
        index = near % RIM + jnp.where(target == follower, 64, 0)
        for k in range(n):
            across = take(rims[k // 2][SHEET * p : SHEET * (p + 1)], index + RIM * (k % 2))
            jumps[k].append(jnp.where(away, across, 0.0))
    return jumps


def merge(before, after):
    lane = iota(before.shape, 1)
    first = jnp.where(lane < 64, before, pltpu.roll(after, 64, 1))
    second = jnp.where(lane < 64, pltpu.roll(before, 64, 1), after)
    return first, second


def edges_of(smooth_ref):
    width = smooth_ref.shape[1]
    wide = jnp.concatenate([smooth_ref[...], jnp.zeros((4, 128 - width), F32)], axis=1)
    turned = jnp.concatenate([wide, jnp.zeros((124, 128), F32)], axis=0).T
    last, first = turned[width - 1 : width], turned[0:1]
    lane = iota((1, 128), 1)
    row = jnp.where(lane < 4, last, pltpu.roll(jnp.broadcast_to(first, (8, 128)), 4, 1)[0:1])
    return row, turned


def own_kernel(
    count_ref, place_ref, field_ref, *refs
):
    sources, refs = refs[:6], refs[6:]
    partial_ref, kernel_ref, edge_ref, turned_ref, stiff_out_ref, pick_ref, lift_ref, project_out_ref = refs[:8]
    wanted_ref, near_out_ref, material_out_ref = refs[8:11]
    held, sems = refs[11:17], refs[17]
    copies = [pltpu.make_async_copy(a, b, sems.at[i]) for i, (a, b) in enumerate(zip(sources, held))]
    for copy in copies:
        copy.start()
    stiff_ref, near_ref, material_ref, smooth_ref, project_ref, destination_ref = held
    live = live_mask(count_ref)
    fields = [field_ref[k] for k in range(6)]
    pick, lift = picker(), lifter()
    pick_ref[...] = pick
    lift_ref[...] = lift
    x = stacked(fields)
    faces = faces_of(pick, x)
    copies[1].wait()
    near_out_ref[...] = near_ref[...]
    lifted = lift_of(lift, own_jumps(place_ref, near_ref, faces))
    copies[0].wait()
    copies[2].wait()
    high, low = split_stiffness(stiff_ref)
    stiff_out_ref[0] = high
    stiff_out_ref[1] = low
    material = jnp.broadcast_to(material_ref[...], (128, 128))
    material_out_ref[...] = jnp.broadcast_to(material_ref[...], (8, 128))
    strain = strains(high, low, x)
    for k in range(6):
        force = 0.5 * lifted[k] - material * strain[k]
        partial_ref[k] = live * (fields[k] + 0.4 * force)
    kernel_ref[...] = sum(fields[c] * strain[3 + c] for c in range(3))
    copies[3].wait()
    row, turned = edges_of(smooth_ref)
    edge_ref[...] = jnp.broadcast_to(row, (8, 128))
    turned_ref[...] = turned[:8]
    copies[4].wait()
    copies[5].wait()
    high, low = halves(jnp.concatenate([project_ref[...], jnp.zeros((64, 128 - NODES), F32)], axis=1))
    project_out_ref[0] = high
    project_out_ref[1] = low
    wanted_ref[...] = jnp.broadcast_to(destination_ref[...].astype(F32), (8, 128))


def step_kernel(
    scale, n_mesh,
    count_ref, place_ref, partial_ref, kernel_ref, before_ref, after_ref, near_ref, stiff_ref, pick_ref, lift_ref,
    project_ref, wanted_ref, edge_ref,
    forward_ref, strain_ref, rim_ref, chunk_ref,
):
    live = live_mask(count_ref)
    first, second = merge(before_ref[:128], after_ref[:128])
    upper, lower = merge(before_ref[128:], after_ref[128:])
    rims = faces_of(pick_ref[...], stacked([first, second, jnp.concatenate([upper, lower], axis=0)]))
    lift = lift_of(lift_ref[...], rim_jumps(place_ref, near_ref, rims, 6))
    fields = [partial_ref[k] + live * (0.2 * lift[k]) for k in range(6)]
    strain = strains(stiff_ref[0], stiff_ref[1], stacked(fields))
    kernel = kernel_ref[...] + sum(fields[c] * strain[3 + c] for c in range(3))
    k_high, k_low = halves(kernel)
    p_high, p_low = project_ref[0], project_ref[1]
    blocks = dot(jnp.concatenate([p_high, p_high], axis=1), jnp.concatenate([k_high, k_low], axis=0))
    blocks = (blocks + dot(p_low, k_high)) * scale
    turned = jnp.concatenate([blocks, pltpu.roll(blocks, 64, 1)], axis=0).T[:64]
    for m in range(n_mesh):
        chunk_ref[m, :64] = turned
        chunk_ref[m, 64:] = wanted_ref[...]
    rim = pack_rim(fields[:3])
    rim_ref[...] = jnp.where(iota((128, 128), 0) == NODES, jnp.broadcast_to(edge_ref[0:1, :], (128, 128)), rim)
    for c in range(3):
        forward_ref[c] = fields[c]
        strain_ref[c] = strain[c]


def dense_kernel(
    n_event, n_mesh, tile_width, place_ref, parts_ref, rim_ref, edge_ref, out_ref, rim_out_ref, edge_out_ref
):
    rim_out_ref[...] = rim_ref[...]
    edge_out_ref[...] = edge_ref[...]
    rows = 4 * n_event
    row = iota((2 * rows, 128), 0)
    within = row % rows
    tile = (within // 4) * (n_mesh * tile_width) + within % 4 + 4 * (row // rows) - 2
    tile = tile.astype(F32) + (place_ref[0] * tile_width).astype(F32)
    lane = iota((64, 128), 1)
    left, right = [], []
    for m in range(n_mesh):
        x = parts_ref[m, :64]
        high = x.astype(BF16).astype(F32)
        low = x - high
        right.append(jnp.where(lane < 64, high, pltpu.roll(low, 64, 1)).astype(BF16))
        right.append(jnp.where(lane < 64, pltpu.roll(high, 64, 1), low).astype(BF16))
        wanted = jnp.broadcast_to(parts_ref[m, 64:65], (2 * rows, 128))
        left.append(jnp.where(wanted == tile, 1.0, 0.0).astype(BF16))
    both = dot(jnp.concatenate(left, axis=1), jnp.concatenate(right, axis=0))
    both = both + pltpu.roll(both, 64, 1)
    out_ref[...] = jnp.where(iota((rows, 128), 1) < 64, both[:rows], both[rows:])


def last_kernel(
    count_ref, place_ref, field_ref, one_ref, strain_ref, before_ref, after_ref, near_ref, material_ref, turned_ref,
    wrap_ref, pick_ref, lift_ref,
    final_ref, coef_ref,
):
    live = live_mask(count_ref)
    material = jnp.broadcast_to(material_ref[0:1], (128, 128))
    fields = [one_ref[c] for c in range(3)]
    jumps = own_jumps(place_ref, near_ref, faces_of(pick_ref[...], stacked(fields)))
    row = iota((128, 128), 0)
    before = jnp.where(row < NODES, before_ref[...], 0.0)
    after = jnp.where(row < NODES, after_ref[...], 0.0)
    rims = faces_of(pick_ref[...], stacked(list(merge(before, after))))
    more = rim_jumps(place_ref, near_ref, rims, 3)
    lift = lift_of(lift_ref[...], [[a + b for a, b in zip(*pair)] for pair in zip(jumps, more)])
    final = rows_of(final_ref)
    for c in range(3):
        force = 0.5 * lift[c] - material * strain_ref[c]
        out = live * (2.0 * fields[c] - field_ref[c] + 0.4 * force)
        final[NODES * c : NODES * (c + 1)] = out[:NODES]
    mine, parts = place_ref[0], place_ref[1]
    wrap = wrap_ref[0:1]
    first = jnp.where(jnp.full((1, 128), mine) == 0, wrap, before_ref[NODES : NODES + 1])
    last = jnp.where(jnp.full((1, 128), mine) == parts - 1, wrap, after_ref[NODES : NODES + 1])
    last = pltpu.roll(jnp.broadcast_to(last, (8, 128)), 124, 1)
    tile = iota((8, 128), 0)
    table = pltpu.roll(turned_ref[...], 2, 0)
    table = jnp.where((tile >= 2) & (tile < 6), table, 0.0)
    table = jnp.where(tile == 1, jnp.broadcast_to(first, (8, 128)), table)
    table = jnp.where(tile == 6, last, table)
    for d in range(4):
        coef_ref[d] = jnp.broadcast_to(table[:, d : d + 1], (8, 128))


def smooth_kernel(x_ref, coef_ref, o_ref):
    total = x_ref[0]
    for i in range(1, x_ref.shape[0]):
        total = total + x_ref[i]
    x = jnp.concatenate([total, pltpu.roll(total, 64, 1)], axis=0)
    node, tile = iota((8, 128), 1), iota((8, 128), 0)
    for _ in range(2):
        right = jnp.where(tile < 7, pltpu.roll(x, 7, 0), 0.0)
        left = jnp.where(tile > 0, pltpu.roll(x, 1, 0), 0.0)
        out = x + coef_ref[0] * (left + right - 2.0 * x)
        for d, stride in ((1, 16), (2, 4), (3, 1)):
            place = (node // stride) % 4
            up = jnp.where(place < 3, pltpu.roll(x, 128 - stride, 1), 0.0)
            down = jnp.where(place > 0, pltpu.roll(x, stride, 1), 0.0)
            out = out + coef_ref[d] * (up + down - 2.0 * x)
        x = out
    o_ref[...] = x[2:6, :64]


def call(kernel, out_shape, n_smem, n_vmem, n_hbm=0, scratch=()):
    many = isinstance(out_shape, tuple)
    return pl.pallas_call(
        kernel,
        out_shape=out_shape,
        in_specs=[SMEM] * n_smem + [VMEM] * n_vmem + [HBM] * n_hbm,
        out_specs=(VMEM,) * len(out_shape) if many else VMEM,
        scratch_shapes=scratch,
        compiler_params=PARAMS,
    )


def per_device(
    forward_start, adjoint_start, stiffness, projection, material, neighbours, destinations, counts, smoothing
):
    elements = forward_start.shape[-1]
    tile_width = smoothing.shape[1]
    n_mesh, n_event = lax.axis_size("mesh"), lax.axis_size("event")
    scale = math.sqrt(tile_width / elements) / STEPS
    forward, adjoint = (x.reshape(3, NODES, 1, 128) for x in (forward_start, adjoint_start))
    place = jnp.stack([lax.axis_index("mesh"), jnp.int32(n_mesh)]).astype(I32)
    up = [(i, (i + 1) % n_mesh) for i in range(n_mesh)]
    down = [(j, i) for i, j in up]
    ends = [((e + 1) * n_mesh - 1, (e + 1) * n_mesh) for e in range(n_event - 1)]
    ends = ends + [(j, i) for i, j in ends]

    held = [pltpu.VMEM(x.shape, F32) for x in (forward, adjoint)] + [pltpu.SemaphoreType.DMA((2,))]
    forward, adjoint = (pltpu.with_memory_space_constraint(x, pltpu.HBM) for x in (forward, adjoint))
    rim, fields = call(pack_kernel, (shape(192, 128), shape(6, 128, 128)), 1, 0, 2, held)(counts, forward, adjoint)
    before, after = lax.ppermute(rim, "mesh", up), lax.ppermute(rim, "mesh", down)
    small = (stiffness, neighbours.reshape(FACES, 1, 128), material, smoothing, projection.T, destinations)
    small = tuple(pltpu.with_memory_space_constraint(x, pltpu.HBM) for x in small)
    partial, kernel, edge, turned, stiff, pick, lift, project, wanted, near, material = call(
        own_kernel,
        (
            shape(6, 128, 128),
            shape(128, 128),
            shape(8, 128),
            shape(8, 128),
            shape(2, 128, 128, dtype=BF16),
            shape(FACES * SHEET, 128, dtype=BF16),
            shape(128, FACES * SHEET, dtype=BF16),
            shape(2, 64, 128, dtype=BF16),
            shape(8, 128),
            shape(FACES, 1, 128, dtype=I32),
            shape(8, 128),
        ),
        2,
        1,
        6,
        [pltpu.VMEM(x.shape, x.dtype) for x in small] + [pltpu.SemaphoreType.DMA((6,))],
    )(counts, place, fields, *small)

    def one_step(*refs):
        step_kernel(scale, n_mesh, *refs)

    one, strain, rim_one, chunk = call(
        one_step, (shape(3, 128, 128), shape(3, 128, 128), shape(128, 128), shape(n_mesh, 72, 128)), 2, 11
    )(counts, place, partial, kernel, before, after, near, stiff, pick, lift, project, wanted, edge)
    parts = lax.all_to_all(chunk, "mesh", 0, 0, tiled=True)

    def dense(*refs):
        dense_kernel(n_event, n_mesh, tile_width, *refs)

    partial, rim_one, edge = call(dense, (shape(4 * n_event, 128), shape(128, 128), shape(8, 128)), 1, 3)(
        place, parts, rim_one, edge
    )
    pieces = lax.all_to_all(partial.reshape(n_event, 4, 128), "event", 0, 0, tiled=True)
    before, after = lax.ppermute(rim_one, "mesh", up), lax.ppermute(rim_one, "mesh", down)
    wrap = lax.ppermute(edge, ("event", "mesh"), ends)
    final, coefs = call(last_kernel, (shape(3, NODES, 1, 128), shape(4, 8, 128)), 2, 11)(
        counts, place, fields, one, strain, before, after, near, material, turned, wrap, pick, lift
    )
    tiles = call(smooth_kernel, shape(tile_width, 64), 0, 2)(pieces, coefs)
    return final.reshape(1, 3, NODES, 128), tiles.T


def solution(mesh):
    in_specs = (
        P("event", None, None, "mesh"),
        P("event", None, None, "mesh"),
        P(),
        P(),
        P("event", "mesh"),
        P("event", None, "mesh"),
        P("event", "mesh"),
        P("event", "mesh"),
        P(None, ("event", "mesh")),
    )
    out_specs = (P("event", None, None, "mesh"), P(None, ("event", "mesh")))
    return jax.shard_map(per_device, mesh=mesh, in_specs=in_specs, out_specs=out_specs, check_vma=False)
```

```python
import math

import jax
import jax.numpy as jnp
from jax import lax
from jax.experimental import pallas as pl
from jax.experimental.pallas import tpu as pltpu
from jax.sharding import PartitionSpec as P

STEPS = 2
NODES = 125
RIM = 32
SHEET = 32
FACES = 6
F32, BF16, I32 = jnp.float32, jnp.bfloat16, jnp.int32
partner_face = (1, 0, 3, 2, 5, 4)

VMEM = pl.BlockSpec(memory_space=pltpu.VMEM)
SMEM = pl.BlockSpec(memory_space=pltpu.SMEM)
HBM = pl.BlockSpec(memory_space=pltpu.HBM)
PARAMS = pltpu.CompilerParams(vmem_limit_bytes=40 * 2**20)


def shape(*dims, dtype=F32):
    return jax.ShapeDtypeStruct(dims, dtype)


def iota(dims, axis):
    return lax.broadcasted_iota(I32, dims, axis)


def halves(x):
    high = x.astype(BF16)
    return high, (x - high.astype(F32)).astype(BF16)


def dot(a, b):
    return lax.dot_general(a, b, (((1,), (0,)), ((), ())), preferred_element_type=F32)


def face_nodes(dims, axis):
    row = iota(dims, axis)
    face, q = row // SHEET, row % SHEET
    a = sum((q >= 5 * i).astype(I32) for i in range(1, 5))
    b = q - 5 * a
    node = jnp.where(face == 0, q, q + 100)
    node = jnp.where(face == 2, 25 * a + b, node)
    node = jnp.where(face == 3, 25 * a + 20 + b, node)
    node = jnp.where(face == 4, 5 * q, node)
    node = jnp.where(face == 5, 5 * q + 4, node)
    return jnp.where(q < 25, node, -1)


def picker():
    dims = (FACES * SHEET, 128)
    return jnp.where(face_nodes(dims, 0) == iota(dims, 1), 1.0, 0.0).astype(BF16)


def lifter():
    dims = (128, FACES * SHEET)
    return jnp.where(face_nodes(dims, 1) == iota(dims, 0), 1.0, 0.0).astype(BF16)


def rows_of(ref):
    return ref.reshape(3 * NODES, 128)


def flat_of(ref):
    return ref.reshape(ref.shape[0], 128)


def padded(ref, c):
    rows = rows_of(ref)[NODES * c : NODES * (c + 1)]
    return jnp.concatenate([rows, jnp.zeros((128 - NODES, 128), F32)], axis=0)


def stacked(fields):
    high, low = halves(jnp.concatenate(fields, axis=1))
    return jnp.concatenate([high, low], axis=0)


def pack_rim(fields):
    lane = iota((128, 128), 1)
    out = fields[0]
    for k in range(1, len(fields)):
        out = jnp.where(lane < RIM * k, out, pltpu.roll(fields[k], RIM * k, 1))
    return jnp.where(lane < RIM * len(fields), out, 0.0)


def fold(x):
    return jnp.where(iota((64, 128), 1) < 64, x[:64], pltpu.roll(x[64:], 64, 1))


def live_mask(count_ref):
    return (iota((128, 128), 1) < count_ref[0, 0]).astype(F32)


def edge_row(smooth_ref):
    width = smooth_ref.shape[1]
    last = jnp.broadcast_to(smooth_ref[:, width - 1 : width], (4, 128))
    first = jnp.broadcast_to(smooth_ref[:, 0:1], (4, 128))
    lane, row = iota((4, 128), 1), iota((4, 128), 0)
    spread = jnp.where(lane == row, last, 0.0) + jnp.where(lane == row + 4, first, 0.0)
    return jnp.sum(spread, axis=0, keepdims=True)


def pack_kernel(count_ref, *refs):
    sources, rim_ref, field_ref, targets, sems = refs[:8], refs[8], refs[9], refs[10:18], refs[18]
    copies = [pltpu.make_async_copy(a, b, sems.at[i]) for i, (a, b) in enumerate(zip(sources, targets))]
    for copy in copies[6:] + copies[:6]:
        copy.start()
    for copy in copies[6:]:
        copy.wait()
    live = live_mask(count_ref)
    fields = [padded(ref, c) * live for ref in targets[6:] for c in range(3)]
    rim_ref[:128] = pack_rim(fields[:4])
    rim_ref[128:192] = fold(pack_rim(fields[4:]))
    for k in range(6):
        field_ref[k] = fields[k]
    for copy in copies[:6]:
        copy.wait()
    rim_ref[192:] = jnp.broadcast_to(edge_row(targets[3]), (8, 128))


def split_stiffness(stiff_ref):
    wide = jnp.concatenate([stiff_ref[...], jnp.zeros((NODES, 128 - NODES), F32)], axis=1)
    return halves(jnp.concatenate([wide, jnp.zeros((128 - NODES, 128), F32)], axis=0))


def columns(x):
    return [x[:, 128 * k : 128 * (k + 1)] for k in range(x.shape[1] // 128)]


def strains(high, low, x):
    return columns(dot(jnp.concatenate([high, high], axis=1), x) + dot(low, x[:128]))


def faces_of(pick, x):
    return columns(dot(jnp.concatenate([pick, pick], axis=1), x))


def take(x, index):
    return jnp.take_along_axis(x, index, axis=1, mode="promise_in_bounds")


def lift_of(lift, jumps):
    high, low = halves(jnp.concatenate([jnp.concatenate(j, axis=0) for j in jumps], axis=1))
    return columns(dot(lift, high) + dot(lift, low))


def own_jumps(place_ref, near_ref, own):
    jumps = [[] for _ in own]
    for face in range(FACES):
        p = partner_face[face]
        near = jnp.broadcast_to(near_ref[face], (SHEET, 128))
        home = near // 128 == place_ref[0]
        slot = near % 128
        for k in range(len(own)):
            here = take(own[k][SHEET * p : SHEET * (p + 1)], slot)
            jumps[k].append(jnp.where(home, here, 0.0) - own[k][SHEET * face : SHEET * (face + 1)])
    return jumps


def rim_jumps(place_ref, near_ref, rims, n):
    mine, parts = place_ref[0], place_ref[1]
    follower = jnp.where(mine + 1 == parts, 0, mine + 1)
    jumps = [[] for _ in range(n)]
    for face in range(FACES):
        p = partner_face[face]
        near = jnp.broadcast_to(near_ref[face], (SHEET, 128))
        target = near // 128
        away = target != mine
        index = near % RIM + jnp.where(target == follower, 64, 0)
        for k in range(n):
            across = take(rims[k // 2][SHEET * p : SHEET * (p + 1)], index + RIM * (k % 2))
            jumps[k].append(jnp.where(away, across, 0.0))
    return jumps


def merge(before, after):
    lane = iota(before.shape, 1)
    first = jnp.where(lane < 64, before, pltpu.roll(after, 64, 1))
    second = jnp.where(lane < 64, pltpu.roll(before, 64, 1), after)
    return first, second


def own_kernel(
    count_ref, place_ref, field_ref, stiff_ref, near_ref, material_ref, smooth_ref, project_ref, destination_ref,
    partial_ref, kernel_ref, turned_ref, stiff_out_ref, pick_ref, lift_ref, project_out_ref, wanted_ref,
):
    live = live_mask(count_ref)
    material = jnp.broadcast_to(material_ref[...], (128, 128))
    fields = [field_ref[k] for k in range(6)]
    pick, lift = picker(), lifter()
    pick_ref[...] = pick
    lift_ref[...] = lift
    x = stacked(fields)
    lifted = lift_of(lift, own_jumps(place_ref, near_ref, faces_of(pick, x)))
    high, low = split_stiffness(stiff_ref)
    stiff_out_ref[0] = high
    stiff_out_ref[1] = low
    strain = strains(high, low, x)
    for k in range(6):
        force = 0.5 * lifted[k] - material * strain[k]
        partial_ref[k] = live * (fields[k] + 0.4 * force)
    kernel_ref[...] = sum(fields[c] * strain[3 + c] for c in range(3))
    high, low = halves(jnp.concatenate([project_ref[...], jnp.zeros((64, 128 - NODES), F32)], axis=1))
    project_out_ref[0] = high
    project_out_ref[1] = low
    wanted_ref[...] = jnp.broadcast_to(destination_ref[...].astype(F32), (8, 128))
    width = smooth_ref.shape[1]
    wide = jnp.concatenate([smooth_ref[...], jnp.zeros((4, 128 - width), F32)], axis=1)
    turned_ref[...] = jnp.concatenate([wide, jnp.zeros((124, 128), F32)], axis=0).T[:8]


def step_kernel(
    scale, n_mesh,
    count_ref, place_ref, partial_ref, kernel_ref, before_ref, after_ref, near_ref, stiff_ref, pick_ref, lift_ref,
    project_ref, wanted_ref,
    forward_ref, strain_ref, rim_ref, edge_ref, chunk_ref,
):
    live = live_mask(count_ref)
    first, second = merge(before_ref[:128], after_ref[:128])
    upper, lower = merge(before_ref[128:192], after_ref[128:192])
    rims = faces_of(pick_ref[...], stacked([first, second, jnp.concatenate([upper, lower], axis=0)]))
    lift = lift_of(lift_ref[...], rim_jumps(place_ref, near_ref, rims, 6))
    fields = [partial_ref[k] + live * (0.2 * lift[k]) for k in range(6)]
    strain = strains(stiff_ref[0], stiff_ref[1], stacked(fields))
    kernel = kernel_ref[...] + sum(fields[c] * strain[3 + c] for c in range(3))
    k_high, k_low = halves(kernel)
    p_high, p_low = project_ref[0], project_ref[1]
    blocks = dot(jnp.concatenate([p_high, p_high], axis=1), jnp.concatenate([k_high, k_low], axis=0))
    blocks = (blocks + dot(p_low, k_high)) * scale
    turned = jnp.concatenate([blocks, pltpu.roll(blocks, 64, 1)], axis=0).T[:64]
    for m in range(n_mesh):
        chunk_ref[m, :64] = turned
        chunk_ref[m, 64:] = wanted_ref[...]
    rim_ref[...] = pack_rim(fields[:3])
    edge_ref[...] = jnp.where(iota((8, 128), 1) < 4, before_ref[192:], after_ref[192:])
    for c in range(3):
        forward_ref[c] = fields[c]
        strain_ref[c] = strain[c]


def dense_kernel(n_event, n_mesh, tile_width, first, place_ref, parts_ref, edge_ref, before_ref, after_ref, out_ref):
    rows = 4 * n_event
    row = iota((2 * rows, 128), 0)
    within = row % rows
    event = (within // 4 + first) % n_event
    tile = event * (n_mesh * tile_width) + within % 4 + 4 * (row // rows) - 2
    tile = tile.astype(F32) + (place_ref[0] * tile_width).astype(F32)
    lane = iota((64, 128), 1)
    left, right = [], []
    for m in range(n_mesh):
        x = parts_ref[m, :64]
        high = x.astype(BF16).astype(F32)
        low = x - high
        right.append(jnp.where(lane < 64, high, pltpu.roll(low, 64, 1)).astype(BF16))
        right.append(jnp.where(lane < 64, pltpu.roll(high, 64, 1), low).astype(BF16))
        wanted = jnp.broadcast_to(parts_ref[m, 64:65], (2 * rows, 128))
        left.append(jnp.where(wanted == tile, 1.0, 0.0).astype(BF16))
    both = dot(jnp.concatenate(left, axis=1), jnp.concatenate(right, axis=0))
    both = both + pltpu.roll(both, 64, 1)
    both = jnp.where(iota((rows, 128), 1) < 64, both[:rows], both[rows:])
    out = flat_of(out_ref)
    for p in range(n_event):
        out[5 * p : 5 * p + 4] = both[4 * p : 4 * p + 4]
        out[5 * p + 4 : 5 * p + 5] = edge_ref[0:1]


def last_kernel(
    count_ref, place_ref, field_ref, one_ref, strain_ref, before_ref, after_ref, near_ref, material_ref, turned_ref,
    edge_ref, pick_ref, lift_ref,
    final_ref, table_ref,
):
    live = live_mask(count_ref)
    material = jnp.broadcast_to(material_ref[...], (128, 128))
    fields = [one_ref[c] for c in range(3)]
    jumps = own_jumps(place_ref, near_ref, faces_of(pick_ref[...], stacked(fields)))
    rims = faces_of(pick_ref[...], stacked(list(merge(before_ref[...], after_ref[...]))))
    more = rim_jumps(place_ref, near_ref, rims, 3)
    lift = lift_of(lift_ref[...], [[a + b for a, b in zip(*pair)] for pair in zip(jumps, more)])
    final = rows_of(final_ref)
    for c in range(3):
        force = 0.5 * lift[c] - material * strain_ref[c]
        out = live * (2.0 * fields[c] - field_ref[c] + 0.4 * force)
        final[NODES * c : NODES * (c + 1)] = out[:NODES]
    tile = iota((8, 128), 0)
    table = jnp.where((tile >= 2) & (tile < 6), pltpu.roll(turned_ref[...], 2, 0), 0.0)
    table = jnp.where(tile == 1, edge_ref[...], table)
    table_ref[...] = jnp.where(tile == 6, pltpu.roll(edge_ref[...], 124, 1), table)


def total_of(parts):
    while len(parts) > 1:
        parts = [sum(parts[i : i + 2][1:], parts[i]) for i in range(0, len(parts), 2)]
    return parts[0]


def smooth_kernel(n_event, first, place_ref, x_ref, table_ref, o_ref):
    rows = flat_of(x_ref)
    mine, parts, event = place_ref[0], place_ref[1], place_ref[2]
    node, tile = iota((8, 128), 1), iota((8, 128), 0)
    table = table_ref[...]
    for row, end, there, by in ((1, mine == 0, event - 1, 0), (6, mine == parts - 1, event + 1, 124)):
        inside = (there >= 0) & (there < n_event)
        index = lax.rem(there - first + 2 * n_event, n_event)
        edge = jnp.broadcast_to(x_ref[5 * index + 4], (8, 128))
        edge = jnp.where(inside, pltpu.roll(edge, by, 1) if by else edge, 0.0)
        table = jnp.where((tile == row) & end, edge, table)
    coef = [jnp.broadcast_to(table[:, d : d + 1], (8, 128)) for d in range(4)]
    total = total_of([rows[5 * p : 5 * p + 4] for p in range(n_event)])
    x = jnp.concatenate([total, pltpu.roll(total, 64, 1)], axis=0)
    for _ in range(2):
        right = jnp.where(tile < 7, pltpu.roll(x, 7, 0), 0.0)
        left = jnp.where(tile > 0, pltpu.roll(x, 1, 0), 0.0)
        out = x + coef[0] * (left + right - 2.0 * x)
        for d, shift in ((1, 4), (2, 2), (3, 0)):
            place, stride = (node >> shift) & 3, 1 << shift
            up = jnp.where(place < 3, pltpu.roll(x, 128 - stride, 1), 0.0)
            down = jnp.where(place > 0, pltpu.roll(x, stride, 1), 0.0)
            out = out + coef[d] * (up + down - 2.0 * x)
        x = out
    o_ref[...] = x[2:6, :64]


def call(kernel, out_shape, n_smem, n_vmem, n_hbm=0, scratch=()):
    many = isinstance(out_shape, tuple)
    return pl.pallas_call(
        kernel,
        out_shape=out_shape,
        in_specs=[SMEM] * n_smem + [VMEM] * n_vmem + [HBM] * n_hbm,
        out_specs=(VMEM,) * len(out_shape) if many else VMEM,
        scratch_shapes=scratch,
        compiler_params=PARAMS,
    )


def per_device(
    forward_start, adjoint_start, stiffness, projection, material, neighbours, destinations, counts, smoothing
):
    elements = forward_start.shape[-1]
    tile_width = smoothing.shape[1]
    n_mesh, n_event = lax.axis_size("mesh"), lax.axis_size("event")
    scale = math.sqrt(tile_width / elements) / STEPS
    forward, adjoint = (x.reshape(3, NODES, 1, 128) for x in (forward_start, adjoint_start))
    place = jnp.stack([lax.axis_index("mesh"), jnp.int32(n_mesh), lax.axis_index("event")]).astype(I32)
    up = [(i, (i + 1) % n_mesh) for i in range(n_mesh)]
    down = [(j, i) for i, j in up]
    first_mesh, first_event = 5 * n_mesh // 8, n_event // 2
    mesh_group = [(i + first_mesh) % n_mesh for i in range(n_mesh)]
    event_group = [(i + first_event) % n_event for i in range(n_event)]

    inputs = (
        stiffness, neighbours.reshape(FACES, 1, 128), material, smoothing, projection.T, destinations, forward, adjoint
    )
    held = tuple(shape(*x.shape, dtype=x.dtype) for x in inputs)
    inputs = tuple(pltpu.with_memory_space_constraint(x, pltpu.HBM) for x in inputs)
    rim, fields, *small = call(
        pack_kernel, (shape(200, 128), shape(6, 128, 128)) + held, 1, 0, 8, [pltpu.SemaphoreType.DMA((8,))]
    )(counts, *inputs)
    small = small[:6]
    near, material = small[1], small[2]
    before, after = lax.ppermute(rim, "mesh", up), lax.ppermute(rim, "mesh", down)
    partial, kernel, turned, stiff, pick, lift, project, wanted = call(
        own_kernel,
        (
            shape(6, 128, 128),
            shape(128, 128),
            shape(8, 128),
            shape(2, 128, 128, dtype=BF16),
            shape(FACES * SHEET, 128, dtype=BF16),
            shape(128, FACES * SHEET, dtype=BF16),
            shape(2, 64, 128, dtype=BF16),
            shape(8, 128),
        ),
        2,
        7,
    )(counts, place, fields, *small)

    def one_step(*refs):
        step_kernel(scale, n_mesh, *refs)

    one, strain, rim_one, edge, chunk = call(
        one_step,
        (shape(3, 128, 128), shape(3, 128, 128), shape(128, 128), shape(8, 128), shape(n_mesh, 72, 128)),
        2,
        10,
    )(counts, place, partial, kernel, before, after, near, stiff, pick, lift, project, wanted)
    parts = lax.all_to_all(chunk, "mesh", 0, 0, tiled=True, axis_index_groups=[mesh_group])
    before, after = lax.ppermute(rim_one, "mesh", up), lax.ppermute(rim_one, "mesh", down)

    def dense(*refs):
        dense_kernel(n_event, n_mesh, tile_width, first_event, *refs)

    partial = call(dense, shape(5 * n_event, 1, 128), 1, 4)(place, parts, edge, before, after)
    pieces = lax.all_to_all(partial, "event", 0, 0, tiled=True, axis_index_groups=[event_group])
    final, table = call(last_kernel, (shape(3, NODES, 1, 128), shape(8, 128)), 2, 11)(
        counts, place, fields, one, strain, before, after, near, material, turned, edge, pick, lift
    )

    def smooth(*refs):
        smooth_kernel(n_event, first_event, *refs)

    tiles = call(smooth, shape(tile_width, 64), 1, 2)(place, pieces, table)
    return final.reshape(1, 3, NODES, 128), tiles.T


def solution(mesh):
    in_specs = (
        P("event", None, None, "mesh"),
        P("event", None, None, "mesh"),
        P(),
        P(),
        P("event", "mesh"),
        P("event", None, "mesh"),
        P("event", "mesh"),
        P("event", "mesh"),
        P(None, ("event", "mesh")),
    )
    out_specs = (P("event", None, None, "mesh"), P(None, ("event", "mesh")))
    return jax.shard_map(per_device, mesh=mesh, in_specs=in_specs, out_specs=out_specs, check_vma=False)
```

```python
import math

import jax
import jax.numpy as jnp
from jax import lax
from jax.experimental import pallas as pl
from jax.experimental.pallas import tpu as pltpu
from jax.sharding import PartitionSpec as P

STEPS = 2
NODES = 125
RIM = 32
SHEET = 32
FACES = 6
F32, BF16, I32 = jnp.float32, jnp.bfloat16, jnp.int32
partner_face = (1, 0, 3, 2, 5, 4)

VMEM = pl.BlockSpec(memory_space=pltpu.VMEM)
SMEM = pl.BlockSpec(memory_space=pltpu.SMEM)
HBM = pl.BlockSpec(memory_space=pltpu.HBM)
PARAMS = pltpu.CompilerParams(vmem_limit_bytes=40 * 2**20)


def shape(*dims, dtype=F32):
    return jax.ShapeDtypeStruct(dims, dtype)


def iota(dims, axis):
    return lax.broadcasted_iota(I32, dims, axis)


def halves(x):
    high = x.astype(BF16)
    return high, (x - high.astype(F32)).astype(BF16)


def dot(a, b):
    return lax.dot_general(a, b, (((1,), (0,)), ((), ())), preferred_element_type=F32)


def face_nodes(dims, axis):
    row = iota(dims, axis)
    face, q = row // SHEET, row % SHEET
    a = sum((q >= 5 * i).astype(I32) for i in range(1, 5))
    b = q - 5 * a
    node = jnp.where(face == 0, q, q + 100)
    node = jnp.where(face == 2, 25 * a + b, node)
    node = jnp.where(face == 3, 25 * a + 20 + b, node)
    node = jnp.where(face == 4, 5 * q, node)
    node = jnp.where(face == 5, 5 * q + 4, node)
    return jnp.where(q < 25, node, -1)


def picker():
    dims = (FACES * SHEET, 128)
    return jnp.where(face_nodes(dims, 0) == iota(dims, 1), 1.0, 0.0).astype(BF16)


def lifter():
    dims = (128, FACES * SHEET)
    return jnp.where(face_nodes(dims, 1) == iota(dims, 0), 1.0, 0.0).astype(BF16)


def rows_of(ref):
    return ref.reshape(3 * NODES, 128)


def flat_of(ref):
    return ref.reshape(ref.shape[0], 128)


def padded(ref, c):
    rows = rows_of(ref)[NODES * c : NODES * (c + 1)]
    return jnp.concatenate([rows, jnp.zeros((128 - NODES, 128), F32)], axis=0)


def stacked(fields):
    high, low = halves(jnp.concatenate(fields, axis=1))
    return jnp.concatenate([high, low], axis=0)


def pack_rim(fields):
    lane = iota((128, 128), 1)
    out = fields[0]
    for k in range(1, len(fields)):
        out = jnp.where(lane < RIM * k, out, pltpu.roll(fields[k], RIM * k, 1))
    return jnp.where(lane < RIM * len(fields), out, 0.0)


def fold(x):
    return jnp.where(iota((64, 128), 1) < 64, x[:64], pltpu.roll(x[64:], 64, 1))


def live_mask(count_ref):
    return (iota((128, 128), 1) < count_ref[0, 0]).astype(F32)


def edge_row(smooth_ref):
    width = smooth_ref.shape[1]
    last = jnp.broadcast_to(smooth_ref[:, width - 1 : width], (4, 128))
    first = jnp.broadcast_to(smooth_ref[:, 0:1], (4, 128))
    lane, row = iota((4, 128), 1), iota((4, 128), 0)
    spread = jnp.where(lane == row, last, 0.0) + jnp.where(lane == row + 4, first, 0.0)
    return jnp.sum(spread, axis=0, keepdims=True)


def copies_of(sources, targets, sems):
    copies = [pltpu.make_async_copy(a, b, sems.at[i]) for i, (a, b) in enumerate(zip(sources, targets))]
    for copy in copies:
        copy.start()
    return copies


def pack_kernel(count_ref, forward_ref, adjoint_ref, smooth_ref, rim_ref, field_ref, smooth_out_ref, *held):
    copies = copies_of((forward_ref, adjoint_ref, smooth_ref), (*held[:2], smooth_out_ref), held[2])
    live = live_mask(count_ref)
    fields = []
    for ref, copy in zip(held[:2], copies):
        copy.wait()
        fields += [padded(ref, c) * live for c in range(3)]
    rim_ref[:128] = pack_rim(fields[:4])
    rim_ref[128:192] = fold(pack_rim(fields[4:]))
    for k in range(6):
        field_ref[k] = fields[k]
    copies[2].wait()
    rim_ref[192:] = jnp.broadcast_to(edge_row(smooth_out_ref), (8, 128))


def split_stiffness(stiff_ref):
    wide = jnp.concatenate([stiff_ref[...], jnp.zeros((NODES, 128 - NODES), F32)], axis=1)
    return halves(jnp.concatenate([wide, jnp.zeros((128 - NODES, 128), F32)], axis=0))


def columns(x):
    return [x[:, 128 * k : 128 * (k + 1)] for k in range(x.shape[1] // 128)]


def strains(high, low, x):
    return columns(dot(jnp.concatenate([high, high], axis=1), x) + dot(low, x[:128]))


def faces_of(pick, x):
    return columns(dot(jnp.concatenate([pick, pick], axis=1), x))


def take(x, index):
    return jnp.take_along_axis(x, index, axis=1, mode="promise_in_bounds")


def lift_of(lift, jumps):
    high, low = halves(jnp.concatenate([jnp.concatenate(j, axis=0) for j in jumps], axis=1))
    return columns(dot(lift, high) + dot(lift, low))


def own_jumps(place_ref, near_ref, own):
    jumps = [[] for _ in own]
    for face in range(FACES):
        p = partner_face[face]
        near = jnp.broadcast_to(near_ref[face], (SHEET, 128))
        home = near // 128 == place_ref[0]
        slot = near % 128
        for k in range(len(own)):
            here = take(own[k][SHEET * p : SHEET * (p + 1)], slot)
            jumps[k].append(jnp.where(home, here, 0.0) - own[k][SHEET * face : SHEET * (face + 1)])
    return jumps


def rim_jumps(place_ref, near_ref, rims, n):
    mine, parts = place_ref[0], place_ref[1]
    follower = jnp.where(mine + 1 == parts, 0, mine + 1)
    jumps = [[] for _ in range(n)]
    for face in range(FACES):
        p = partner_face[face]
        near = jnp.broadcast_to(near_ref[face], (SHEET, 128))
        target = near // 128
        away = target != mine
        index = near % RIM + jnp.where(target == follower, 64, 0)
        for k in range(n):
            across = take(rims[k // 2][SHEET * p : SHEET * (p + 1)], index + RIM * (k % 2))
            jumps[k].append(jnp.where(away, across, 0.0))
    return jumps


def merge(before, after):
    lane = iota(before.shape, 1)
    first = jnp.where(lane < 64, before, pltpu.roll(after, 64, 1))
    second = jnp.where(lane < 64, pltpu.roll(before, 64, 1), after)
    return first, second


def own_kernel(
    count_ref, place_ref, field_ref, smooth_ref, near_in, stiff_in, material_in, project_in, destination_in,
    partial_ref, kernel_ref, turned_ref, stiff_out_ref, pick_ref, lift_ref, project_out_ref, wanted_ref, near_ref,
    material_ref, stiff_ref, project_ref, destination_ref, sems,
):
    copies = copies_of(
        (near_in, stiff_in, material_in, project_in, destination_in),
        (near_ref, stiff_ref, material_ref, project_ref, destination_ref),
        sems,
    )
    live = live_mask(count_ref)
    fields = [field_ref[k] for k in range(6)]
    pick, lift = picker(), lifter()
    pick_ref[...] = pick
    lift_ref[...] = lift
    x = stacked(fields)
    faces = faces_of(pick, x)
    copies[0].wait()
    lifted = lift_of(lift, own_jumps(place_ref, near_ref, faces))
    for copy in copies[1:]:
        copy.wait()
    material = jnp.broadcast_to(material_ref[...], (128, 128))
    high, low = split_stiffness(stiff_ref)
    stiff_out_ref[0] = high
    stiff_out_ref[1] = low
    strain = strains(high, low, x)
    for k in range(6):
        force = 0.5 * lifted[k] - material * strain[k]
        partial_ref[k] = live * (fields[k] + 0.4 * force)
    kernel_ref[...] = sum(fields[c] * strain[3 + c] for c in range(3))
    high, low = halves(jnp.concatenate([project_ref[...], jnp.zeros((64, 128 - NODES), F32)], axis=1))
    project_out_ref[0] = high
    project_out_ref[1] = low
    wanted_ref[...] = jnp.broadcast_to(destination_ref[...].astype(F32), (8, 128))
    width = smooth_ref.shape[1]
    wide = jnp.concatenate([smooth_ref[...], jnp.zeros((4, 128 - width), F32)], axis=1)
    turned_ref[...] = jnp.concatenate([wide, jnp.zeros((124, 128), F32)], axis=0).T[:8]


def step_kernel(
    scale, n_mesh,
    count_ref, place_ref, partial_ref, kernel_ref, before_ref, after_ref, near_ref, stiff_ref, pick_ref, lift_ref,
    project_ref, wanted_ref,
    forward_ref, strain_ref, rim_ref, edge_ref, chunk_ref,
):
    live = live_mask(count_ref)
    first, second = merge(before_ref[:128], after_ref[:128])
    upper, lower = merge(before_ref[128:192], after_ref[128:192])
    rims = faces_of(pick_ref[...], stacked([first, second, jnp.concatenate([upper, lower], axis=0)]))
    lift = lift_of(lift_ref[...], rim_jumps(place_ref, near_ref, rims, 6))
    fields = [partial_ref[k] + live * (0.2 * lift[k]) for k in range(6)]
    strain = strains(stiff_ref[0], stiff_ref[1], stacked(fields))
    kernel = kernel_ref[...] + sum(fields[c] * strain[3 + c] for c in range(3))
    k_high, k_low = halves(kernel)
    p_high, p_low = project_ref[0], project_ref[1]
    blocks = dot(jnp.concatenate([p_high, p_high], axis=1), jnp.concatenate([k_high, k_low], axis=0))
    blocks = (blocks + dot(p_low, k_high)) * scale
    turned = jnp.concatenate([blocks, pltpu.roll(blocks, 64, 1)], axis=0).T[:64]
    for m in range(n_mesh):
        chunk_ref[m, :64] = turned
        chunk_ref[m, 64:] = wanted_ref[...]
    rim_ref[...] = pack_rim(fields[:3])
    edge_ref[...] = jnp.where(iota((8, 128), 1) < 4, before_ref[192:], after_ref[192:])
    for c in range(3):
        forward_ref[c] = fields[c]
        strain_ref[c] = strain[c]


def dense_kernel(n_event, n_mesh, tile_width, first, place_ref, parts_ref, edge_ref, final_ref, out_ref):
    rows = 4 * n_event
    row = iota((2 * rows, 128), 0)
    within = row % rows
    event = (within // 4 + first) % n_event
    tile = event * (n_mesh * tile_width) + within % 4 + 4 * (row // rows) - 2
    tile = tile.astype(F32) + (place_ref[0] * tile_width).astype(F32)
    lane = iota((64, 128), 1)
    left, right = [], []
    for m in range(n_mesh):
        x = parts_ref[m, :64]
        high = x.astype(BF16).astype(F32)
        low = x - high
        right.append(jnp.where(lane < 64, high, pltpu.roll(low, 64, 1)).astype(BF16))
        right.append(jnp.where(lane < 64, pltpu.roll(high, 64, 1), low).astype(BF16))
        wanted = jnp.broadcast_to(parts_ref[m, 64:65], (2 * rows, 128))
        left.append(jnp.where(wanted == tile, 1.0, 0.0).astype(BF16))
    both = dot(jnp.concatenate(left, axis=1), jnp.concatenate(right, axis=0))
    both = both + pltpu.roll(both, 64, 1)
    both = jnp.where(iota((rows, 128), 1) < 64, both[:rows], both[rows:])
    out = flat_of(out_ref)
    lane, apart = iota((n_event, 128), 1), (iota((n_event, 128), 0) + first) % n_event - place_ref[2]
    used = ((apart == 1) & (lane < 4)) | ((apart == -1) & (lane >= 4) & (lane < 8))
    edges = jnp.where(used, jnp.broadcast_to(edge_ref[0:1], (n_event, 128)), 0.0)
    for p in range(n_event):
        out[5 * p : 5 * p + 4] = both[4 * p : 4 * p + 4]
        out[5 * p + 4 : 5 * p + 5] = edges[p : p + 1]


def last_kernel(
    count_ref, place_ref, field_ref, one_ref, strain_ref, before_ref, after_ref, near_ref, material_ref,
    pick_ref, lift_ref,
    final_ref,
):
    live = live_mask(count_ref)
    material = jnp.broadcast_to(material_ref[...], (128, 128))
    fields = [one_ref[c] for c in range(3)]
    jumps = own_jumps(place_ref, near_ref, faces_of(pick_ref[...], stacked(fields)))
    rims = faces_of(pick_ref[...], stacked(list(merge(before_ref[...], after_ref[...]))))
    more = rim_jumps(place_ref, near_ref, rims, 3)
    lift = lift_of(lift_ref[...], [[a + b for a, b in zip(*pair)] for pair in zip(jumps, more)])
    final = rows_of(final_ref)
    for c in range(3):
        force = 0.5 * lift[c] - material * strain_ref[c]
        out = live * (2.0 * fields[c] - field_ref[c] + 0.4 * force)
        final[NODES * c : NODES * (c + 1)] = out[:NODES]


def total_of(parts):
    while len(parts) > 1:
        parts = [sum(parts[i : i + 2][1:], parts[i]) for i in range(0, len(parts), 2)]
    return parts[0]


def smooth_kernel(n_event, place_ref, x_ref, turned_ref, edge_ref, o_ref):
    rows = flat_of(x_ref)
    mine, parts = place_ref[0], place_ref[1]
    node, tile = iota((8, 128), 1), iota((8, 128), 0)
    total = total_of([rows[5 * p : 5 * p + 5] for p in range(n_event)])
    lane = iota((1, 128), 1)
    beside = ((lane < 4) & (mine > 0)) | ((lane >= 4) & (mine < parts - 1))
    edge = jnp.broadcast_to(jnp.where(beside, edge_ref[0:1], total[4:5]), (8, 128))
    table = jnp.where((tile >= 2) & (tile < 6), pltpu.roll(turned_ref[...], 2, 0), 0.0)
    table = jnp.where(tile == 1, edge, table)
    table = jnp.where(tile == 6, pltpu.roll(edge, 124, 1), table)
    coef = [jnp.broadcast_to(table[:, d : d + 1], (8, 128)) for d in range(4)]
    total = total[:4]
    x = jnp.concatenate([total, pltpu.roll(total, 64, 1)], axis=0)
    for _ in range(2):
        right = jnp.where(tile < 7, pltpu.roll(x, 7, 0), 0.0)
        left = jnp.where(tile > 0, pltpu.roll(x, 1, 0), 0.0)
        out = x + coef[0] * (left + right - 2.0 * x)
        for d, shift in ((1, 4), (2, 2), (3, 0)):
            place, stride = (node >> shift) & 3, 1 << shift
            up = jnp.where(place < 3, pltpu.roll(x, 128 - stride, 1), 0.0)
            down = jnp.where(place > 0, pltpu.roll(x, stride, 1), 0.0)
            out = out + coef[d] * (up + down - 2.0 * x)
        x = out
    o_ref[...] = x[2:6, :64]


def call(kernel, out_shape, n_smem, n_vmem, n_hbm=0, scratch=()):
    many = isinstance(out_shape, tuple)
    return pl.pallas_call(
        kernel,
        out_shape=out_shape,
        in_specs=[SMEM] * n_smem + [VMEM] * n_vmem + [HBM] * n_hbm,
        out_specs=(VMEM,) * len(out_shape) if many else VMEM,
        scratch_shapes=scratch,
        compiler_params=PARAMS,
    )


def per_device(
    forward_start, adjoint_start, stiffness, projection, material, neighbours, destinations, counts, smoothing
):
    elements = forward_start.shape[-1]
    tile_width = smoothing.shape[1]
    n_mesh, n_event = lax.axis_size("mesh"), lax.axis_size("event")
    scale = math.sqrt(tile_width / elements) / STEPS
    forward, adjoint = (x.reshape(3, NODES, 1, 128) for x in (forward_start, adjoint_start))
    place = jnp.stack([lax.axis_index("mesh"), jnp.int32(n_mesh), lax.axis_index("event")]).astype(I32)
    up = [(i, (i + 1) % n_mesh) for i in range(n_mesh)]
    down = [(j, i) for i, j in up]
    first_mesh, first_event = 5 * n_mesh // 8, n_event // 2
    mesh_group = [(i + first_mesh) % n_mesh for i in range(n_mesh)]
    event_group = [(i + first_event) % n_event for i in range(n_event)]

    near, project = neighbours.reshape(FACES, 1, 128), projection.T
    inputs = (forward, adjoint, smoothing, near, stiffness, material, project, destinations)
    inputs = [pltpu.with_memory_space_constraint(x, pltpu.HBM) for x in inputs]
    rim, fields, smooth_in = call(
        pack_kernel,
        (shape(200, 128), shape(6, 128, 128), shape(4, tile_width)),
        1,
        0,
        3,
        [pltpu.VMEM(x.shape, F32) for x in (forward, adjoint)] + [pltpu.SemaphoreType.DMA((3,))],
    )(counts, *inputs[:3])
    cores = min(n_event, 2)
    planes, event = n_event // cores, lax.axis_index("event")
    is_near = (event < cores * (planes // 4 + 1)) | (event >= cores * (planes - planes // 4))
    is_near, rim = lax.optimization_barrier((is_near, rim))
    before, after = lax.ppermute(rim, "mesh", up), lax.ppermute(rim, "mesh", down)
    partial, kernel, turned, stiff, pick, lift, project, wanted, near, material = call(
        own_kernel,
        (
            shape(6, 128, 128),
            shape(128, 128),
            shape(8, 128),
            shape(2, 128, 128, dtype=BF16),
            shape(FACES * SHEET, 128, dtype=BF16),
            shape(128, FACES * SHEET, dtype=BF16),
            shape(2, 64, 128, dtype=BF16),
            shape(8, 128),
            shape(FACES, 1, 128, dtype=I32),
            shape(1, 128),
        ),
        2,
        2,
        5,
        [pltpu.VMEM(x.shape, x.dtype) for x in (stiffness, project, destinations)] + [pltpu.SemaphoreType.DMA((5,))],
    )(counts, place, fields, smooth_in, *inputs[3:])

    def one_step(*refs):
        step_kernel(scale, n_mesh, *refs)

    one, strain, rim_one, edge, chunk = call(
        one_step,
        (shape(3, 128, 128), shape(3, 128, 128), shape(128, 128), shape(8, 128), shape(n_mesh, 72, 128)),
        2,
        10,
    )(counts, place, partial, kernel, before, after, near, stiff, pick, lift, project, wanted)
    parts = lax.all_to_all(chunk, "mesh", 0, 0, tiled=True, axis_index_groups=[mesh_group])

    def last(rim_one, *rest):
        before, after = lax.ppermute(rim_one, "mesh", up), lax.ppermute(rim_one, "mesh", down)
        return call(last_kernel, shape(3, NODES, 1, 128), 2, 9)(
            counts, place, fields, one, strain, before, after, near, material, pick, lift
        )

    rim_one, parts, is_near = lax.optimization_barrier((rim_one, parts, is_near))
    final = lax.cond(is_near, last, lambda rim_one: jnp.zeros((3, NODES, 1, 128), F32), rim_one)

    def dense(*refs):
        dense_kernel(n_event, n_mesh, tile_width, first_event, *refs)

    partial = call(dense, shape(5 * n_event, 1, 128), 1, 3)(place, parts, edge, final)
    pieces = lax.all_to_all(partial, "event", 0, 0, tiled=True, axis_index_groups=[event_group])
    rim_one, final, _ = lax.optimization_barrier((rim_one, final, partial))
    final = lax.cond(is_near, lambda rim_one, final: final, last, rim_one, final)

    def smooth(*refs):
        smooth_kernel(n_event, *refs)

    tiles = call(smooth, shape(tile_width, 64), 1, 3)(place, pieces, turned, edge)
    return final.reshape(1, 3, NODES, 128), tiles.T


def solution(mesh):
    in_specs = (
        P("event", None, None, "mesh"),
        P("event", None, None, "mesh"),
        P(),
        P(),
        P("event", "mesh"),
        P("event", None, "mesh"),
        P("event", "mesh"),
        P("event", "mesh"),
        P(None, ("event", "mesh")),
    )
    out_specs = (P("event", None, None, "mesh"), P(None, ("event", "mesh")))
    return jax.shard_map(per_device, mesh=mesh, in_specs=in_specs, out_specs=out_specs, check_vma=False)
```

```python
import math

import jax
import jax.numpy as jnp
from jax import lax
from jax.experimental import pallas as pl
from jax.experimental.pallas import tpu as pltpu
from jax.sharding import PartitionSpec as P

STEPS = 2
NODES = 125
RIM = 32
SHEET = 32
FACES = 6
F32, BF16, I32 = jnp.float32, jnp.bfloat16, jnp.int32
partner_face = (1, 0, 3, 2, 5, 4)

VMEM = pl.BlockSpec(memory_space=pltpu.VMEM)
SMEM = pl.BlockSpec(memory_space=pltpu.SMEM)
HBM = pl.BlockSpec(memory_space=pltpu.HBM)
PARAMS = pltpu.CompilerParams(vmem_limit_bytes=40 * 2**20)


def shape(*dims, dtype=F32):
    return jax.ShapeDtypeStruct(dims, dtype)


def iota(dims, axis):
    return lax.broadcasted_iota(I32, dims, axis)


def halves(x):
    high = x.astype(BF16)
    return high, (x - high.astype(F32)).astype(BF16)


def dot(a, b):
    return lax.dot_general(a, b, (((1,), (0,)), ((), ())), preferred_element_type=F32)


def face_nodes(dims, axis):
    row = iota(dims, axis)
    face, q = row // SHEET, row % SHEET
    a = sum((q >= 5 * i).astype(I32) for i in range(1, 5))
    b = q - 5 * a
    node = jnp.where(face == 0, q, q + 100)
    node = jnp.where(face == 2, 25 * a + b, node)
    node = jnp.where(face == 3, 25 * a + 20 + b, node)
    node = jnp.where(face == 4, 5 * q, node)
    node = jnp.where(face == 5, 5 * q + 4, node)
    return jnp.where(q < 25, node, -1)


def picker():
    dims = (FACES * SHEET, 128)
    return jnp.where(face_nodes(dims, 0) == iota(dims, 1), 1.0, 0.0).astype(BF16)


def lifter():
    dims = (128, FACES * SHEET)
    return jnp.where(face_nodes(dims, 1) == iota(dims, 0), 1.0, 0.0).astype(BF16)


def rows_of(ref):
    return ref.reshape(3 * NODES, 128)


def flat_of(ref):
    return ref.reshape(ref.shape[0], 128)


def padded(ref, c):
    rows = rows_of(ref)[NODES * c : NODES * (c + 1)]
    return jnp.concatenate([rows, jnp.zeros((128 - NODES, 128), F32)], axis=0)


def stacked(fields):
    high, low = halves(jnp.concatenate(fields, axis=1))
    return jnp.concatenate([high, low], axis=0)


def pack_rim(fields):
    lane = iota((128, 128), 1)
    out = fields[0]
    for k in range(1, len(fields)):
        out = jnp.where(lane < RIM * k, out, pltpu.roll(fields[k], RIM * k, 1))
    return jnp.where(lane < RIM * len(fields), out, 0.0)


def fold(x):
    return jnp.where(iota((64, 128), 1) < 64, x[:64], pltpu.roll(x[64:], 64, 1))


def live_mask(count_ref):
    return (iota((128, 128), 1) < count_ref[0, 0]).astype(F32)


def edge_row(smooth_ref):
    width = smooth_ref.shape[1]
    last = jnp.broadcast_to(smooth_ref[:, width - 1 : width], (4, 128))
    first = jnp.broadcast_to(smooth_ref[:, 0:1], (4, 128))
    lane, row = iota((4, 128), 1), iota((4, 128), 0)
    spread = jnp.where(lane == row, last, 0.0) + jnp.where(lane == row + 4, first, 0.0)
    return jnp.sum(spread, axis=0, keepdims=True)


def copies_of(sources, targets, sems):
    copies = [pltpu.make_async_copy(a, b, sems.at[i]) for i, (a, b) in enumerate(zip(sources, targets))]
    for copy in copies:
        copy.start()
    return copies


def pack_kernel(count_ref, forward_ref, adjoint_ref, smooth_ref, rim_ref, field_ref, smooth_out_ref, *held):
    copies = copies_of((forward_ref, adjoint_ref, smooth_ref), (*held[:2], smooth_out_ref), held[2])
    live = live_mask(count_ref)
    fields = []
    for ref, copy in zip(held[:2], copies):
        copy.wait()
        fields += [padded(ref, c) * live for c in range(3)]
    rim_ref[:128] = pack_rim(fields[:4])
    rim_ref[128:192] = fold(pack_rim(fields[4:]))
    for k in range(6):
        field_ref[k] = fields[k]
    copies[2].wait()
    rim_ref[192:] = jnp.broadcast_to(edge_row(smooth_out_ref), (8, 128))


def split_stiffness(stiff_ref):
    wide = jnp.concatenate([stiff_ref[...], jnp.zeros((NODES, 128 - NODES), F32)], axis=1)
    return halves(jnp.concatenate([wide, jnp.zeros((128 - NODES, 128), F32)], axis=0))


def columns(x):
    return [x[:, 128 * k : 128 * (k + 1)] for k in range(x.shape[1] // 128)]


def strains(high, low, x):
    return columns(dot(jnp.concatenate([high, high], axis=1), x) + dot(low, x[:128]))


def faces_of(pick, x):
    return columns(dot(jnp.concatenate([pick, pick], axis=1), x))


def take(x, index):
    return jnp.take_along_axis(x, index, axis=1, mode="promise_in_bounds")


def lift_of(lift, jumps):
    high, low = halves(jnp.concatenate([jnp.concatenate(j, axis=0) for j in jumps], axis=1))
    return columns(dot(lift, high) + dot(lift, low))


def own_jumps(place_ref, near_ref, own):
    jumps = [[] for _ in own]
    for face in range(FACES):
        p = partner_face[face]
        near = jnp.broadcast_to(near_ref[face], (SHEET, 128))
        home = near // 128 == place_ref[0]
        slot = near % 128
        for k in range(len(own)):
            here = take(own[k][SHEET * p : SHEET * (p + 1)], slot)
            jumps[k].append(jnp.where(home, here, 0.0) - own[k][SHEET * face : SHEET * (face + 1)])
    return jumps


def rim_jumps(place_ref, near_ref, rims, n):
    mine, parts = place_ref[0], place_ref[1]
    follower = jnp.where(mine + 1 == parts, 0, mine + 1)
    jumps = [[] for _ in range(n)]
    for face in range(FACES):
        p = partner_face[face]
        near = jnp.broadcast_to(near_ref[face], (SHEET, 128))
        target = near // 128
        away = target != mine
        index = near % RIM + jnp.where(target == follower, 64, 0)
        for k in range(n):
            across = take(rims[k // 2][SHEET * p : SHEET * (p + 1)], index + RIM * (k % 2))
            jumps[k].append(jnp.where(away, across, 0.0))
    return jumps


def merge(before, after):
    lane = iota(before.shape, 1)
    first = jnp.where(lane < 64, before, pltpu.roll(after, 64, 1))
    second = jnp.where(lane < 64, pltpu.roll(before, 64, 1), after)
    return first, second


def own_kernel(
    count_ref, place_ref, field_ref, smooth_ref, near_in, stiff_in, material_in, project_in, destination_in,
    partial_ref, kernel_ref, turned_ref, stiff_out_ref, pick_ref, lift_ref, project_out_ref, wanted_ref, near_ref,
    material_ref, stiff_ref, project_ref, destination_ref, sems,
):
    copies = copies_of(
        (near_in, stiff_in, material_in, project_in, destination_in),
        (near_ref, stiff_ref, material_ref, project_ref, destination_ref),
        sems,
    )
    live = live_mask(count_ref)
    fields = [field_ref[k] for k in range(6)]
    pick, lift = picker(), lifter()
    pick_ref[...] = pick
    lift_ref[...] = lift
    x = stacked(fields)
    faces = faces_of(pick, x)
    copies[0].wait()
    lifted = lift_of(lift, own_jumps(place_ref, near_ref, faces))
    for copy in copies[1:]:
        copy.wait()
    material = jnp.broadcast_to(material_ref[...], (128, 128))
    high, low = split_stiffness(stiff_ref)
    stiff_out_ref[0] = high
    stiff_out_ref[1] = low
    strain = strains(high, low, x)
    for k in range(6):
        force = 0.5 * lifted[k] - material * strain[k]
        partial_ref[k] = live * (fields[k] + 0.4 * force)
    kernel_ref[...] = sum(fields[c] * strain[3 + c] for c in range(3))
    high, low = halves(jnp.concatenate([project_ref[...], jnp.zeros((64, 128 - NODES), F32)], axis=1))
    project_out_ref[0] = high
    project_out_ref[1] = low
    wanted_ref[...] = jnp.broadcast_to(destination_ref[...].astype(F32), (8, 128))
    width = smooth_ref.shape[1]
    wide = jnp.concatenate([smooth_ref[...], jnp.zeros((4, 128 - width), F32)], axis=1)
    turned_ref[...] = jnp.concatenate([wide, jnp.zeros((124, 128), F32)], axis=0).T[:8]


def step_kernel(
    scale, n_mesh,
    count_ref, place_ref, partial_ref, kernel_ref, before_ref, after_ref, near_ref, stiff_ref, pick_ref, lift_ref,
    project_ref, wanted_ref,
    forward_ref, strain_ref, rim_ref, edge_ref, chunk_ref,
):
    live = live_mask(count_ref)
    first, second = merge(before_ref[:128], after_ref[:128])
    upper, lower = merge(before_ref[128:192], after_ref[128:192])
    rims = faces_of(pick_ref[...], stacked([first, second, jnp.concatenate([upper, lower], axis=0)]))
    lift = lift_of(lift_ref[...], rim_jumps(place_ref, near_ref, rims, 6))
    fields = [partial_ref[k] + live * (0.2 * lift[k]) for k in range(6)]
    strain = strains(stiff_ref[0], stiff_ref[1], stacked(fields))
    kernel = kernel_ref[...] + sum(fields[c] * strain[3 + c] for c in range(3))
    k_high, k_low = halves(kernel)
    p_high, p_low = project_ref[0], project_ref[1]
    blocks = dot(jnp.concatenate([p_high, p_high], axis=1), jnp.concatenate([k_high, k_low], axis=0))
    blocks = (blocks + dot(p_low, k_high)) * scale
    turned = jnp.concatenate([blocks, pltpu.roll(blocks, 64, 1)], axis=0).T[:64]
    for m in range(n_mesh):
        chunk_ref[m, :64] = turned
        chunk_ref[m, 64:] = wanted_ref[...]
    rim_ref[...] = pack_rim(fields[:3])
    edge_ref[...] = jnp.where(iota((8, 128), 1) < 4, before_ref[192:], after_ref[192:])
    for c in range(3):
        forward_ref[c] = fields[c]
        strain_ref[c] = strain[c]


def dense_kernel(n_event, n_mesh, tile_width, first, place_ref, parts_ref, edge_ref, out_ref):
    rows = 4 * n_event
    row = iota((2 * rows, 128), 0)
    within = row % rows
    event = (within // 4 + first) % n_event
    tile = event * (n_mesh * tile_width) + within % 4 + 4 * (row // rows) - 2
    tile = tile.astype(F32) + (place_ref[0] * tile_width).astype(F32)
    lane = iota((64, 128), 1)
    left, right = [], []
    for m in range(n_mesh):
        x = parts_ref[m, :64]
        high = x.astype(BF16).astype(F32)
        low = x - high
        right.append(jnp.where(lane < 64, high, pltpu.roll(low, 64, 1)).astype(BF16))
        right.append(jnp.where(lane < 64, pltpu.roll(high, 64, 1), low).astype(BF16))
        wanted = jnp.broadcast_to(parts_ref[m, 64:65], (2 * rows, 128))
        left.append(jnp.where(wanted == tile, 1.0, 0.0).astype(BF16))
    both = dot(jnp.concatenate(left, axis=1), jnp.concatenate(right, axis=0))
    both = both + pltpu.roll(both, 64, 1)
    both = jnp.where(iota((rows, 128), 1) < 64, both[:rows], both[rows:])
    out = flat_of(out_ref)
    lane, apart = iota((n_event, 128), 1), (iota((n_event, 128), 0) + first) % n_event - place_ref[2]
    used = ((apart == 1) & (lane < 4)) | ((apart == -1) & (lane >= 4) & (lane < 8))
    edges = jnp.where(used, jnp.broadcast_to(edge_ref[0:1], (n_event, 128)), 0.0)
    for p in range(n_event):
        out[5 * p : 5 * p + 4] = both[4 * p : 4 * p + 4]
        out[5 * p + 4 : 5 * p + 5] = edges[p : p + 1]


def last_kernel(
    count_ref, place_ref, field_ref, one_ref, strain_ref, before_ref, after_ref, near_ref, material_ref,
    pick_ref, lift_ref,
    final_ref,
):
    live = live_mask(count_ref)
    material = jnp.broadcast_to(material_ref[...], (128, 128))
    fields = [one_ref[c] for c in range(3)]
    jumps = own_jumps(place_ref, near_ref, faces_of(pick_ref[...], stacked(fields)))
    rims = faces_of(pick_ref[...], stacked(list(merge(before_ref[...], after_ref[...]))))
    more = rim_jumps(place_ref, near_ref, rims, 3)
    lift = lift_of(lift_ref[...], [[a + b for a, b in zip(*pair)] for pair in zip(jumps, more)])
    final = rows_of(final_ref)
    for c in range(3):
        force = 0.5 * lift[c] - material * strain_ref[c]
        out = live * (2.0 * fields[c] - field_ref[c] + 0.4 * force)
        final[NODES * c : NODES * (c + 1)] = out[:NODES]


def total_of(parts):
    while len(parts) > 1:
        parts = [sum(parts[i : i + 2][1:], parts[i]) for i in range(0, len(parts), 2)]
    return parts[0]


def smooth_kernel(n_event, place_ref, x_ref, turned_ref, edge_ref, o_ref):
    rows = flat_of(x_ref)
    mine, parts = place_ref[0], place_ref[1]
    node, tile = iota((8, 128), 1), iota((8, 128), 0)
    span = 40 if n_event % 8 == 0 else 5 * n_event
    total = total_of([rows[i : i + span] for i in range(0, 5 * n_event, span)])
    total = total_of([total[i : i + 5] for i in range(0, span, 5)])
    lane = iota((1, 128), 1)
    beside = ((lane < 4) & (mine > 0)) | ((lane >= 4) & (mine < parts - 1))
    edge = jnp.broadcast_to(jnp.where(beside, edge_ref[0:1], total[4:5]), (8, 128))
    table = jnp.where((tile >= 2) & (tile < 6), pltpu.roll(turned_ref[...], 2, 0), 0.0)
    table = jnp.where(tile == 1, edge, table)
    table = jnp.where(tile == 6, pltpu.roll(edge, 124, 1), table)
    coef = [jnp.broadcast_to(table[:, d : d + 1], (8, 128)) for d in range(4)]
    total = total[:4]
    x = jnp.concatenate([total, pltpu.roll(total, 64, 1)], axis=0)
    for _ in range(2):
        right = jnp.where(tile < 7, pltpu.roll(x, 7, 0), 0.0)
        left = jnp.where(tile > 0, pltpu.roll(x, 1, 0), 0.0)
        out = x + coef[0] * (left + right - 2.0 * x)
        for d, shift in ((1, 4), (2, 2), (3, 0)):
            place, stride = (node >> shift) & 3, 1 << shift
            up = jnp.where(place < 3, pltpu.roll(x, 128 - stride, 1), 0.0)
            down = jnp.where(place > 0, pltpu.roll(x, stride, 1), 0.0)
            out = out + coef[d] * (up + down - 2.0 * x)
        x = out
    o_ref[...] = x[2:6, :64]


def call(kernel, out_shape, n_smem, n_vmem, n_hbm=0, scratch=()):
    many = isinstance(out_shape, tuple)
    return pl.pallas_call(
        kernel,
        out_shape=out_shape,
        in_specs=[SMEM] * n_smem + [VMEM] * n_vmem + [HBM] * n_hbm,
        out_specs=(VMEM,) * len(out_shape) if many else VMEM,
        scratch_shapes=scratch,
        compiler_params=PARAMS,
    )


def per_device(
    forward_start, adjoint_start, stiffness, projection, material, neighbours, destinations, counts, smoothing
):
    elements = forward_start.shape[-1]
    tile_width = smoothing.shape[1]
    n_mesh, n_event = lax.axis_size("mesh"), lax.axis_size("event")
    scale = math.sqrt(tile_width / elements) / STEPS
    forward, adjoint = (x.reshape(3, NODES, 1, 128) for x in (forward_start, adjoint_start))
    place = jnp.stack([lax.axis_index("mesh"), jnp.int32(n_mesh), lax.axis_index("event")]).astype(I32)
    up = [(i, (i + 1) % n_mesh) for i in range(n_mesh)]
    down = [(j, i) for i, j in up]
    first_mesh, first_event = 5 * n_mesh // 8, n_event // 2
    mesh_group = [(i + first_mesh) % n_mesh for i in range(n_mesh)]
    event_group = [(i + first_event) % n_event for i in range(n_event)]

    near, project = neighbours.reshape(FACES, 1, 128), projection.T
    inputs = (forward, adjoint, smoothing, near, stiffness, material, project, destinations)
    inputs = [pltpu.with_memory_space_constraint(x, pltpu.HBM) for x in inputs]
    rim, fields, smooth_in = call(
        pack_kernel,
        (shape(200, 128), shape(6, 128, 128), shape(4, tile_width)),
        1,
        0,
        3,
        [pltpu.VMEM(x.shape, F32) for x in (forward, adjoint)] + [pltpu.SemaphoreType.DMA((3,))],
    )(counts, *inputs[:3])
    cores = min(n_event, 2)
    event = lax.axis_index("event")
    is_near = event < cores
    is_near, rim = lax.optimization_barrier((is_near, rim))
    before, after = lax.ppermute(rim, "mesh", up), lax.ppermute(rim, "mesh", down)
    partial, kernel, turned, stiff, pick, lift, project, wanted, near, material = call(
        own_kernel,
        (
            shape(6, 128, 128),
            shape(128, 128),
            shape(8, 128),
            shape(2, 128, 128, dtype=BF16),
            shape(FACES * SHEET, 128, dtype=BF16),
            shape(128, FACES * SHEET, dtype=BF16),
            shape(2, 64, 128, dtype=BF16),
            shape(8, 128),
            shape(FACES, 1, 128, dtype=I32),
            shape(1, 128),
        ),
        2,
        2,
        5,
        [pltpu.VMEM(x.shape, x.dtype) for x in (stiffness, project, destinations)] + [pltpu.SemaphoreType.DMA((5,))],
    )(counts, place, fields, smooth_in, *inputs[3:])

    def one_step(*refs):
        step_kernel(scale, n_mesh, *refs)

    one, strain, rim_one, edge, chunk = call(
        one_step,
        (shape(3, 128, 128), shape(3, 128, 128), shape(128, 128), shape(8, 128), shape(n_mesh, 72, 128)),
        2,
        10,
    )(counts, place, partial, kernel, before, after, near, stiff, pick, lift, project, wanted)
    def halo(rim_one, *_):
        return lax.ppermute(rim_one, "mesh", up), lax.ppermute(rim_one, "mesh", down)

    none = jnp.zeros((128, 128), F32)
    sides = lax.cond(is_near, halo, lambda rim_one: (none, none), rim_one)
    chunk, sides = lax.optimization_barrier((chunk, sides))
    parts = lax.all_to_all(chunk, "mesh", 0, 0, tiled=True, axis_index_groups=[mesh_group])

    def dense(*refs):
        dense_kernel(n_event, n_mesh, tile_width, first_event, *refs)

    partial = call(dense, shape(5 * n_event, 1, 128), 1, 2)(place, parts, edge)
    pieces = lax.all_to_all(partial, "event", 0, 0, tiled=True, axis_index_groups=[event_group])
    rim_one, is_near, _ = lax.optimization_barrier((rim_one, is_near, partial))
    before, after = lax.cond(is_near, lambda rim_one, sides: sides, halo, rim_one, sides)
    final = call(last_kernel, shape(3, NODES, 1, 128), 2, 9)(
        counts, place, fields, one, strain, before, after, near, material, pick, lift
    )

    def smooth(*refs):
        smooth_kernel(n_event, *refs)

    tiles = call(smooth, shape(tile_width, 64), 1, 3)(place, pieces, turned, edge)
    return final.reshape(1, 3, NODES, 128), tiles.T


def solution(mesh):
    in_specs = (
        P("event", None, None, "mesh"),
        P("event", None, None, "mesh"),
        P(),
        P(),
        P("event", "mesh"),
        P("event", None, "mesh"),
        P("event", "mesh"),
        P("event", "mesh"),
        P(None, ("event", "mesh")),
    )
    out_specs = (P("event", None, None, "mesh"), P(None, ("event", "mesh")))
    return jax.shard_map(per_device, mesh=mesh, in_specs=in_specs, out_specs=out_specs, check_vma=False)
```

```python
import math

import jax
import jax.numpy as jnp
from jax import lax
from jax.experimental import pallas as pl
from jax.experimental.pallas import tpu as pltpu
from jax.sharding import PartitionSpec as P

STEPS = 2
NODES = 125
RIM = 32
SHEET = 32
FACES = 6
F32, BF16, I32 = jnp.float32, jnp.bfloat16, jnp.int32
partner_face = (1, 0, 3, 2, 5, 4)

VMEM = pl.BlockSpec(memory_space=pltpu.VMEM)
SMEM = pl.BlockSpec(memory_space=pltpu.SMEM)
HBM = pl.BlockSpec(memory_space=pltpu.HBM)
PARAMS = pltpu.CompilerParams(vmem_limit_bytes=40 * 2**20)


def shape(*dims, dtype=F32):
    return jax.ShapeDtypeStruct(dims, dtype)


def iota(dims, axis):
    return lax.broadcasted_iota(I32, dims, axis)


def halves(x):
    high = x.astype(BF16)
    return high, (x - high.astype(F32)).astype(BF16)


def dot(a, b):
    return lax.dot_general(a, b, (((1,), (0,)), ((), ())), preferred_element_type=F32)


def face_nodes(dims, axis):
    row = iota(dims, axis)
    face, q = row // SHEET, row % SHEET
    a = sum((q >= 5 * i).astype(I32) for i in range(1, 5))
    b = q - 5 * a
    node = jnp.where(face == 0, q, q + 100)
    node = jnp.where(face == 2, 25 * a + b, node)
    node = jnp.where(face == 3, 25 * a + 20 + b, node)
    node = jnp.where(face == 4, 5 * q, node)
    node = jnp.where(face == 5, 5 * q + 4, node)
    return jnp.where(q < 25, node, -1)


def picker():
    dims = (FACES * SHEET, 128)
    return jnp.where(face_nodes(dims, 0) == iota(dims, 1), 1.0, 0.0).astype(BF16)


def lifter():
    dims = (128, FACES * SHEET)
    return jnp.where(face_nodes(dims, 1) == iota(dims, 0), 1.0, 0.0).astype(BF16)


def rows_of(ref):
    return ref.reshape(3 * NODES, 128)


def padded(ref, c):
    rows = rows_of(ref)[NODES * c : NODES * (c + 1)]
    return jnp.concatenate([rows, jnp.zeros((128 - NODES, 128), F32)], axis=0)


def stacked(fields):
    high, low = halves(jnp.concatenate(fields, axis=1))
    return jnp.concatenate([high, low], axis=0)


def pack_rim(fields):
    lane = iota((128, 128), 1)
    out = fields[0]
    for k in range(1, len(fields)):
        out = jnp.where(lane < RIM * k, out, pltpu.roll(fields[k], RIM * k, 1))
    return jnp.where(lane < RIM * len(fields), out, 0.0)


def fold(x):
    return jnp.where(iota((64, 128), 1) < 64, x[:64], pltpu.roll(x[64:], 64, 1))


def live_mask(count_ref):
    return (iota((128, 128), 1) < count_ref[0, 0]).astype(F32)


def edge_row(smooth_ref):
    width = smooth_ref.shape[1]
    last = jnp.broadcast_to(smooth_ref[:, width - 1 : width], (4, 128))
    first = jnp.broadcast_to(smooth_ref[:, 0:1], (4, 128))
    lane, row = iota((4, 128), 1), iota((4, 128), 0)
    spread = jnp.where(lane == row, last, 0.0) + jnp.where(lane == row + 4, first, 0.0)
    return jnp.sum(spread, axis=0, keepdims=True)


def copies_of(sources, targets, sems):
    copies = [pltpu.make_async_copy(a, b, sems.at[i]) for i, (a, b) in enumerate(zip(sources, targets))]
    for copy in copies:
        copy.start()
    return copies


def pack_kernel(count_ref, forward_ref, adjoint_ref, smooth_ref, rim_ref, field_ref, smooth_out_ref, *held):
    copies = copies_of((forward_ref, adjoint_ref, smooth_ref), (*held[:2], smooth_out_ref), held[2])
    live = live_mask(count_ref)
    fields = []
    for ref, copy in zip(held[:2], copies):
        copy.wait()
        fields += [padded(ref, c) * live for c in range(3)]
    rim_ref[:128] = pack_rim(fields[:4])
    rim_ref[128:192] = fold(pack_rim(fields[4:]))
    for k in range(6):
        field_ref[k] = fields[k]
    copies[2].wait()
    rim_ref[192:] = jnp.broadcast_to(edge_row(smooth_out_ref), (8, 128))


def split_stiffness(stiff_ref):
    wide = jnp.concatenate([stiff_ref[...], jnp.zeros((NODES, 128 - NODES), F32)], axis=1)
    return halves(jnp.concatenate([wide, jnp.zeros((128 - NODES, 128), F32)], axis=0))


def columns(x):
    return [x[:, 128 * k : 128 * (k + 1)] for k in range(x.shape[1] // 128)]


def strains(high, low, x):
    return columns(dot(jnp.concatenate([high, high], axis=1), x) + dot(low, x[:128]))


def faces_of(pick, x):
    return columns(dot(jnp.concatenate([pick, pick], axis=1), x))


def take(x, index):
    return jnp.take_along_axis(x, index, axis=1, mode="promise_in_bounds")


def lift_of(lift, jumps):
    high, low = halves(jnp.concatenate([jnp.concatenate(j, axis=0) for j in jumps], axis=1))
    return columns(dot(lift, high) + dot(lift, low))


def own_jumps(place_ref, near_ref, own):
    jumps = [[] for _ in own]
    for face in range(FACES):
        p = partner_face[face]
        near = jnp.broadcast_to(near_ref[face], (SHEET, 128))
        home = near // 128 == place_ref[0]
        slot = near % 128
        for k in range(len(own)):
            here = take(own[k][SHEET * p : SHEET * (p + 1)], slot)
            jumps[k].append(jnp.where(home, here, 0.0) - own[k][SHEET * face : SHEET * (face + 1)])
    return jumps


def rim_jumps(place_ref, near_ref, rims, n):
    mine, parts = place_ref[0], place_ref[1]
    follower = jnp.where(mine + 1 == parts, 0, mine + 1)
    jumps = [[] for _ in range(n)]
    for face in range(FACES):
        p = partner_face[face]
        near = jnp.broadcast_to(near_ref[face], (SHEET, 128))
        target = near // 128
        away = target != mine
        index = near % RIM + jnp.where(target == follower, 64, 0)
        for k in range(n):
            across = take(rims[k // 2][SHEET * p : SHEET * (p + 1)], index + RIM * (k % 2))
            jumps[k].append(jnp.where(away, across, 0.0))
    return jumps


def merge(before, after):
    lane = iota(before.shape, 1)
    first = jnp.where(lane < 64, before, pltpu.roll(after, 64, 1))
    second = jnp.where(lane < 64, pltpu.roll(before, 64, 1), after)
    return first, second


def own_kernel(
    count_ref, place_ref, field_ref, smooth_ref, near_in, stiff_in, material_in, project_in, destination_in,
    partial_ref, kernel_ref, turned_ref, stiff_out_ref, pick_ref, lift_ref, project_out_ref, wanted_ref, near_ref,
    material_ref, stiff_ref, project_ref, destination_ref, sems,
):
    copies = copies_of(
        (near_in, stiff_in, material_in, project_in, destination_in),
        (near_ref, stiff_ref, material_ref, project_ref, destination_ref),
        sems,
    )
    live = live_mask(count_ref)
    fields = [field_ref[k] for k in range(6)]
    pick, lift = picker(), lifter()
    pick_ref[...] = pick
    lift_ref[...] = lift
    x = stacked(fields)
    faces = faces_of(pick, x)
    copies[0].wait()
    lifted = lift_of(lift, own_jumps(place_ref, near_ref, faces))
    for copy in copies[1:]:
        copy.wait()
    material = jnp.broadcast_to(material_ref[...], (128, 128))
    high, low = split_stiffness(stiff_ref)
    stiff_out_ref[0] = high
    stiff_out_ref[1] = low
    strain = strains(high, low, x)
    for k in range(6):
        force = 0.5 * lifted[k] - material * strain[k]
        partial_ref[k] = live * (fields[k] + 0.4 * force)
    kernel_ref[...] = sum(fields[c] * strain[3 + c] for c in range(3))
    high, low = halves(jnp.concatenate([project_ref[...], jnp.zeros((64, 128 - NODES), F32)], axis=1))
    project_out_ref[0] = high
    project_out_ref[1] = low
    wanted_ref[...] = jnp.broadcast_to(destination_ref[...].astype(F32), (8, 128))
    width = smooth_ref.shape[1]
    wide = jnp.concatenate([smooth_ref[...], jnp.zeros((4, 128 - width), F32)], axis=1)
    turned_ref[...] = jnp.concatenate([wide, jnp.zeros((124, 128), F32)], axis=0).T[:8]


def step_kernel(
    scale, n_mesh,
    count_ref, place_ref, partial_ref, kernel_ref, before_ref, after_ref, near_ref, stiff_ref, pick_ref, lift_ref,
    project_ref, wanted_ref,
    forward_ref, strain_ref, rim_ref, edge_ref, chunk_ref,
):
    live = live_mask(count_ref)
    first, second = merge(before_ref[:128], after_ref[:128])
    upper, lower = merge(before_ref[128:192], after_ref[128:192])
    rims = faces_of(pick_ref[...], stacked([first, second, jnp.concatenate([upper, lower], axis=0)]))
    lift = lift_of(lift_ref[...], rim_jumps(place_ref, near_ref, rims, 6))
    fields = [partial_ref[k] + live * (0.2 * lift[k]) for k in range(6)]
    strain = strains(stiff_ref[0], stiff_ref[1], stacked(fields))
    kernel = kernel_ref[...] + sum(fields[c] * strain[3 + c] for c in range(3))
    k_high, k_low = halves(kernel)
    p_high, p_low = project_ref[0], project_ref[1]
    blocks = dot(jnp.concatenate([p_high, p_high], axis=1), jnp.concatenate([k_high, k_low], axis=0))
    blocks = (blocks + dot(p_low, k_high)) * scale
    turned = jnp.concatenate([blocks, pltpu.roll(blocks, 64, 1)], axis=0).T[:64]
    for m in range(n_mesh):
        chunk_ref[m, :64] = turned
        chunk_ref[m, 64:] = wanted_ref[...]
    rim_ref[...] = pack_rim(fields[:3])
    edge_ref[...] = jnp.where(iota((8, 128), 1) < 4, before_ref[192:], after_ref[192:])
    for c in range(3):
        forward_ref[c] = fields[c]
        strain_ref[c] = strain[c]


def dense_kernel(n_event, n_mesh, tile_width, first, place_ref, parts_ref, edge_ref, out_ref):
    rows = 4 * n_event
    row = iota((2 * rows, 128), 0)
    within = row % rows
    event = (within // 4 + first) % n_event
    tile = event * (n_mesh * tile_width) + within % 4 + 4 * (row // rows) - 2
    tile = tile.astype(F32) + (place_ref[0] * tile_width).astype(F32)
    lane = iota((64, 128), 1)
    left, right = [], []
    for m in range(n_mesh):
        x = parts_ref[m, :64]
        high = x.astype(BF16).astype(F32)
        low = x - high
        right.append(jnp.where(lane < 64, high, pltpu.roll(low, 64, 1)).astype(BF16))
        right.append(jnp.where(lane < 64, pltpu.roll(high, 64, 1), low).astype(BF16))
        wanted = jnp.broadcast_to(parts_ref[m, 64:65], (2 * rows, 128))
        left.append(jnp.where(wanted == tile, 1.0, 0.0).astype(BF16))
    both = dot(jnp.concatenate(left, axis=1), jnp.concatenate(right, axis=0))
    both = both + pltpu.roll(both, 64, 1)
    both = jnp.where(iota((rows, 128), 1) < 64, both[:rows], both[rows:])
    lane, apart = iota((n_event, 128), 1), (iota((n_event, 128), 0) + first) % n_event - place_ref[2]
    used = ((apart == 1) & (lane < 4)) | ((apart == -1) & (lane >= 4) & (lane < 8))
    edges = jnp.where(used, jnp.broadcast_to(edge_ref[0:1], (n_event, 128)), 0.0)
    for p in range(n_event):
        out_ref[5 * p : 5 * p + 4] = both[4 * p : 4 * p + 4]
        out_ref[5 * p + 4 : 5 * p + 5] = edges[p : p + 1]


def last_own_kernel(
    count_ref, place_ref, field_ref, one_ref, strain_ref, near_ref, material_ref, pick_ref, lift_ref, partial_ref
):
    live = live_mask(count_ref)
    material = jnp.broadcast_to(material_ref[...], (128, 128))
    fields = [one_ref[c] for c in range(3)]
    lift = lift_of(lift_ref[...], own_jumps(place_ref, near_ref, faces_of(pick_ref[...], stacked(fields))))
    for c in range(3):
        force = 0.5 * lift[c] - material * strain_ref[c]
        partial_ref[c] = live * (2.0 * fields[c] - field_ref[c] + 0.4 * force)


def last_kernel(count_ref, place_ref, partial_ref, before_ref, after_ref, near_ref, pick_ref, lift_ref, final_ref):
    live = live_mask(count_ref)
    rims = faces_of(pick_ref[...], stacked(list(merge(before_ref[...], after_ref[...]))))
    lift = lift_of(lift_ref[...], rim_jumps(place_ref, near_ref, rims, 3))
    final = rows_of(final_ref)
    for c in range(3):
        out = partial_ref[c] + live * (0.2 * lift[c])
        final[NODES * c : NODES * (c + 1)] = out[:NODES]


def total_of(parts):
    while len(parts) > 1:
        parts = [sum(parts[i : i + 2][1:], parts[i]) for i in range(0, len(parts), 2)]
    return parts[0]


def smooth_kernel(n_event, place_ref, x_ref, turned_ref, edge_ref, o_ref):
    mine, parts = place_ref[0], place_ref[1]
    node, tile = iota((8, 128), 1), iota((8, 128), 0)
    span = 40 if n_event % 8 == 0 else 5 * n_event
    total = total_of([x_ref[i : i + span] for i in range(0, 5 * n_event, span)])
    total = total_of([total[i : i + 5] for i in range(0, span, 5)])
    lane = iota((1, 128), 1)
    beside = ((lane < 4) & (mine > 0)) | ((lane >= 4) & (mine < parts - 1))
    edge = jnp.broadcast_to(jnp.where(beside, edge_ref[0:1], total[4:5]), (8, 128))
    table = jnp.where((tile >= 2) & (tile < 6), pltpu.roll(turned_ref[...], 2, 0), 0.0)
    table = jnp.where(tile == 1, edge, table)
    table = jnp.where(tile == 6, pltpu.roll(edge, 124, 1), table)
    coef = [jnp.broadcast_to(table[:, d : d + 1], (8, 128)) for d in range(4)]
    total = total[:4]
    x = jnp.concatenate([total, pltpu.roll(total, 64, 1)], axis=0)
    for _ in range(2):
        right = jnp.where(tile < 7, pltpu.roll(x, 7, 0), 0.0)
        left = jnp.where(tile > 0, pltpu.roll(x, 1, 0), 0.0)
        out = x + coef[0] * (left + right - 2.0 * x)
        for d, shift in ((1, 4), (2, 2), (3, 0)):
            place, stride = (node >> shift) & 3, 1 << shift
            up = jnp.where(place < 3, pltpu.roll(x, 128 - stride, 1), 0.0)
            down = jnp.where(place > 0, pltpu.roll(x, stride, 1), 0.0)
            out = out + coef[d] * (up + down - 2.0 * x)
        x = out
    o_ref[...] = x[2:6, :64]


def call(kernel, out_shape, n_smem, n_vmem, n_hbm=0, scratch=()):
    many = isinstance(out_shape, tuple)
    return pl.pallas_call(
        kernel,
        out_shape=out_shape,
        in_specs=[SMEM] * n_smem + [VMEM] * n_vmem + [HBM] * n_hbm,
        out_specs=(VMEM,) * len(out_shape) if many else VMEM,
        scratch_shapes=scratch,
        compiler_params=PARAMS,
    )


def per_device(
    forward_start, adjoint_start, stiffness, projection, material, neighbours, destinations, counts, smoothing
):
    elements = forward_start.shape[-1]
    tile_width = smoothing.shape[1]
    n_mesh, n_event = lax.axis_size("mesh"), lax.axis_size("event")
    scale = math.sqrt(tile_width / elements) / STEPS
    forward, adjoint = (x.reshape(3, NODES, 1, 128) for x in (forward_start, adjoint_start))
    place = jnp.stack([lax.axis_index("mesh"), jnp.int32(n_mesh), lax.axis_index("event")]).astype(I32)
    up = [(i, (i + 1) % n_mesh) for i in range(n_mesh)]
    down = [(j, i) for i, j in up]
    first_mesh, first_event = 5 * n_mesh // 8, 3 * n_event // 4
    mesh_group = [(i + first_mesh) % n_mesh for i in range(n_mesh)]
    event_group = [(i + first_event) % n_event for i in range(n_event)]

    near, project = neighbours.reshape(FACES, 1, 128), projection.T
    inputs = (forward, adjoint, smoothing, near, stiffness, material, project, destinations)
    inputs = [pltpu.with_memory_space_constraint(x, pltpu.HBM) for x in inputs]
    rim, fields, smooth_in = call(
        pack_kernel,
        (shape(200, 128), shape(6, 128, 128), shape(4, tile_width)),
        1,
        0,
        3,
        [pltpu.VMEM(x.shape, F32) for x in (forward, adjoint)] + [pltpu.SemaphoreType.DMA((3,))],
    )(counts, *inputs[:3])
    before, after = lax.ppermute(rim, "mesh", up), lax.ppermute(rim, "mesh", down)
    partial, kernel, turned, stiff, pick, lift, project, wanted, near, material = call(
        own_kernel,
        (
            shape(6, 128, 128),
            shape(128, 128),
            shape(8, 128),
            shape(2, 128, 128, dtype=BF16),
            shape(FACES * SHEET, 128, dtype=BF16),
            shape(128, FACES * SHEET, dtype=BF16),
            shape(2, 64, 128, dtype=BF16),
            shape(8, 128),
            shape(FACES, 1, 128, dtype=I32),
            shape(1, 128),
        ),
        2,
        2,
        5,
        [pltpu.VMEM(x.shape, x.dtype) for x in (stiffness, project, destinations)] + [pltpu.SemaphoreType.DMA((5,))],
    )(counts, place, fields, smooth_in, *inputs[3:])

    def one_step(*refs):
        step_kernel(scale, n_mesh, *refs)

    one, strain, rim_one, edge, chunk = call(
        one_step,
        (shape(3, 128, 128), shape(3, 128, 128), shape(128, 128), shape(8, 128), shape(n_mesh, 72, 128)),
        2,
        10,
    )(counts, place, partial, kernel, before, after, near, stiff, pick, lift, project, wanted)
    parts = lax.all_to_all(chunk, "mesh", 0, 0, tiled=True, axis_index_groups=[mesh_group])

    def dense(*refs):
        dense_kernel(n_event, n_mesh, tile_width, first_event, *refs)

    partial = call(dense, shape(5 * n_event, 128), 1, 2)(place, parts, edge)
    pieces = lax.all_to_all(partial.reshape(-1, 1, 128), "event", 0, 0, tiled=True, axis_index_groups=[event_group])
    pieces = pieces.reshape(-1, 128)
    rim_one, one, _ = lax.optimization_barrier((rim_one, one, partial))
    before, after = lax.ppermute(rim_one, "mesh", up), lax.ppermute(rim_one, "mesh", down)
    partial = call(last_own_kernel, shape(3, 128, 128), 2, 7)(
        counts, place, fields, one, strain, near, material, pick, lift
    )
    final = call(last_kernel, shape(3, NODES, 1, 128), 2, 6)(
        counts, place, partial, before, after, near, pick, lift
    )

    def smooth(*refs):
        smooth_kernel(n_event, *refs)

    tiles = call(smooth, shape(tile_width, 64), 1, 3)(place, pieces, turned, edge)
    return final.reshape(1, 3, NODES, 128), tiles.T


def solution(mesh):
    in_specs = (
        P("event", None, None, "mesh"),
        P("event", None, None, "mesh"),
        P(),
        P(),
        P("event", "mesh"),
        P("event", None, "mesh"),
        P("event", "mesh"),
        P("event", "mesh"),
        P(None, ("event", "mesh")),
    )
    out_specs = (P("event", None, None, "mesh"), P(None, ("event", "mesh")))
    return jax.shard_map(per_device, mesh=mesh, in_specs=in_specs, out_specs=out_specs, check_vma=False)
```

```python
import math

import jax
import jax.numpy as jnp
from jax import lax
from jax.experimental import pallas as pl
from jax.experimental.pallas import tpu as pltpu
from jax.sharding import PartitionSpec as P

STEPS = 2
NODES = 125
RIM = 32
SHEET = 32
FACES = 6
F32, BF16, I32 = jnp.float32, jnp.bfloat16, jnp.int32
partner_face = (1, 0, 3, 2, 5, 4)

VMEM = pl.BlockSpec(memory_space=pltpu.VMEM)
SMEM = pl.BlockSpec(memory_space=pltpu.SMEM)
HBM = pl.BlockSpec(memory_space=pltpu.HBM)
PARAMS = pltpu.CompilerParams(vmem_limit_bytes=40 * 2**20)


def shape(*dims, dtype=F32):
    return jax.ShapeDtypeStruct(dims, dtype)


def iota(dims, axis):
    return lax.broadcasted_iota(I32, dims, axis)


def halves(x):
    high = x.astype(BF16)
    return high, (x - high.astype(F32)).astype(BF16)


def dot(a, b):
    return lax.dot_general(a, b, (((1,), (0,)), ((), ())), preferred_element_type=F32)


def face_nodes(dims, axis):
    row = iota(dims, axis)
    face, q = row // SHEET, row % SHEET
    a = sum((q >= 5 * i).astype(I32) for i in range(1, 5))
    b = q - 5 * a
    node = jnp.where(face == 0, q, q + 100)
    node = jnp.where(face == 2, 25 * a + b, node)
    node = jnp.where(face == 3, 25 * a + 20 + b, node)
    node = jnp.where(face == 4, 5 * q, node)
    node = jnp.where(face == 5, 5 * q + 4, node)
    return jnp.where(q < 25, node, -1)


def picker():
    dims = (FACES * SHEET, 128)
    return jnp.where(face_nodes(dims, 0) == iota(dims, 1), 1.0, 0.0).astype(BF16)


def lifter():
    dims = (128, FACES * SHEET)
    return jnp.where(face_nodes(dims, 1) == iota(dims, 0), 1.0, 0.0).astype(BF16)


def rows_of(ref):
    return ref.reshape(3 * NODES, 128)


def padded(ref, c):
    rows = rows_of(ref)[NODES * c : NODES * (c + 1)]
    return jnp.concatenate([rows, jnp.zeros((128 - NODES, 128), F32)], axis=0)


def stacked(fields):
    high, low = halves(jnp.concatenate(fields, axis=1))
    return jnp.concatenate([high, low], axis=0)


def pack_rim(fields):
    lane = iota((128, 128), 1)
    out = fields[0]
    for k in range(1, len(fields)):
        out = jnp.where(lane < RIM * k, out, pltpu.roll(fields[k], RIM * k, 1))
    return jnp.where(lane < RIM * len(fields), out, 0.0)


def fold(x):
    return jnp.where(iota((64, 128), 1) < 64, x[:64], pltpu.roll(x[64:], 64, 1))


def live_mask(count_ref):
    return (iota((128, 128), 1) < count_ref[0, 0]).astype(F32)


def edge_row(smooth_ref):
    width = smooth_ref.shape[1]
    last = jnp.broadcast_to(smooth_ref[:, width - 1 : width], (4, 128))
    first = jnp.broadcast_to(smooth_ref[:, 0:1], (4, 128))
    lane, row = iota((4, 128), 1), iota((4, 128), 0)
    spread = jnp.where(lane == row, last, 0.0) + jnp.where(lane == row + 4, first, 0.0)
    return jnp.sum(spread, axis=0, keepdims=True)


def copies_of(sources, targets, sems):
    copies = [pltpu.make_async_copy(a, b, sems.at[i]) for i, (a, b) in enumerate(zip(sources, targets))]
    for copy in copies:
        copy.start()
    return copies


def pack_kernel(count_ref, forward_ref, adjoint_ref, smooth_ref, rim_ref, field_ref, smooth_out_ref, *held):
    copies = copies_of((forward_ref, adjoint_ref, smooth_ref), (*held[:2], smooth_out_ref), held[2])
    live = live_mask(count_ref)
    fields = []
    for ref, copy in zip(held[:2], copies):
        copy.wait()
        fields += [padded(ref, c) * live for c in range(3)]
    rim_ref[:128] = pack_rim(fields[:4])
    rim_ref[128:192] = fold(pack_rim(fields[4:]))
    for k in range(6):
        field_ref[k] = fields[k]
    copies[2].wait()
    rim_ref[192:] = jnp.broadcast_to(edge_row(smooth_out_ref), (8, 128))


def split_stiffness(stiff_ref):
    wide = jnp.concatenate([stiff_ref[...], jnp.zeros((NODES, 128 - NODES), F32)], axis=1)
    return halves(jnp.concatenate([wide, jnp.zeros((128 - NODES, 128), F32)], axis=0))


def columns(x):
    return [x[:, 128 * k : 128 * (k + 1)] for k in range(x.shape[1] // 128)]


def strains(high, low, x):
    return columns(dot(jnp.concatenate([high, high], axis=1), x) + dot(low, x[:128]))


def faces_of(pick, x):
    return columns(dot(jnp.concatenate([pick, pick], axis=1), x))


def take(x, index):
    return jnp.take_along_axis(x, index, axis=1, mode="promise_in_bounds")


def lift_of(lift, jumps):
    high, low = halves(jnp.concatenate([jnp.concatenate(j, axis=0) for j in jumps], axis=1))
    return columns(dot(lift, high) + dot(lift, low))


def own_jumps(near_ref, own):
    jumps = [[] for _ in own]
    for face in range(FACES):
        p = partner_face[face]
        near = jnp.broadcast_to(near_ref[face], (SHEET, 128))
        home = near // 128 == lax.axis_index("mesh")
        slot = near % 128
        for k in range(len(own)):
            here = take(own[k][SHEET * p : SHEET * (p + 1)], slot)
            jumps[k].append(jnp.where(home, here, 0.0) - own[k][SHEET * face : SHEET * (face + 1)])
    return jumps


def rim_jumps(near_ref, rims, n):
    mine, parts = lax.axis_index("mesh"), lax.axis_size("mesh")
    follower = jnp.where(mine + 1 == parts, 0, mine + 1)
    jumps = [[] for _ in range(n)]
    for face in range(FACES):
        p = partner_face[face]
        near = jnp.broadcast_to(near_ref[face], (SHEET, 128))
        target = near // 128
        away = target != mine
        index = near % RIM + jnp.where(target == follower, 64, 0)
        for k in range(n):
            across = take(rims[k // 2][SHEET * p : SHEET * (p + 1)], index + RIM * (k % 2))
            jumps[k].append(jnp.where(away, across, 0.0))
    return jumps


def merge(before, after):
    lane = iota(before.shape, 1)
    first = jnp.where(lane < 64, before, pltpu.roll(after, 64, 1))
    second = jnp.where(lane < 64, pltpu.roll(before, 64, 1), after)
    return first, second


def own_kernel(
    count_ref, field_ref, smooth_ref, near_in, stiff_in, material_in, project_in, destination_in,
    partial_ref, kernel_ref, turned_ref, stiff_out_ref, pick_ref, lift_ref, project_out_ref, wanted_ref, near_ref,
    material_ref, stiff_ref, project_ref, destination_ref, sems,
):
    copies = copies_of(
        (near_in, stiff_in, material_in, project_in, destination_in),
        (near_ref, stiff_ref, material_ref, project_ref, destination_ref),
        sems,
    )
    live = live_mask(count_ref)
    fields = [field_ref[k] for k in range(6)]
    pick, lift = picker(), lifter()
    pick_ref[...] = pick
    lift_ref[...] = lift
    x = stacked(fields)
    faces = faces_of(pick, x)
    copies[0].wait()
    lifted = lift_of(lift, own_jumps(near_ref, faces))
    for copy in copies[1:]:
        copy.wait()
    material = jnp.broadcast_to(material_ref[...], (128, 128))
    high, low = split_stiffness(stiff_ref)
    stiff_out_ref[0] = high
    stiff_out_ref[1] = low
    strain = strains(high, low, x)
    for k in range(6):
        force = 0.5 * lifted[k] - material * strain[k]
        partial_ref[k] = live * (fields[k] + 0.4 * force)
    kernel_ref[...] = sum(fields[c] * strain[3 + c] for c in range(3))
    high, low = halves(jnp.concatenate([project_ref[...], jnp.zeros((64, 128 - NODES), F32)], axis=1))
    project_out_ref[0] = high
    project_out_ref[1] = low
    wanted_ref[...] = jnp.broadcast_to(destination_ref[...].astype(F32), (8, 128))
    width = smooth_ref.shape[1]
    wide = jnp.concatenate([smooth_ref[...], jnp.zeros((4, 128 - width), F32)], axis=1)
    turned_ref[...] = jnp.concatenate([wide, jnp.zeros((124, 128), F32)], axis=0).T[:8]


def step_kernel(
    scale, n_mesh,
    count_ref, partial_ref, kernel_ref, before_ref, after_ref, near_ref, stiff_ref, pick_ref, lift_ref,
    project_ref, wanted_ref,
    forward_ref, strain_ref, rim_ref, edge_ref, chunk_ref,
):
    live = live_mask(count_ref)
    first, second = merge(before_ref[:128], after_ref[:128])
    upper, lower = merge(before_ref[128:192], after_ref[128:192])
    rims = faces_of(pick_ref[...], stacked([first, second, jnp.concatenate([upper, lower], axis=0)]))
    lift = lift_of(lift_ref[...], rim_jumps(near_ref, rims, 6))
    fields = [partial_ref[k] + live * (0.2 * lift[k]) for k in range(6)]
    strain = strains(stiff_ref[0], stiff_ref[1], stacked(fields))
    kernel = kernel_ref[...] + sum(fields[c] * strain[3 + c] for c in range(3))
    k_high, k_low = halves(kernel)
    p_high, p_low = project_ref[0], project_ref[1]
    blocks = dot(jnp.concatenate([p_high, p_high], axis=1), jnp.concatenate([k_high, k_low], axis=0))
    blocks = (blocks + dot(p_low, k_high)) * scale
    for m in range(n_mesh):
        chunk_ref[m, :64] = blocks
        chunk_ref[m, 64:] = wanted_ref[...]
    rim_ref[...] = pack_rim(fields[:3])
    edge_ref[...] = jnp.where(iota((8, 128), 1) < 4, before_ref[192:], after_ref[192:])
    for c in range(3):
        forward_ref[c] = fields[c]
        strain_ref[c] = strain[c]


def dense_kernel(n_event, n_mesh, tile_width, first, parts_ref, edge_ref, before_ref, after_ref, out_ref):
    rows = 8 * n_event
    row = iota((rows, 128), 0)
    tile = (row % n_event + first) % n_event * (n_mesh * tile_width) + row // n_event - 2
    tile = tile.astype(F32) + (lax.axis_index("mesh") * tile_width).astype(F32)
    left, right = [], []
    for m in range(n_mesh):
        left.append(jnp.concatenate(halves(parts_ref[m, :64]), axis=0))
        wanted = jnp.broadcast_to(parts_ref[m, 64:65], (rows, 128))
        right.append(jnp.where(wanted == tile, 1.0, 0.0).astype(BF16))
    left, right = jnp.concatenate(left, axis=1), jnp.concatenate(right, axis=1)
    both = lax.dot_general(left, right, (((1,), (1,)), ((), ())), preferred_element_type=F32)
    both = both[:64] + both[64:]
    half = 4 * n_event
    both = jnp.concatenate([both[:, :half], both[:, half:]], axis=0).T
    for j in range(4):
        out_ref[pl.ds(j, n_event, stride=5)] = both[n_event * j : n_event * (j + 1)]
    lane, event = iota((n_event, 128), 1), (iota((n_event, 128), 0) + first) % n_event
    apart = event - lax.axis_index("event")
    used = ((apart == 1) & (lane < 4)) | ((apart == -1) & (lane >= 4) & (lane < 8))
    edges = jnp.where(used, jnp.broadcast_to(edge_ref[0:1], (n_event, 128)), 0.0)
    out_ref[pl.ds(4, n_event, stride=5)] = edges


def last_kernel(
    count_ref, field_ref, one_ref, strain_ref, before_ref, after_ref, near_ref, material_ref, pick_ref, lift_ref,
    turned_ref, edge_ref,
    final_ref, table_ref, open_ref,
):
    live = live_mask(count_ref)
    material = jnp.broadcast_to(material_ref[...], (128, 128))
    fields = [one_ref[c] for c in range(3)]
    jumps = own_jumps(near_ref, faces_of(pick_ref[...], stacked(fields)))
    rims = faces_of(pick_ref[...], stacked(list(merge(before_ref[...], after_ref[...]))))
    more = rim_jumps(near_ref, rims, 3)
    lift = lift_of(lift_ref[...], [[a + b for a, b in zip(*pair)] for pair in zip(jumps, more)])
    final = rows_of(final_ref)
    for c in range(3):
        force = 0.5 * lift[c] - material * strain_ref[c]
        out = live * (2.0 * fields[c] - field_ref[c] + 0.4 * force)
        final[NODES * c : NODES * (c + 1)] = out[:NODES]
    mine, parts = lax.axis_index("mesh"), lax.axis_size("mesh")
    tile = iota((8, 128), 0)
    is_open = ((tile == 1) & (mine == 0)) | ((tile == 6) & (mine == parts - 1))
    edge = jnp.where(tile == 6, pltpu.roll(edge_ref[...], 124, 1), edge_ref[...])
    edge = jnp.where(((tile == 1) | (tile == 6)) & ~is_open, edge, 0.0)
    table_ref[...] = jnp.where((tile >= 2) & (tile < 6), pltpu.roll(turned_ref[...], 2, 0), edge)
    open_ref[...] = is_open.astype(F32)


def total_of(parts):
    while len(parts) > 1:
        parts = [sum(parts[i : i + 2][1:], parts[i]) for i in range(0, len(parts), 2)]
    return parts[0]


def smooth_kernel(n_event, x_ref, table_ref, open_ref, o_ref):
    node, tile = iota((8, 128), 1), iota((8, 128), 0)
    span = 40 if n_event % 8 == 0 else 5 * n_event
    total = total_of([x_ref[i : i + span] for i in range(0, 5 * n_event, span)])
    total = total_of([total[i : i + 5] for i in range(0, span, 5)])
    edge = jnp.broadcast_to(total[4:5], (8, 128))
    edge = jnp.where(tile == 6, pltpu.roll(edge, 124, 1), edge)
    table = table_ref[...] + open_ref[...] * edge
    coef = [jnp.broadcast_to(table[:, d : d + 1], (8, 128)) for d in range(4)]
    total = total[:4]
    x = jnp.concatenate([total, pltpu.roll(total, 64, 1)], axis=0)
    for _ in range(2):
        right = jnp.where(tile < 7, pltpu.roll(x, 7, 0), 0.0)
        left = jnp.where(tile > 0, pltpu.roll(x, 1, 0), 0.0)
        out = x + coef[0] * (left + right - 2.0 * x)
        for d, shift in ((1, 4), (2, 2), (3, 0)):
            place, stride = (node >> shift) & 3, 1 << shift
            up = jnp.where(place < 3, pltpu.roll(x, 128 - stride, 1), 0.0)
            down = jnp.where(place > 0, pltpu.roll(x, stride, 1), 0.0)
            out = out + coef[d] * (up + down - 2.0 * x)
        x = out
    o_ref[...] = x[2:6, :64]


def call(kernel, out_shape, n_smem, n_vmem, n_hbm=0, scratch=()):
    many = isinstance(out_shape, tuple)
    return pl.pallas_call(
        kernel,
        out_shape=out_shape,
        in_specs=[SMEM] * n_smem + [VMEM] * n_vmem + [HBM] * n_hbm,
        out_specs=(VMEM,) * len(out_shape) if many else VMEM,
        scratch_shapes=scratch,
        compiler_params=PARAMS,
    )


def per_device(
    forward_start, adjoint_start, stiffness, projection, material, neighbours, destinations, counts, smoothing
):
    elements = forward_start.shape[-1]
    tile_width = smoothing.shape[1]
    n_mesh, n_event = lax.axis_size("mesh"), lax.axis_size("event")
    scale = math.sqrt(tile_width / elements) / STEPS
    forward, adjoint = (x.reshape(3, NODES, 1, 128) for x in (forward_start, adjoint_start))
    up = [(i, (i + 1) % n_mesh) for i in range(n_mesh)]
    down = [(j, i) for i, j in up]
    first_mesh, first_event = 5 * n_mesh // 8, n_event // 2
    mesh_group = [(i + first_mesh) % n_mesh for i in range(n_mesh)]
    event_group = [(i + first_event) % n_event for i in range(n_event)]

    near, project = neighbours.reshape(FACES, 1, 128), projection.T
    inputs = (forward, adjoint, smoothing, near, stiffness, material, project, destinations)
    inputs = [pltpu.with_memory_space_constraint(x, pltpu.HBM) for x in inputs]
    rim, fields, smooth_in = call(
        pack_kernel,
        (shape(200, 128), shape(6, 128, 128), shape(4, tile_width)),
        1,
        0,
        3,
        [pltpu.VMEM(x.shape, F32) for x in (forward, adjoint)] + [pltpu.SemaphoreType.DMA((3,))],
    )(counts, *inputs[:3])
    before, after = lax.ppermute(rim, "mesh", up), lax.ppermute(rim, "mesh", down)
    partial, kernel, turned, stiff, pick, lift, project, wanted, near, material = call(
        own_kernel,
        (
            shape(6, 128, 128),
            shape(128, 128),
            shape(8, 128),
            shape(2, 128, 128, dtype=BF16),
            shape(FACES * SHEET, 128, dtype=BF16),
            shape(128, FACES * SHEET, dtype=BF16),
            shape(2, 64, 128, dtype=BF16),
            shape(8, 128),
            shape(FACES, 1, 128, dtype=I32),
            shape(1, 128),
        ),
        1,
        2,
        5,
        [pltpu.VMEM(x.shape, x.dtype) for x in (stiffness, project, destinations)] + [pltpu.SemaphoreType.DMA((5,))],
    )(counts, fields, smooth_in, *inputs[3:])

    def one_step(*refs):
        step_kernel(scale, n_mesh, *refs)

    one, strain, rim_one, edge, chunk = call(
        one_step,
        (shape(3, 128, 128), shape(3, 128, 128), shape(128, 128), shape(8, 128), shape(n_mesh, 72, 128)),
        1,
        10,
    )(counts, partial, kernel, before, after, near, stiff, pick, lift, project, wanted)
    parts = lax.all_to_all(chunk, "mesh", 0, 0, tiled=True, axis_index_groups=[mesh_group])

    before, after = lax.ppermute(rim_one, "mesh", up), lax.ppermute(rim_one, "mesh", down)

    def dense(*refs):
        dense_kernel(n_event, n_mesh, tile_width, first_event, *refs)

    partial = call(dense, shape(5 * n_event, 128), 0, 4)(parts, edge, before, after)
    pieces = lax.all_to_all(partial.reshape(-1, 1, 128), "event", 0, 0, tiled=True, axis_index_groups=[event_group])
    final, table, is_open = call(last_kernel, (shape(3, NODES, 1, 128), shape(8, 128), shape(8, 128)), 1, 11)(
        counts, fields, one, strain, before, after, near, material, pick, lift, turned, edge
    )

    def smooth(*refs):
        smooth_kernel(n_event, *refs)

    tiles = call(smooth, shape(tile_width, 64), 0, 3)(pieces.reshape(-1, 128), table, is_open)
    return final.reshape(1, 3, NODES, 128), tiles.T


def solution(mesh):
    in_specs = (
        P("event", None, None, "mesh"),
        P("event", None, None, "mesh"),
        P(),
        P(),
        P("event", "mesh"),
        P("event", None, "mesh"),
        P("event", "mesh"),
        P("event", "mesh"),
        P(None, ("event", "mesh")),
    )
    out_specs = (P("event", None, None, "mesh"), P(None, ("event", "mesh")))
    return jax.shard_map(per_device, mesh=mesh, in_specs=in_specs, out_specs=out_specs, check_vma=False)
```

```python
import math

import jax
import jax.numpy as jnp
from jax import lax
from jax.experimental import pallas as pl
from jax.experimental.pallas import tpu as pltpu
from jax.sharding import PartitionSpec as P

STEPS = 2
NODES = 125
RIM = 32
SHEET = 32
FACES = 6
F32, BF16, I32 = jnp.float32, jnp.bfloat16, jnp.int32
partner_face = (1, 0, 3, 2, 5, 4)

VMEM = pl.BlockSpec(memory_space=pltpu.VMEM)
SMEM = pl.BlockSpec(memory_space=pltpu.SMEM)
HBM = pl.BlockSpec(memory_space=pltpu.HBM)
PARAMS = pltpu.CompilerParams(vmem_limit_bytes=40 * 2**20)


def shape(*dims, dtype=F32):
    return jax.ShapeDtypeStruct(dims, dtype)


def iota(dims, axis):
    return lax.broadcasted_iota(I32, dims, axis)


def halves(x):
    high = x.astype(BF16)
    return high, (x - high.astype(F32)).astype(BF16)


def dot(a, b):
    return lax.dot_general(a, b, (((1,), (0,)), ((), ())), preferred_element_type=F32)


def face_nodes(dims, axis):
    row = iota(dims, axis)
    face, q = row // SHEET, row % SHEET
    a = sum((q >= 5 * i).astype(I32) for i in range(1, 5))
    b = q - 5 * a
    node = jnp.where(face == 0, q, q + 100)
    node = jnp.where(face == 2, 25 * a + b, node)
    node = jnp.where(face == 3, 25 * a + 20 + b, node)
    node = jnp.where(face == 4, 5 * q, node)
    node = jnp.where(face == 5, 5 * q + 4, node)
    return jnp.where(q < 25, node, -1)


def picker():
    dims = (FACES * SHEET, 128)
    return jnp.where(face_nodes(dims, 0) == iota(dims, 1), 1.0, 0.0).astype(BF16)


def lifter():
    dims = (128, FACES * SHEET)
    return jnp.where(face_nodes(dims, 1) == iota(dims, 0), 1.0, 0.0).astype(BF16)


def rows_of(ref):
    return ref.reshape(3 * NODES, 128)


def padded(ref, c):
    rows = rows_of(ref)[NODES * c : NODES * (c + 1)]
    return jnp.concatenate([rows, jnp.zeros((128 - NODES, 128), F32)], axis=0)


def stacked(fields):
    high, low = halves(jnp.concatenate(fields, axis=1))
    return jnp.concatenate([high, low], axis=0)


def pack_rim(fields):
    lane = iota((128, 128), 1)
    out = fields[0]
    for k in range(1, len(fields)):
        out = jnp.where(lane < RIM * k, out, pltpu.roll(fields[k], RIM * k, 1))
    return jnp.where(lane < RIM * len(fields), out, 0.0)


def fold(x):
    return jnp.where(iota((64, 128), 1) < 64, x[:64], pltpu.roll(x[64:], 64, 1))


def live_mask(count_ref):
    return (iota((128, 128), 1) < count_ref[0, 0]).astype(F32)


def edge_row(smooth_ref):
    width = smooth_ref.shape[1]
    last = jnp.broadcast_to(smooth_ref[:, width - 1 : width], (4, 128))
    first = jnp.broadcast_to(smooth_ref[:, 0:1], (4, 128))
    lane, row = iota((4, 128), 1), iota((4, 128), 0)
    spread = jnp.where(lane == row, last, 0.0) + jnp.where(lane == row + 4, first, 0.0)
    return jnp.sum(spread, axis=0, keepdims=True)


def copies_of(sources, targets, sems):
    copies = [pltpu.make_async_copy(a, b, sems.at[i]) for i, (a, b) in enumerate(zip(sources, targets))]
    for copy in copies:
        copy.start()
    return copies


def pack_kernel(count_ref, forward_ref, adjoint_ref, smooth_ref, rim_ref, field_ref, smooth_out_ref, *held):
    copies = copies_of((forward_ref, adjoint_ref, smooth_ref), (*held[:2], smooth_out_ref), held[2])
    live = live_mask(count_ref)
    fields = []
    for ref, copy in zip(held[:2], copies):
        copy.wait()
        fields += [padded(ref, c) * live for c in range(3)]
    rim_ref[:128] = pack_rim(fields[:4])
    rim_ref[128:192] = fold(pack_rim(fields[4:]))
    for k in range(6):
        field_ref[k] = fields[k]
    copies[2].wait()
    rim_ref[192:] = jnp.broadcast_to(edge_row(smooth_out_ref), (8, 128))


def split_stiffness(stiff_ref):
    wide = jnp.concatenate([stiff_ref[...], jnp.zeros((NODES, 128 - NODES), F32)], axis=1)
    return halves(jnp.concatenate([wide, jnp.zeros((128 - NODES, 128), F32)], axis=0))


def columns(x):
    return [x[:, 128 * k : 128 * (k + 1)] for k in range(x.shape[1] // 128)]


def strains(high, low, x):
    return columns(dot(jnp.concatenate([high, high], axis=1), x) + dot(low, x[:128]))


def faces_of(pick, x):
    return columns(dot(jnp.concatenate([pick, pick], axis=1), x))


def take(x, index):
    return jnp.take_along_axis(x, index, axis=1, mode="promise_in_bounds")


def lift_of(lift, jumps):
    high, low = halves(jnp.concatenate([jnp.concatenate(j, axis=0) for j in jumps], axis=1))
    return columns(dot(lift, high) + dot(lift, low))


def own_jumps(near_ref, own):
    jumps = [[] for _ in own]
    for face in range(FACES):
        p = partner_face[face]
        near = jnp.broadcast_to(near_ref[face], (SHEET, 128))
        home = near // 128 == lax.axis_index("mesh")
        slot = near % 128
        for k in range(len(own)):
            here = take(own[k][SHEET * p : SHEET * (p + 1)], slot)
            jumps[k].append(jnp.where(home, here, 0.0) - own[k][SHEET * face : SHEET * (face + 1)])
    return jumps


def rim_jumps(near_ref, rims, n):
    mine, parts = lax.axis_index("mesh"), lax.axis_size("mesh")
    follower = jnp.where(mine + 1 == parts, 0, mine + 1)
    jumps = [[] for _ in range(n)]
    for face in range(FACES):
        p = partner_face[face]
        near = jnp.broadcast_to(near_ref[face], (SHEET, 128))
        target = near // 128
        away = target != mine
        index = near % RIM + jnp.where(target == follower, 64, 0)
        for k in range(n):
            across = take(rims[k // 2][SHEET * p : SHEET * (p + 1)], index + RIM * (k % 2))
            jumps[k].append(jnp.where(away, across, 0.0))
    return jumps


def merge(before, after):
    lane = iota(before.shape, 1)
    first = jnp.where(lane < 64, before, pltpu.roll(after, 64, 1))
    second = jnp.where(lane < 64, pltpu.roll(before, 64, 1), after)
    return first, second


def own_kernel(
    count_ref, field_ref, smooth_ref, near_in, stiff_in, material_in, project_in, destination_in,
    partial_ref, kernel_ref, turned_ref, stiff_out_ref, pick_ref, lift_ref, project_out_ref, wanted_ref, near_ref,
    material_ref, stiff_ref, project_ref, destination_ref, sems,
):
    copies = copies_of(
        (near_in, stiff_in, material_in, project_in, destination_in),
        (near_ref, stiff_ref, material_ref, project_ref, destination_ref),
        sems,
    )
    live = live_mask(count_ref)
    fields = [field_ref[k] for k in range(6)]
    pick, lift = picker(), lifter()
    pick_ref[...] = pick
    lift_ref[...] = lift
    x = stacked(fields)
    faces = faces_of(pick, x)
    copies[0].wait()
    lifted = lift_of(lift, own_jumps(near_ref, faces))
    for copy in copies[1:]:
        copy.wait()
    material = jnp.broadcast_to(material_ref[...], (128, 128))
    high, low = split_stiffness(stiff_ref)
    stiff_out_ref[0] = high
    stiff_out_ref[1] = low
    strain = strains(high, low, x)
    for k in range(6):
        force = 0.5 * lifted[k] - material * strain[k]
        partial_ref[k] = live * (fields[k] + 0.4 * force)
    kernel_ref[...] = sum(fields[c] * strain[3 + c] for c in range(3))
    high, low = halves(jnp.concatenate([project_ref[...], jnp.zeros((64, 128 - NODES), F32)], axis=1))
    project_out_ref[0] = high
    project_out_ref[1] = low
    wanted_ref[...] = jnp.broadcast_to(destination_ref[...].astype(F32), (8, 128))
    width = smooth_ref.shape[1]
    wide = jnp.concatenate([smooth_ref[...], jnp.zeros((4, 128 - width), F32)], axis=1)
    turned_ref[...] = jnp.concatenate([wide, jnp.zeros((124, 128), F32)], axis=0).T[:8]


def step_kernel(
    scale, n_mesh,
    count_ref, partial_ref, kernel_ref, after_ref, before_ref, near_ref, stiff_ref, pick_ref, lift_ref,
    project_ref, wanted_ref,
    forward_ref, strain_ref, rim_ref, edge_ref, chunk_ref,
):
    live = live_mask(count_ref)
    first, second = merge(before_ref[:128], after_ref[:128])
    upper, lower = merge(before_ref[128:192], after_ref[128:192])
    rims = faces_of(pick_ref[...], stacked([first, second, jnp.concatenate([upper, lower], axis=0)]))
    lift = lift_of(lift_ref[...], rim_jumps(near_ref, rims, 6))
    fields = [partial_ref[k] + live * (0.2 * lift[k]) for k in range(6)]
    strain = strains(stiff_ref[0], stiff_ref[1], stacked(fields))
    kernel = kernel_ref[...] + sum(fields[c] * strain[3 + c] for c in range(3))
    k_high, k_low = halves(kernel)
    p_high, p_low = project_ref[0], project_ref[1]
    blocks = dot(jnp.concatenate([p_high, p_high], axis=1), jnp.concatenate([k_high, k_low], axis=0))
    blocks = (blocks + dot(p_low, k_high)) * scale
    for m in range(n_mesh):
        chunk_ref[m, :64] = blocks
        chunk_ref[m, 64:] = wanted_ref[...]
    rim_ref[...] = pack_rim(fields[:3])
    edge_ref[...] = jnp.where(iota((8, 128), 1) < 4, before_ref[192:], after_ref[192:])
    for c in range(3):
        forward_ref[c] = fields[c]
        strain_ref[c] = strain[c]


def dense_kernel(n_event, n_mesh, tile_width, first, parts_ref, edge_ref, after_ref, before_ref, out_ref):
    rows = 8 * n_event
    row = iota((rows, 128), 0)
    tile = (row % n_event + first) % n_event * (n_mesh * tile_width) + row // n_event - 2
    tile = tile.astype(F32) + (lax.axis_index("mesh") * tile_width).astype(F32)
    left, right = [], []
    for m in range(n_mesh):
        left.append(jnp.concatenate(halves(parts_ref[m, :64]), axis=0))
        wanted = jnp.broadcast_to(parts_ref[m, 64:65], (rows, 128))
        right.append(jnp.where(wanted == tile, 1.0, 0.0).astype(BF16))
    left, right = jnp.concatenate(left, axis=1), jnp.concatenate(right, axis=1)
    both = lax.dot_general(left, right, (((1,), (1,)), ((), ())), preferred_element_type=F32)
    both = both[:64] + both[64:]
    half = 4 * n_event
    both = jnp.concatenate([both[:, :half], both[:, half:]], axis=0).T
    for j in range(4):
        out_ref[pl.ds(j, n_event, stride=5)] = both[n_event * j : n_event * (j + 1)]
    lane, event = iota((n_event, 128), 1), (iota((n_event, 128), 0) + first) % n_event
    apart = event - lax.axis_index("event")
    used = ((apart == 1) & (lane < 4)) | ((apart == -1) & (lane >= 4) & (lane < 8))
    edges = jnp.where(used, jnp.broadcast_to(edge_ref[0:1], (n_event, 128)), 0.0)
    out_ref[pl.ds(4, n_event, stride=5)] = edges


def last_kernel(
    count_ref, field_ref, one_ref, strain_ref, before_ref, after_ref, near_ref, material_ref, pick_ref, lift_ref,
    turned_ref, edge_ref,
    final_ref, table_ref, open_ref,
):
    live = live_mask(count_ref)
    material = jnp.broadcast_to(material_ref[...], (128, 128))
    fields = [one_ref[c] for c in range(3)]
    jumps = own_jumps(near_ref, faces_of(pick_ref[...], stacked(fields)))
    rims = faces_of(pick_ref[...], stacked(list(merge(before_ref[...], after_ref[...]))))
    more = rim_jumps(near_ref, rims, 3)
    lift = lift_of(lift_ref[...], [[a + b for a, b in zip(*pair)] for pair in zip(jumps, more)])
    final = rows_of(final_ref)
    for c in range(3):
        force = 0.5 * lift[c] - material * strain_ref[c]
        out = live * (2.0 * fields[c] - field_ref[c] + 0.4 * force)
        final[NODES * c : NODES * (c + 1)] = out[:NODES]
    mine, parts = lax.axis_index("mesh"), lax.axis_size("mesh")
    tile = iota((8, 128), 0)
    is_open = ((tile == 1) & (mine == 0)) | ((tile == 6) & (mine == parts - 1))
    edge = jnp.where(tile == 6, pltpu.roll(edge_ref[...], 124, 1), edge_ref[...])
    edge = jnp.where(((tile == 1) | (tile == 6)) & ~is_open, edge, 0.0)
    table_ref[...] = jnp.where((tile >= 2) & (tile < 6), pltpu.roll(turned_ref[...], 2, 0), edge)
    open_ref[...] = is_open.astype(F32)


def total_of(parts):
    while len(parts) > 1:
        parts = [sum(parts[i : i + 2][1:], parts[i]) for i in range(0, len(parts), 2)]
    return parts[0]


def smooth_kernel(n_event, x_ref, table_ref, open_ref, o_ref):
    node, tile = iota((8, 128), 1), iota((8, 128), 0)
    span = 40 if n_event % 8 == 0 else 5 * n_event
    total = total_of([x_ref[i : i + span] for i in range(0, 5 * n_event, span)])
    total = total_of([total[i : i + 5] for i in range(0, span, 5)])
    edge = jnp.broadcast_to(total[4:5], (8, 128))
    edge = jnp.where(tile == 6, pltpu.roll(edge, 124, 1), edge)
    table = table_ref[...] + open_ref[...] * edge
    coef = [jnp.broadcast_to(table[:, d : d + 1], (8, 128)) for d in range(4)]
    total = total[:4]
    x = jnp.concatenate([total, pltpu.roll(total, 64, 1)], axis=0)
    for _ in range(2):
        right = jnp.where(tile < 7, pltpu.roll(x, 7, 0), 0.0)
        left = jnp.where(tile > 0, pltpu.roll(x, 1, 0), 0.0)
        out = x + coef[0] * (left + right - 2.0 * x)
        for d, shift in ((1, 4), (2, 2), (3, 0)):
            place, stride = (node >> shift) & 3, 1 << shift
            up = jnp.where(place < 3, pltpu.roll(x, 128 - stride, 1), 0.0)
            down = jnp.where(place > 0, pltpu.roll(x, stride, 1), 0.0)
            out = out + coef[d] * (up + down - 2.0 * x)
        x = out
    o_ref[...] = x[2:6, :64]


def call(kernel, out_shape, n_smem, n_vmem, n_hbm=0, scratch=()):
    many = isinstance(out_shape, tuple)
    return pl.pallas_call(
        kernel,
        out_shape=out_shape,
        in_specs=[SMEM] * n_smem + [VMEM] * n_vmem + [HBM] * n_hbm,
        out_specs=(VMEM,) * len(out_shape) if many else VMEM,
        scratch_shapes=scratch,
        compiler_params=PARAMS,
    )


def per_device(
    forward_start, adjoint_start, stiffness, projection, material, neighbours, destinations, counts, smoothing
):
    elements = forward_start.shape[-1]
    tile_width = smoothing.shape[1]
    n_mesh, n_event = lax.axis_size("mesh"), lax.axis_size("event")
    scale = math.sqrt(tile_width / elements) / STEPS
    forward, adjoint = (x.reshape(3, NODES, 1, 128) for x in (forward_start, adjoint_start))
    up = [(i, (i + 1) % n_mesh) for i in range(n_mesh)]
    down = [(j, i) for i, j in up]
    first_mesh, first_event = 5 * n_mesh // 8, n_event // 2
    mesh_group = [(i + first_mesh) % n_mesh for i in range(n_mesh)]
    event_group = [(i + first_event) % n_event for i in range(n_event)]

    near, project = neighbours.reshape(FACES, 1, 128), projection.T
    inputs = (forward, adjoint, smoothing, near, stiffness, material, project, destinations)
    inputs = [pltpu.with_memory_space_constraint(x, pltpu.HBM) for x in inputs]
    rim, fields, smooth_in = call(
        pack_kernel,
        (shape(200, 128), shape(6, 128, 128), shape(4, tile_width)),
        1,
        0,
        3,
        [pltpu.VMEM(x.shape, F32) for x in (forward, adjoint)] + [pltpu.SemaphoreType.DMA((3,))],
    )(counts, *inputs[:3])
    after, before = lax.ppermute(rim, "mesh", down), lax.ppermute(rim, "mesh", up)
    partial, kernel, turned, stiff, pick, lift, project, wanted, near, material = call(
        own_kernel,
        (
            shape(6, 128, 128),
            shape(128, 128),
            shape(8, 128),
            shape(2, 128, 128, dtype=BF16),
            shape(FACES * SHEET, 128, dtype=BF16),
            shape(128, FACES * SHEET, dtype=BF16),
            shape(2, 64, 128, dtype=BF16),
            shape(8, 128),
            shape(FACES, 1, 128, dtype=I32),
            shape(1, 128),
        ),
        1,
        2,
        5,
        [pltpu.VMEM(x.shape, x.dtype) for x in (stiffness, project, destinations)] + [pltpu.SemaphoreType.DMA((5,))],
    )(counts, fields, smooth_in, *inputs[3:])

    def one_step(*refs):
        step_kernel(scale, n_mesh, *refs)

    one, strain, rim_one, edge, chunk = call(
        one_step,
        (shape(3, 128, 128), shape(3, 128, 128), shape(128, 128), shape(8, 128), shape(n_mesh, 72, 128)),
        1,
        10,
    )(counts, partial, kernel, after, before, near, stiff, pick, lift, project, wanted)
    parts = lax.all_to_all(chunk, "mesh", 0, 0, tiled=True, axis_index_groups=[mesh_group])

    after, before = lax.ppermute(rim_one, "mesh", down), lax.ppermute(rim_one, "mesh", up)

    def dense(*refs):
        dense_kernel(n_event, n_mesh, tile_width, first_event, *refs)

    partial = call(dense, shape(5 * n_event, 128), 0, 4)(parts, edge, after, before)
    pieces = lax.all_to_all(partial.reshape(-1, 1, 128), "event", 0, 0, tiled=True, axis_index_groups=[event_group])
    final, table, is_open = call(last_kernel, (shape(3, NODES, 1, 128), shape(8, 128), shape(8, 128)), 1, 11)(
        counts, fields, one, strain, before, after, near, material, pick, lift, turned, edge
    )

    def smooth(*refs):
        smooth_kernel(n_event, *refs)

    tiles = call(smooth, shape(tile_width, 64), 0, 3)(pieces.reshape(-1, 128), table, is_open)
    return final.reshape(1, 3, NODES, 128), tiles.T


def solution(mesh):
    in_specs = (
        P("event", None, None, "mesh"),
        P("event", None, None, "mesh"),
        P(),
        P(),
        P("event", "mesh"),
        P("event", None, "mesh"),
        P("event", "mesh"),
        P("event", "mesh"),
        P(None, ("event", "mesh")),
    )
    out_specs = (P("event", None, None, "mesh"), P(None, ("event", "mesh")))
    return jax.shard_map(per_device, mesh=mesh, in_specs=in_specs, out_specs=out_specs, check_vma=False)
```

```python
import math

import jax
import jax.numpy as jnp
from jax import lax
from jax.experimental import pallas as pl
from jax.experimental.pallas import tpu as pltpu
from jax.sharding import PartitionSpec as P

STEPS = 2
NODES = 125
RIM = 32
SHEET = 32
FACES = 6
F32, BF16, I32 = jnp.float32, jnp.bfloat16, jnp.int32
partner_face = (1, 0, 3, 2, 5, 4)

VMEM = pl.BlockSpec(memory_space=pltpu.VMEM)
SMEM = pl.BlockSpec(memory_space=pltpu.SMEM)
HBM = pl.BlockSpec(memory_space=pltpu.HBM)
PARAMS = pltpu.CompilerParams(vmem_limit_bytes=40 * 2**20)


def shape(*dims, dtype=F32):
    return jax.ShapeDtypeStruct(dims, dtype)


def iota(dims, axis):
    return lax.broadcasted_iota(I32, dims, axis)


def halves(x):
    high = x.astype(BF16)
    return high, (x - high.astype(F32)).astype(BF16)


def dot(a, b):
    return lax.dot_general(a, b, (((1,), (0,)), ((), ())), preferred_element_type=F32)


def face_nodes(dims, axis):
    row = iota(dims, axis)
    face, q = row // SHEET, row % SHEET
    a = sum((q >= 5 * i).astype(I32) for i in range(1, 5))
    b = q - 5 * a
    node = jnp.where(face == 0, q, q + 100)
    node = jnp.where(face == 2, 25 * a + b, node)
    node = jnp.where(face == 3, 25 * a + 20 + b, node)
    node = jnp.where(face == 4, 5 * q, node)
    node = jnp.where(face == 5, 5 * q + 4, node)
    return jnp.where(q < 25, node, -1)


def picker():
    dims = (FACES * SHEET, 128)
    return jnp.where(face_nodes(dims, 0) == iota(dims, 1), 1.0, 0.0).astype(BF16)


def lifter():
    dims = (128, FACES * SHEET)
    return jnp.where(face_nodes(dims, 1) == iota(dims, 0), 1.0, 0.0).astype(BF16)


def rows_of(ref):
    return ref.reshape(3 * NODES, 128)


def padded(ref, c):
    rows = rows_of(ref)[NODES * c : NODES * (c + 1)]
    return jnp.concatenate([rows, jnp.zeros((128 - NODES, 128), F32)], axis=0)


def stacked(fields):
    high, low = halves(jnp.concatenate(fields, axis=1))
    return jnp.concatenate([high, low], axis=0)


def pack_rim(fields):
    lane = iota((128, 128), 1)
    out = fields[0]
    for k in range(1, len(fields)):
        out = jnp.where(lane < RIM * k, out, pltpu.roll(fields[k], RIM * k, 1))
    return jnp.where(lane < RIM * len(fields), out, 0.0)


def fold(x):
    return jnp.where(iota((64, 128), 1) < 64, x[:64], pltpu.roll(x[64:], 64, 1))


def live_mask(count_ref):
    return (iota((128, 128), 1) < count_ref[0, 0]).astype(F32)


def edge_row(smooth_ref):
    width = smooth_ref.shape[1]
    last = jnp.broadcast_to(smooth_ref[:, width - 1 : width], (4, 128))
    first = jnp.broadcast_to(smooth_ref[:, 0:1], (4, 128))
    lane, row = iota((4, 128), 1), iota((4, 128), 0)
    spread = jnp.where(lane == row, last, 0.0) + jnp.where(lane == row + 4, first, 0.0)
    return jnp.sum(spread, axis=0, keepdims=True)


def copies_of(sources, targets, sems):
    copies = [pltpu.make_async_copy(a, b, sems.at[i]) for i, (a, b) in enumerate(zip(sources, targets))]
    for copy in copies:
        copy.start()
    return copies


def pack_kernel(count_ref, forward_ref, adjoint_ref, smooth_ref, rim_ref, field_ref, smooth_out_ref, *held):
    copies = copies_of((forward_ref, adjoint_ref, smooth_ref), (*held[:2], smooth_out_ref), held[2])
    live = live_mask(count_ref)
    fields = []
    for ref, copy in zip(held[:2], copies):
        copy.wait()
        fields += [padded(ref, c) * live for c in range(3)]
    rim_ref[:128] = pack_rim(fields[:4])
    rim_ref[128:192] = fold(pack_rim(fields[4:]))
    for k in range(6):
        field_ref[k] = fields[k]
    copies[2].wait()
    rim_ref[192:] = jnp.broadcast_to(edge_row(smooth_out_ref), (8, 128))


def split_stiffness(stiff_ref):
    wide = jnp.concatenate([stiff_ref[...], jnp.zeros((NODES, 128 - NODES), F32)], axis=1)
    return halves(jnp.concatenate([wide, jnp.zeros((128 - NODES, 128), F32)], axis=0))


def columns(x):
    return [x[:, 128 * k : 128 * (k + 1)] for k in range(x.shape[1] // 128)]


def strains(high, low, x):
    return columns(dot(jnp.concatenate([high, high], axis=1), x) + dot(low, x[:128]))


def faces_of(pick, x):
    return columns(dot(jnp.concatenate([pick, pick], axis=1), x))


def take(x, index):
    return jnp.take_along_axis(x, index, axis=1, mode="promise_in_bounds")


def lift_of(lift, jumps):
    high, low = halves(jnp.concatenate([jnp.concatenate(j, axis=0) for j in jumps], axis=1))
    return columns(dot(lift, high) + dot(lift, low))


def own_jumps(near_ref, own):
    jumps = [[] for _ in own]
    for face in range(FACES):
        p = partner_face[face]
        near = jnp.broadcast_to(near_ref[face], (SHEET, 128))
        home = near // 128 == lax.axis_index("mesh")
        slot = near % 128
        for k in range(len(own)):
            here = take(own[k][SHEET * p : SHEET * (p + 1)], slot)
            jumps[k].append(jnp.where(home, here, 0.0) - own[k][SHEET * face : SHEET * (face + 1)])
    return jumps


def rim_jumps(near_ref, rims, n):
    mine, parts = lax.axis_index("mesh"), lax.axis_size("mesh")
    follower = jnp.where(mine + 1 == parts, 0, mine + 1)
    jumps = [[] for _ in range(n)]
    for face in range(FACES):
        p = partner_face[face]
        near = jnp.broadcast_to(near_ref[face], (SHEET, 128))
        target = near // 128
        away = target != mine
        index = near % RIM + jnp.where(target == follower, 64, 0)
        for k in range(n):
            across = take(rims[k // 2][SHEET * p : SHEET * (p + 1)], index + RIM * (k % 2))
            jumps[k].append(jnp.where(away, across, 0.0))
    return jumps


def merge(before, after):
    lane = iota(before.shape, 1)
    first = jnp.where(lane < 64, before, pltpu.roll(after, 64, 1))
    second = jnp.where(lane < 64, pltpu.roll(before, 64, 1), after)
    return first, second


def own_kernel(
    count_ref, field_ref, smooth_ref, near_in, stiff_in, material_in, project_in, destination_in,
    partial_ref, kernel_ref, turned_ref, stiff_out_ref, pick_ref, lift_ref, project_out_ref, wanted_ref, near_ref,
    material_ref, stiff_ref, project_ref, destination_ref, sems,
):
    copies = copies_of(
        (near_in, stiff_in, material_in, project_in, destination_in),
        (near_ref, stiff_ref, material_ref, project_ref, destination_ref),
        sems,
    )
    live = live_mask(count_ref)
    fields = [field_ref[k] for k in range(6)]
    pick, lift = picker(), lifter()
    pick_ref[...] = pick
    lift_ref[...] = lift
    x = stacked(fields)
    faces = faces_of(pick, x)
    copies[0].wait()
    lifted = lift_of(lift, own_jumps(near_ref, faces))
    for copy in copies[1:]:
        copy.wait()
    material = jnp.broadcast_to(material_ref[...], (128, 128))
    high, low = split_stiffness(stiff_ref)
    stiff_out_ref[0] = high
    stiff_out_ref[1] = low
    strain = strains(high, low, x)
    for k in range(6):
        force = 0.5 * lifted[k] - material * strain[k]
        partial_ref[k] = live * (fields[k] + 0.4 * force)
    kernel_ref[...] = sum(fields[c] * strain[3 + c] for c in range(3))
    high, low = halves(jnp.concatenate([project_ref[...], jnp.zeros((64, 128 - NODES), F32)], axis=1))
    project_out_ref[0] = high
    project_out_ref[1] = low
    wanted_ref[...] = jnp.broadcast_to(destination_ref[...].astype(F32), (8, 128))
    width = smooth_ref.shape[1]
    wide = jnp.concatenate([smooth_ref[...], jnp.zeros((4, 128 - width), F32)], axis=1)
    turned_ref[...] = jnp.concatenate([wide, jnp.zeros((124, 128), F32)], axis=0).T[:8]


def step_kernel(
    scale, n_mesh,
    count_ref, partial_ref, kernel_ref, after_ref, before_ref, near_ref, stiff_ref, pick_ref, lift_ref,
    project_ref, wanted_ref,
    forward_ref, strain_ref, rim_ref, edge_ref, chunk_ref,
):
    live = live_mask(count_ref)
    first, second = merge(before_ref[:128], after_ref[:128])
    upper, lower = merge(before_ref[128:192], after_ref[128:192])
    rims = faces_of(pick_ref[...], stacked([first, second, jnp.concatenate([upper, lower], axis=0)]))
    lift = lift_of(lift_ref[...], rim_jumps(near_ref, rims, 6))
    fields = [partial_ref[k] + live * (0.2 * lift[k]) for k in range(6)]
    strain = strains(stiff_ref[0], stiff_ref[1], stacked(fields))
    kernel = kernel_ref[...] + sum(fields[c] * strain[3 + c] for c in range(3))
    k_high, k_low = halves(kernel)
    p_high, p_low = project_ref[0], project_ref[1]
    blocks = dot(jnp.concatenate([p_high, p_high], axis=1), jnp.concatenate([k_high, k_low], axis=0))
    blocks = (blocks + dot(p_low, k_high)) * scale
    for m in range(n_mesh):
        chunk_ref[m, :64] = blocks
        chunk_ref[m, 64:] = wanted_ref[...]
    rim_ref[...] = pack_rim(fields[:3])
    edge_ref[...] = jnp.where(iota((8, 128), 1) < 4, before_ref[192:], after_ref[192:])
    for c in range(3):
        forward_ref[c] = fields[c]
        strain_ref[c] = strain[c]


def dense_kernel(n_event, n_mesh, tile_width, first, parts_ref, edge_ref, after_ref, before_ref, out_ref):
    rows = 8 * n_event
    row = iota((rows, 128), 0)
    tile = (row % n_event + first) % n_event * (n_mesh * tile_width) + row // n_event - 2
    tile = tile.astype(F32) + (lax.axis_index("mesh") * tile_width).astype(F32)
    left, right = [], []
    for m in range(n_mesh):
        left.append(jnp.concatenate(halves(parts_ref[m, :64]), axis=0))
        wanted = jnp.broadcast_to(parts_ref[m, 64:65], (rows, 128))
        right.append(jnp.where(wanted == tile, 1.0, 0.0).astype(BF16))
    left, right = jnp.concatenate(left, axis=1), jnp.concatenate(right, axis=1)
    both = lax.dot_general(left, right, (((1,), (1,)), ((), ())), preferred_element_type=F32)
    both = both[:64] + both[64:]
    half = 4 * n_event
    both = jnp.concatenate([both[:, :half], both[:, half:]], axis=0).T
    for j in range(4):
        out_ref[pl.ds(j, n_event, stride=5)] = both[n_event * j : n_event * (j + 1)]
    lane, event = iota((n_event, 128), 1), (iota((n_event, 128), 0) + first) % n_event
    apart = event - lax.axis_index("event")
    used = ((apart == 1) & (lane < 4)) | ((apart == -1) & (lane >= 4) & (lane < 8))
    edges = jnp.where(used, jnp.broadcast_to(edge_ref[0:1], (n_event, 128)), 0.0)
    out_ref[pl.ds(4, n_event, stride=5)] = edges


def last_kernel(
    count_ref, field_ref, one_ref, strain_ref, after_ref, before_ref, near_ref, material_ref, pick_ref, lift_ref,
    turned_ref, edge_ref,
    final_ref, table_ref, open_ref,
):
    live = live_mask(count_ref)
    material = jnp.broadcast_to(material_ref[...], (128, 128))
    fields = [one_ref[c] for c in range(3)]
    jumps = own_jumps(near_ref, faces_of(pick_ref[...], stacked(fields)))
    rims = faces_of(pick_ref[...], stacked(list(merge(before_ref[...], after_ref[...]))))
    more = rim_jumps(near_ref, rims, 3)
    lift = lift_of(lift_ref[...], [[a + b for a, b in zip(*pair)] for pair in zip(jumps, more)])
    final = rows_of(final_ref)
    for c in range(3):
        force = 0.5 * lift[c] - material * strain_ref[c]
        out = live * (2.0 * fields[c] - field_ref[c] + 0.4 * force)
        final[NODES * c : NODES * (c + 1)] = out[:NODES]
    mine, parts = lax.axis_index("mesh"), lax.axis_size("mesh")
    tile = iota((8, 128), 0)
    is_open = ((tile == 1) & (mine == 0)) | ((tile == 6) & (mine == parts - 1))
    edge = jnp.where(tile == 6, pltpu.roll(edge_ref[...], 124, 1), edge_ref[...])
    edge = jnp.where(((tile == 1) | (tile == 6)) & ~is_open, edge, 0.0)
    table_ref[...] = jnp.where((tile >= 2) & (tile < 6), pltpu.roll(turned_ref[...], 2, 0), edge)
    open_ref[...] = is_open.astype(F32)


def total_of(parts):
    while len(parts) > 1:
        parts = [sum(parts[i : i + 2][1:], parts[i]) for i in range(0, len(parts), 2)]
    return parts[0]


def smooth_kernel(n_event, x_ref, table_ref, open_ref, o_ref):
    node, tile = iota((8, 128), 1), iota((8, 128), 0)
    span = 40 if n_event % 8 == 0 else 5 * n_event
    total = total_of([x_ref[i : i + span] for i in range(0, 5 * n_event, span)])
    total = total_of([total[i : i + 5] for i in range(0, span, 5)])
    edge = jnp.broadcast_to(total[4:5], (8, 128))
    edge = jnp.where(tile == 6, pltpu.roll(edge, 124, 1), edge)
    table = table_ref[...] + open_ref[...] * edge
    coef = [jnp.broadcast_to(table[:, d : d + 1], (8, 128)) for d in range(4)]
    total = total[:4]
    x = jnp.concatenate([total, pltpu.roll(total, 64, 1)], axis=0)
    for _ in range(2):
        right = jnp.where(tile < 7, pltpu.roll(x, 7, 0), 0.0)
        left = jnp.where(tile > 0, pltpu.roll(x, 1, 0), 0.0)
        out = x + coef[0] * (left + right - 2.0 * x)
        for d, shift in ((1, 4), (2, 2), (3, 0)):
            place, stride = (node >> shift) & 3, 1 << shift
            up = jnp.where(place < 3, pltpu.roll(x, 128 - stride, 1), 0.0)
            down = jnp.where(place > 0, pltpu.roll(x, stride, 1), 0.0)
            out = out + coef[d] * (up + down - 2.0 * x)
        x = out
    o_ref[...] = x[2:6, :64]


def call(kernel, out_shape, n_smem, n_vmem, n_hbm=0, scratch=()):
    many = isinstance(out_shape, tuple)
    return pl.pallas_call(
        kernel,
        out_shape=out_shape,
        in_specs=[SMEM] * n_smem + [VMEM] * n_vmem + [HBM] * n_hbm,
        out_specs=(VMEM,) * len(out_shape) if many else VMEM,
        scratch_shapes=scratch,
        compiler_params=PARAMS,
    )


def per_device(
    forward_start, adjoint_start, stiffness, projection, material, neighbours, destinations, counts, smoothing
):
    elements = forward_start.shape[-1]
    tile_width = smoothing.shape[1]
    n_mesh, n_event = lax.axis_size("mesh"), lax.axis_size("event")
    scale = math.sqrt(tile_width / elements) / STEPS
    forward, adjoint = (x.reshape(3, NODES, 1, 128) for x in (forward_start, adjoint_start))
    up = [(i, (i + 1) % n_mesh) for i in range(n_mesh)]
    down = [(j, i) for i, j in up]
    first_mesh, first_event = 5 * n_mesh // 8, n_event // 2
    mesh_group = [(i + first_mesh) % n_mesh for i in range(n_mesh)]
    event_group = [(i + first_event) % n_event for i in range(n_event)]

    near, project = neighbours.reshape(FACES, 1, 128), projection.T
    inputs = (forward, adjoint, smoothing, near, stiffness, material, project, destinations)
    inputs = [pltpu.with_memory_space_constraint(x, pltpu.HBM) for x in inputs]
    rim, fields, smooth_in = call(
        pack_kernel,
        (shape(200, 128), shape(6, 128, 128), shape(4, tile_width)),
        1,
        0,
        3,
        [pltpu.VMEM(x.shape, F32) for x in (forward, adjoint)] + [pltpu.SemaphoreType.DMA((3,))],
    )(counts, *inputs[:3])
    after, before = lax.ppermute(rim, "mesh", down), lax.ppermute(rim, "mesh", up)
    partial, kernel, turned, stiff, pick, lift, project, wanted, near, material = call(
        own_kernel,
        (
            shape(6, 128, 128),
            shape(128, 128),
            shape(8, 128),
            shape(2, 128, 128, dtype=BF16),
            shape(FACES * SHEET, 128, dtype=BF16),
            shape(128, FACES * SHEET, dtype=BF16),
            shape(2, 64, 128, dtype=BF16),
            shape(8, 128),
            shape(FACES, 1, 128, dtype=I32),
            shape(1, 128),
        ),
        1,
        2,
        5,
        [pltpu.VMEM(x.shape, x.dtype) for x in (stiffness, project, destinations)] + [pltpu.SemaphoreType.DMA((5,))],
    )(counts, fields, smooth_in, *inputs[3:])

    def one_step(*refs):
        step_kernel(scale, n_mesh, *refs)

    one, strain, rim_one, edge, chunk = call(
        one_step,
        (shape(3, 128, 128), shape(3, 128, 128), shape(128, 128), shape(8, 128), shape(n_mesh, 72, 128)),
        1,
        10,
    )(counts, partial, kernel, after, before, near, stiff, pick, lift, project, wanted)
    parts = lax.all_to_all(chunk, "mesh", 0, 0, tiled=True, axis_index_groups=[mesh_group])

    after, before = lax.ppermute(rim_one, "mesh", down), lax.ppermute(rim_one, "mesh", up)

    def dense(*refs):
        dense_kernel(n_event, n_mesh, tile_width, first_event, *refs)

    partial = call(dense, shape(5 * n_event, 128), 0, 4)(parts, edge, after, before)
    pieces = lax.all_to_all(partial.reshape(-1, 1, 128), "event", 0, 0, tiled=True, axis_index_groups=[event_group])
    final, table, is_open = call(last_kernel, (shape(3, NODES, 1, 128), shape(8, 128), shape(8, 128)), 1, 11)(
        counts, fields, one, strain, after, before, near, material, pick, lift, turned, edge
    )

    def smooth(*refs):
        smooth_kernel(n_event, *refs)

    tiles = call(smooth, shape(tile_width, 64), 0, 3)(pieces.reshape(-1, 128), table, is_open)
    return final.reshape(1, 3, NODES, 128), tiles.T


def solution(mesh):
    in_specs = (
        P("event", None, None, "mesh"),
        P("event", None, None, "mesh"),
        P(),
        P(),
        P("event", "mesh"),
        P("event", None, "mesh"),
        P("event", "mesh"),
        P("event", "mesh"),
        P(None, ("event", "mesh")),
    )
    out_specs = (P("event", None, None, "mesh"), P(None, ("event", "mesh")))
    return jax.shard_map(per_device, mesh=mesh, in_specs=in_specs, out_specs=out_specs, check_vma=False)
```

```python
import math

import jax
import jax.numpy as jnp
from jax import lax
from jax.experimental import pallas as pl
from jax.experimental.pallas import tpu as pltpu
from jax.sharding import PartitionSpec as P

STEPS = 2
NODES = 125
RIM = 32
SHEET = 32
FACES = 6
F32, BF16, I32 = jnp.float32, jnp.bfloat16, jnp.int32
partner_face = (1, 0, 3, 2, 5, 4)

VMEM = pl.BlockSpec(memory_space=pltpu.VMEM)
SMEM = pl.BlockSpec(memory_space=pltpu.SMEM)
HBM = pl.BlockSpec(memory_space=pltpu.HBM)
PARAMS = pltpu.CompilerParams(vmem_limit_bytes=40 * 2**20)


def shape(*dims, dtype=F32):
    return jax.ShapeDtypeStruct(dims, dtype)


def iota(dims, axis):
    return lax.broadcasted_iota(I32, dims, axis)


def halves(x):
    high = x.astype(BF16)
    return high, (x - high.astype(F32)).astype(BF16)


def dot(a, b):
    return lax.dot_general(a, b, (((1,), (0,)), ((), ())), preferred_element_type=F32)


def face_nodes(dims, axis):
    row = iota(dims, axis)
    face, q = row // SHEET, row % SHEET
    a = sum((q >= 5 * i).astype(I32) for i in range(1, 5))
    b = q - 5 * a
    node = jnp.where(face == 0, q, q + 100)
    node = jnp.where(face == 2, 25 * a + b, node)
    node = jnp.where(face == 3, 25 * a + 20 + b, node)
    node = jnp.where(face == 4, 5 * q, node)
    node = jnp.where(face == 5, 5 * q + 4, node)
    return jnp.where(q < 25, node, -1)


def picker():
    dims = (FACES * SHEET, 128)
    return jnp.where(face_nodes(dims, 0) == iota(dims, 1), 1.0, 0.0).astype(BF16)


def lifter():
    dims = (128, FACES * SHEET)
    return jnp.where(face_nodes(dims, 1) == iota(dims, 0), 1.0, 0.0).astype(BF16)


def rows_of(ref):
    return ref.reshape(3 * NODES, 128)


def padded(ref, c):
    rows = rows_of(ref)[NODES * c : NODES * (c + 1)]
    return jnp.concatenate([rows, jnp.zeros((128 - NODES, 128), F32)], axis=0)


def stacked(fields):
    high, low = halves(jnp.concatenate(fields, axis=1))
    return jnp.concatenate([high, low], axis=0)


def pack_rim(fields):
    lane = iota((128, 128), 1)
    out = fields[0]
    for k in range(1, len(fields)):
        out = jnp.where(lane < RIM * k, out, pltpu.roll(fields[k], RIM * k, 1))
    return jnp.where(lane < RIM * len(fields), out, 0.0)


def fold(x):
    return jnp.where(iota((64, 128), 1) < 64, x[:64], pltpu.roll(x[64:], 64, 1))


def live_mask(count_ref):
    return (iota((128, 128), 1) < count_ref[0, 0]).astype(F32)


def edge_row(smooth_ref):
    width = smooth_ref.shape[1]
    last = jnp.broadcast_to(smooth_ref[:, width - 1 : width], (4, 128))
    first = jnp.broadcast_to(smooth_ref[:, 0:1], (4, 128))
    lane, row = iota((4, 128), 1), iota((4, 128), 0)
    spread = jnp.where(lane == row, last, 0.0) + jnp.where(lane == row + 4, first, 0.0)
    return jnp.sum(spread, axis=0, keepdims=True)


def copies_of(sources, targets, sems):
    copies = [pltpu.make_async_copy(a, b, sems.at[i]) for i, (a, b) in enumerate(zip(sources, targets))]
    for copy in copies:
        copy.start()
    return copies


def pack_kernel(count_ref, forward_ref, adjoint_ref, smooth_ref, rim_ref, field_ref, smooth_out_ref, *held):
    copies = copies_of((forward_ref, adjoint_ref, smooth_ref), (*held[:2], smooth_out_ref), held[2])
    live = live_mask(count_ref)
    fields = []
    for ref, copy in zip(held[:2], copies):
        copy.wait()
        fields += [padded(ref, c) * live for c in range(3)]
    rim_ref[:128] = pack_rim(fields[:4])
    rim_ref[128:192] = fold(pack_rim(fields[4:]))
    for k in range(6):
        field_ref[k] = fields[k]
    copies[2].wait()
    rim_ref[192:] = jnp.broadcast_to(edge_row(smooth_out_ref), (8, 128))


def split_stiffness(stiff_ref):
    wide = jnp.concatenate([stiff_ref[...], jnp.zeros((NODES, 128 - NODES), F32)], axis=1)
    return halves(jnp.concatenate([wide, jnp.zeros((128 - NODES, 128), F32)], axis=0))


def columns(x):
    return [x[:, 128 * k : 128 * (k + 1)] for k in range(x.shape[1] // 128)]


def strains(high, low, x):
    return columns(dot(jnp.concatenate([high, high], axis=1), x) + dot(low, x[:128]))


def faces_of(pick, x):
    return columns(dot(jnp.concatenate([pick, pick], axis=1), x))


def take(x, index):
    return jnp.take_along_axis(x, index, axis=1, mode="promise_in_bounds")


def lift_of(lift, jumps):
    high, low = halves(jnp.concatenate([jnp.concatenate(j, axis=0) for j in jumps], axis=1))
    return columns(dot(lift, high) + dot(lift, low))


def own_jumps(near_ref, own):
    jumps = [[] for _ in own]
    for face in range(FACES):
        p = partner_face[face]
        near = jnp.broadcast_to(near_ref[face], (SHEET, 128))
        home = near // 128 == lax.axis_index("mesh")
        slot = near % 128
        for k in range(len(own)):
            here = take(own[k][SHEET * p : SHEET * (p + 1)], slot)
            jumps[k].append(jnp.where(home, here, 0.0) - own[k][SHEET * face : SHEET * (face + 1)])
    return jumps


def rim_jumps(near_ref, rims, n):
    mine, parts = lax.axis_index("mesh"), lax.axis_size("mesh")
    follower = jnp.where(mine + 1 == parts, 0, mine + 1)
    jumps = [[] for _ in range(n)]
    for face in range(FACES):
        p = partner_face[face]
        near = jnp.broadcast_to(near_ref[face], (SHEET, 128))
        target = near // 128
        away = target != mine
        index = near % RIM + jnp.where(target == follower, 64, 0)
        for k in range(n):
            across = take(rims[k // 2][SHEET * p : SHEET * (p + 1)], index + RIM * (k % 2))
            jumps[k].append(jnp.where(away, across, 0.0))
    return jumps


def merge(before, after):
    lane = iota(before.shape, 1)
    first = jnp.where(lane < 64, before, pltpu.roll(after, 64, 1))
    second = jnp.where(lane < 64, pltpu.roll(before, 64, 1), after)
    return first, second


def own_kernel(
    count_ref, field_ref, smooth_ref, near_in, stiff_in, material_in, project_in, destination_in,
    partial_ref, kernel_ref, turned_ref, stiff_out_ref, pick_ref, lift_ref, project_out_ref, wanted_ref, near_ref,
    material_ref, stiff_ref, project_ref, destination_ref, sems,
):
    copies = copies_of(
        (near_in, stiff_in, material_in, project_in, destination_in),
        (near_ref, stiff_ref, material_ref, project_ref, destination_ref),
        sems,
    )
    live = live_mask(count_ref)
    fields = [field_ref[k] for k in range(6)]
    pick, lift = picker(), lifter()
    pick_ref[...] = pick
    lift_ref[...] = lift
    x = stacked(fields)
    faces = faces_of(pick, x)
    copies[0].wait()
    lifted = lift_of(lift, own_jumps(near_ref, faces))
    for copy in copies[1:]:
        copy.wait()
    material = jnp.broadcast_to(material_ref[...], (128, 128))
    high, low = split_stiffness(stiff_ref)
    stiff_out_ref[0] = high
    stiff_out_ref[1] = low
    strain = strains(high, low, x)
    for k in range(6):
        force = 0.5 * lifted[k] - material * strain[k]
        partial_ref[k] = live * (fields[k] + 0.4 * force)
    kernel_ref[...] = sum(fields[c] * strain[3 + c] for c in range(3))
    high, low = halves(jnp.concatenate([project_ref[...], jnp.zeros((64, 128 - NODES), F32)], axis=1))
    project_out_ref[0] = high
    project_out_ref[1] = low
    wanted_ref[...] = jnp.broadcast_to(destination_ref[...].astype(F32), (8, 128))
    width = smooth_ref.shape[1]
    wide = jnp.concatenate([smooth_ref[...], jnp.zeros((4, 128 - width), F32)], axis=1)
    turned_ref[...] = jnp.concatenate([wide, jnp.zeros((124, 128), F32)], axis=0).T[:8]


def step_kernel(
    scale, n_mesh,
    count_ref, partial_ref, kernel_ref, after_ref, before_ref, near_ref, stiff_ref, pick_ref, lift_ref,
    project_ref, wanted_ref,
    forward_ref, strain_ref, rim_ref, edge_ref, chunk_ref,
):
    live = live_mask(count_ref)
    first, second = merge(before_ref[:128], after_ref[:128])
    upper, lower = merge(before_ref[128:192], after_ref[128:192])
    rims = faces_of(pick_ref[...], stacked([first, second, jnp.concatenate([upper, lower], axis=0)]))
    lift = lift_of(lift_ref[...], rim_jumps(near_ref, rims, 6))
    fields = [partial_ref[k] + live * (0.2 * lift[k]) for k in range(6)]
    strain = strains(stiff_ref[0], stiff_ref[1], stacked(fields))
    kernel = kernel_ref[...] + sum(fields[c] * strain[3 + c] for c in range(3))
    k_high, k_low = halves(kernel)
    p_high, p_low = project_ref[0], project_ref[1]
    blocks = dot(jnp.concatenate([p_high, p_high], axis=1), jnp.concatenate([k_high, k_low], axis=0))
    blocks = (blocks + dot(p_low, k_high)) * scale
    for m in range(n_mesh):
        chunk_ref[m, :64] = blocks
        chunk_ref[m, 64:] = wanted_ref[...]
    rim_ref[...] = pack_rim(fields[:3])
    edge_ref[...] = jnp.where(iota((8, 128), 1) < 4, before_ref[192:], after_ref[192:])
    for c in range(3):
        forward_ref[c] = fields[c]
        strain_ref[c] = strain[c]


def dense_kernel(n_event, n_mesh, tile_width, first, parts_ref, edge_ref, before_ref, out_ref):
    rows = 8 * n_event
    row = iota((rows, 128), 0)
    tile = (row % n_event + first) % n_event * (n_mesh * tile_width) + row // n_event - 2
    tile = tile.astype(F32) + (lax.axis_index("mesh") * tile_width).astype(F32)
    left, right = [], []
    for m in range(n_mesh):
        left.append(jnp.concatenate(halves(parts_ref[m, :64]), axis=0))
        wanted = jnp.broadcast_to(parts_ref[m, 64:65], (rows, 128))
        right.append(jnp.where(wanted == tile, 1.0, 0.0).astype(BF16))
    left, right = jnp.concatenate(left, axis=1), jnp.concatenate(right, axis=1)
    both = lax.dot_general(left, right, (((1,), (1,)), ((), ())), preferred_element_type=F32)
    both = both[:64] + both[64:]
    half = 4 * n_event
    both = jnp.concatenate([both[:, :half], both[:, half:]], axis=0).T
    for j in range(4):
        out_ref[pl.ds(j, n_event, stride=5)] = both[n_event * j : n_event * (j + 1)]
    lane, event = iota((n_event, 128), 1), (iota((n_event, 128), 0) + first) % n_event
    apart = event - lax.axis_index("event")
    used = ((apart == 1) & (lane < 4)) | ((apart == -1) & (lane >= 4) & (lane < 8))
    edges = jnp.where(used, jnp.broadcast_to(edge_ref[0:1], (n_event, 128)), 0.0)
    out_ref[pl.ds(4, n_event, stride=5)] = edges


def last_kernel(
    count_ref, field_ref, one_ref, strain_ref, after_ref, before_ref, near_ref, material_ref, pick_ref, lift_ref,
    turned_ref, edge_ref,
    final_ref, table_ref, open_ref,
):
    live = live_mask(count_ref)
    material = jnp.broadcast_to(material_ref[...], (128, 128))
    fields = [one_ref[c] for c in range(3)]
    jumps = own_jumps(near_ref, faces_of(pick_ref[...], stacked(fields)))
    rims = faces_of(pick_ref[...], stacked(list(merge(before_ref[...], after_ref[...]))))
    more = rim_jumps(near_ref, rims, 3)
    lift = lift_of(lift_ref[...], [[a + b for a, b in zip(*pair)] for pair in zip(jumps, more)])
    final = rows_of(final_ref)
    for c in range(3):
        force = 0.5 * lift[c] - material * strain_ref[c]
        out = live * (2.0 * fields[c] - field_ref[c] + 0.4 * force)
        final[NODES * c : NODES * (c + 1)] = out[:NODES]
    mine, parts = lax.axis_index("mesh"), lax.axis_size("mesh")
    tile = iota((8, 128), 0)
    is_open = ((tile == 1) & (mine == 0)) | ((tile == 6) & (mine == parts - 1))
    edge = jnp.where(tile == 6, pltpu.roll(edge_ref[...], 124, 1), edge_ref[...])
    edge = jnp.where(((tile == 1) | (tile == 6)) & ~is_open, edge, 0.0)
    table_ref[...] = jnp.where((tile >= 2) & (tile < 6), pltpu.roll(turned_ref[...], 2, 0), edge)
    open_ref[...] = is_open.astype(F32)


def total_of(parts):
    while len(parts) > 1:
        parts = [sum(parts[i : i + 2][1:], parts[i]) for i in range(0, len(parts), 2)]
    return parts[0]


def smooth_kernel(n_event, x_ref, table_ref, open_ref, o_ref):
    node, tile = iota((8, 128), 1), iota((8, 128), 0)
    span = 40 if n_event % 8 == 0 else 5 * n_event
    total = total_of([x_ref[i : i + span] for i in range(0, 5 * n_event, span)])
    total = total_of([total[i : i + 5] for i in range(0, span, 5)])
    edge = jnp.broadcast_to(total[4:5], (8, 128))
    edge = jnp.where(tile == 6, pltpu.roll(edge, 124, 1), edge)
    table = table_ref[...] + open_ref[...] * edge
    coef = [jnp.broadcast_to(table[:, d : d + 1], (8, 128)) for d in range(4)]
    total = total[:4]
    x = jnp.concatenate([total, pltpu.roll(total, 64, 1)], axis=0)
    for _ in range(2):
        right = jnp.where(tile < 7, pltpu.roll(x, 7, 0), 0.0)
        left = jnp.where(tile > 0, pltpu.roll(x, 1, 0), 0.0)
        out = x + coef[0] * (left + right - 2.0 * x)
        for d, shift in ((1, 4), (2, 2), (3, 0)):
            place, stride = (node >> shift) & 3, 1 << shift
            up = jnp.where(place < 3, pltpu.roll(x, 128 - stride, 1), 0.0)
            down = jnp.where(place > 0, pltpu.roll(x, stride, 1), 0.0)
            out = out + coef[d] * (up + down - 2.0 * x)
        x = out
    o_ref[...] = x[2:6, :64]


def call(kernel, out_shape, n_smem, n_vmem, n_hbm=0, scratch=()):
    many = isinstance(out_shape, tuple)
    return pl.pallas_call(
        kernel,
        out_shape=out_shape,
        in_specs=[SMEM] * n_smem + [VMEM] * n_vmem + [HBM] * n_hbm,
        out_specs=(VMEM,) * len(out_shape) if many else VMEM,
        scratch_shapes=scratch,
        compiler_params=PARAMS,
    )


def per_device(
    forward_start, adjoint_start, stiffness, projection, material, neighbours, destinations, counts, smoothing
):
    elements = forward_start.shape[-1]
    tile_width = smoothing.shape[1]
    n_mesh, n_event = lax.axis_size("mesh"), lax.axis_size("event")
    scale = math.sqrt(tile_width / elements) / STEPS
    forward, adjoint = (x.reshape(3, NODES, 1, 128) for x in (forward_start, adjoint_start))
    up = [(i, (i + 1) % n_mesh) for i in range(n_mesh)]
    down = [(j, i) for i, j in up]
    first_mesh, first_event = 5 * n_mesh // 8, n_event // 2
    mesh_group = [(i + first_mesh) % n_mesh for i in range(n_mesh)]
    event_group = [(i + first_event) % n_event for i in range(n_event)]

    near, project = neighbours.reshape(FACES, 1, 128), projection.T
    inputs = (forward, adjoint, smoothing, near, stiffness, material, project, destinations)
    inputs = [pltpu.with_memory_space_constraint(x, pltpu.HBM) for x in inputs]
    rim, fields, smooth_in = call(
        pack_kernel,
        (shape(200, 128), shape(6, 128, 128), shape(4, tile_width)),
        1,
        0,
        3,
        [pltpu.VMEM(x.shape, F32) for x in (forward, adjoint)] + [pltpu.SemaphoreType.DMA((3,))],
    )(counts, *inputs[:3])
    after, before = lax.ppermute(rim, "mesh", down), lax.ppermute(rim, "mesh", up)
    partial, kernel, turned, stiff, pick, lift, project, wanted, near, material = call(
        own_kernel,
        (
            shape(6, 128, 128),
            shape(128, 128),
            shape(8, 128),
            shape(2, 128, 128, dtype=BF16),
            shape(FACES * SHEET, 128, dtype=BF16),
            shape(128, FACES * SHEET, dtype=BF16),
            shape(2, 64, 128, dtype=BF16),
            shape(8, 128),
            shape(FACES, 1, 128, dtype=I32),
            shape(1, 128),
        ),
        1,
        2,
        5,
        [pltpu.VMEM(x.shape, x.dtype) for x in (stiffness, project, destinations)] + [pltpu.SemaphoreType.DMA((5,))],
    )(counts, fields, smooth_in, *inputs[3:])

    def one_step(*refs):
        step_kernel(scale, n_mesh, *refs)

    one, strain, rim_one, edge, chunk = call(
        one_step,
        (shape(3, 128, 128), shape(3, 128, 128), shape(128, 128), shape(8, 128), shape(n_mesh, 72, 128)),
        1,
        10,
    )(counts, partial, kernel, after, before, near, stiff, pick, lift, project, wanted)
    parts = lax.all_to_all(chunk, "mesh", 0, 0, tiled=True, axis_index_groups=[mesh_group])

    before = lax.ppermute(rim_one, "mesh", up)

    def dense(*refs):
        dense_kernel(n_event, n_mesh, tile_width, first_event, *refs)

    partial = call(dense, shape(5 * n_event, 128), 0, 3)(parts, edge, before)
    pieces = lax.all_to_all(partial.reshape(-1, 1, 128), "event", 0, 0, tiled=True, axis_index_groups=[event_group])
    rim_one, _ = lax.optimization_barrier((rim_one, partial))
    after = lax.ppermute(rim_one, "mesh", down)
    final, table, is_open = call(last_kernel, (shape(3, NODES, 1, 128), shape(8, 128), shape(8, 128)), 1, 11)(
        counts, fields, one, strain, after, before, near, material, pick, lift, turned, edge
    )

    def smooth(*refs):
        smooth_kernel(n_event, *refs)

    tiles = call(smooth, shape(tile_width, 64), 0, 3)(pieces.reshape(-1, 128), table, is_open)
    return final.reshape(1, 3, NODES, 128), tiles.T


def solution(mesh):
    in_specs = (
        P("event", None, None, "mesh"),
        P("event", None, None, "mesh"),
        P(),
        P(),
        P("event", "mesh"),
        P("event", None, "mesh"),
        P("event", "mesh"),
        P("event", "mesh"),
        P(None, ("event", "mesh")),
    )
    out_specs = (P("event", None, None, "mesh"), P(None, ("event", "mesh")))
    return jax.shard_map(per_device, mesh=mesh, in_specs=in_specs, out_specs=out_specs, check_vma=False)
```

```python
import math

import jax
import jax.numpy as jnp
from jax import lax
from jax.experimental import pallas as pl
from jax.experimental.pallas import tpu as pltpu
from jax.sharding import PartitionSpec as P

STEPS = 2
NODES = 125
RIM = 32
SHEET = 32
FACES = 6
F32, BF16, I32 = jnp.float32, jnp.bfloat16, jnp.int32
partner_face = (1, 0, 3, 2, 5, 4)

VMEM = pl.BlockSpec(memory_space=pltpu.VMEM)
SMEM = pl.BlockSpec(memory_space=pltpu.SMEM)
HBM = pl.BlockSpec(memory_space=pltpu.HBM)
PARAMS = pltpu.CompilerParams(vmem_limit_bytes=40 * 2**20)


def shape(*dims, dtype=F32):
    return jax.ShapeDtypeStruct(dims, dtype)


def iota(dims, axis):
    return lax.broadcasted_iota(I32, dims, axis)


def halves(x):
    high = x.astype(BF16)
    return high, (x - high.astype(F32)).astype(BF16)


def dot(a, b):
    return lax.dot_general(a, b, (((1,), (0,)), ((), ())), preferred_element_type=F32)


def face_nodes(dims, axis):
    row = iota(dims, axis)
    face, q = row // SHEET, row % SHEET
    a = sum((q >= 5 * i).astype(I32) for i in range(1, 5))
    b = q - 5 * a
    node = jnp.where(face == 0, q, q + 100)
    node = jnp.where(face == 2, 25 * a + b, node)
    node = jnp.where(face == 3, 25 * a + 20 + b, node)
    node = jnp.where(face == 4, 5 * q, node)
    node = jnp.where(face == 5, 5 * q + 4, node)
    return jnp.where(q < 25, node, -1)


def picker():
    dims = (FACES * SHEET, 128)
    return jnp.where(face_nodes(dims, 0) == iota(dims, 1), 1.0, 0.0).astype(BF16)


def lifter():
    dims = (128, FACES * SHEET)
    return jnp.where(face_nodes(dims, 1) == iota(dims, 0), 1.0, 0.0).astype(BF16)


def rows_of(ref):
    return ref.reshape(3 * NODES, 128)


def padded(ref, c):
    rows = rows_of(ref)[NODES * c : NODES * (c + 1)]
    return jnp.concatenate([rows, jnp.zeros((128 - NODES, 128), F32)], axis=0)


def stacked(fields):
    high, low = halves(jnp.concatenate(fields, axis=1))
    return jnp.concatenate([high, low], axis=0)


def pack_rim(fields):
    lane = iota((128, 128), 1)
    out = fields[0]
    for k in range(1, len(fields)):
        out = jnp.where(lane < RIM * k, out, pltpu.roll(fields[k], RIM * k, 1))
    return jnp.where(lane < RIM * len(fields), out, 0.0)


def fold(x):
    return jnp.where(iota((64, 128), 1) < 64, x[:64], pltpu.roll(x[64:], 64, 1))


def live_mask(count_ref):
    return (iota((128, 128), 1) < count_ref[0, 0]).astype(F32)


def edge_row(smooth_ref):
    width = smooth_ref.shape[1]
    last = jnp.broadcast_to(smooth_ref[:, width - 1 : width], (4, 128))
    first = jnp.broadcast_to(smooth_ref[:, 0:1], (4, 128))
    lane, row = iota((4, 128), 1), iota((4, 128), 0)
    spread = jnp.where(lane == row, last, 0.0) + jnp.where(lane == row + 4, first, 0.0)
    return jnp.sum(spread, axis=0, keepdims=True)


def copies_of(sources, targets, sems):
    copies = [pltpu.make_async_copy(a, b, sems.at[i]) for i, (a, b) in enumerate(zip(sources, targets))]
    for copy in copies:
        copy.start()
    return copies


def pack_kernel(count_ref, forward_ref, adjoint_ref, smooth_ref, rim_ref, field_ref, smooth_out_ref, *held):
    copies = copies_of((forward_ref, adjoint_ref, smooth_ref), (*held[:2], smooth_out_ref), held[2])
    live = live_mask(count_ref)
    fields = []
    for ref, copy in zip(held[:2], copies):
        copy.wait()
        fields += [padded(ref, c) * live for c in range(3)]
    rim_ref[:128] = pack_rim(fields[:4])
    rim_ref[128:192] = fold(pack_rim(fields[4:]))
    for k in range(6):
        field_ref[k] = fields[k]
    copies[2].wait()
    rim_ref[192:] = jnp.broadcast_to(edge_row(smooth_out_ref), (8, 128))


def split_stiffness(stiff_ref):
    wide = jnp.concatenate([stiff_ref[...], jnp.zeros((NODES, 128 - NODES), F32)], axis=1)
    return halves(jnp.concatenate([wide, jnp.zeros((128 - NODES, 128), F32)], axis=0))


def columns(x):
    return [x[:, 128 * k : 128 * (k + 1)] for k in range(x.shape[1] // 128)]


def strains(high, low, x):
    return columns(dot(jnp.concatenate([high, high], axis=1), x) + dot(low, x[:128]))


def faces_of(pick, x):
    return columns(dot(jnp.concatenate([pick, pick], axis=1), x))


def take(x, index):
    return jnp.take_along_axis(x, index, axis=1, mode="promise_in_bounds")


def lift_of(lift, jumps):
    high, low = halves(jnp.concatenate([jnp.concatenate(j, axis=0) for j in jumps], axis=1))
    return columns(dot(lift, high) + dot(lift, low))


def own_jumps(near_ref, own):
    jumps = [[] for _ in own]
    for face in range(FACES):
        p = partner_face[face]
        near = jnp.broadcast_to(near_ref[face], (SHEET, 128))
        home = near // 128 == lax.axis_index("mesh")
        slot = near % 128
        for k in range(len(own)):
            here = take(own[k][SHEET * p : SHEET * (p + 1)], slot)
            jumps[k].append(jnp.where(home, here, 0.0) - own[k][SHEET * face : SHEET * (face + 1)])
    return jumps


def rim_jumps(near_ref, rims, n):
    mine, parts = lax.axis_index("mesh"), lax.axis_size("mesh")
    follower = jnp.where(mine + 1 == parts, 0, mine + 1)
    jumps = [[] for _ in range(n)]
    for face in range(FACES):
        p = partner_face[face]
        near = jnp.broadcast_to(near_ref[face], (SHEET, 128))
        target = near // 128
        away = target != mine
        index = near % RIM + jnp.where(target == follower, 64, 0)
        for k in range(n):
            across = take(rims[k // 2][SHEET * p : SHEET * (p + 1)], index + RIM * (k % 2))
            jumps[k].append(jnp.where(away, across, 0.0))
    return jumps


def merge(before, after):
    lane = iota(before.shape, 1)
    first = jnp.where(lane < 64, before, pltpu.roll(after, 64, 1))
    second = jnp.where(lane < 64, pltpu.roll(before, 64, 1), after)
    return first, second


def own_kernel(
    count_ref, field_ref, smooth_ref, near_in, stiff_in, material_in, project_in, destination_in,
    partial_ref, kernel_ref, turned_ref, stiff_out_ref, pick_ref, lift_ref, project_out_ref, wanted_ref, near_ref,
    material_ref, stiff_ref, project_ref, destination_ref, sems,
):
    copies = copies_of(
        (near_in, stiff_in, material_in, project_in, destination_in),
        (near_ref, stiff_ref, material_ref, project_ref, destination_ref),
        sems,
    )
    live = live_mask(count_ref)
    fields = [field_ref[k] for k in range(6)]
    pick, lift = picker(), lifter()
    pick_ref[...] = pick
    lift_ref[...] = lift
    x = stacked(fields)
    faces = faces_of(pick, x)
    copies[0].wait()
    lifted = lift_of(lift, own_jumps(near_ref, faces))
    for copy in copies[1:]:
        copy.wait()
    material = jnp.broadcast_to(material_ref[...], (128, 128))
    high, low = split_stiffness(stiff_ref)
    stiff_out_ref[0] = high
    stiff_out_ref[1] = low
    strain = strains(high, low, x)
    for k in range(6):
        force = 0.5 * lifted[k] - material * strain[k]
        partial_ref[k] = live * (fields[k] + 0.4 * force)
    kernel_ref[...] = sum(fields[c] * strain[3 + c] for c in range(3))
    high, low = halves(jnp.concatenate([project_ref[...], jnp.zeros((64, 128 - NODES), F32)], axis=1))
    project_out_ref[0] = high
    project_out_ref[1] = low
    wanted_ref[...] = jnp.broadcast_to(destination_ref[...].astype(F32), (8, 128))
    width = smooth_ref.shape[1]
    wide = jnp.concatenate([smooth_ref[...], jnp.zeros((4, 128 - width), F32)], axis=1)
    turned_ref[...] = jnp.concatenate([wide, jnp.zeros((124, 128), F32)], axis=0).T[:8]


def step_kernel(
    scale, n_mesh,
    count_ref, partial_ref, kernel_ref, after_ref, before_ref, near_ref, stiff_ref, pick_ref, lift_ref,
    project_ref, wanted_ref,
    forward_ref, strain_ref, rim_ref, edge_ref, chunk_ref,
):
    live = live_mask(count_ref)
    first, second = merge(before_ref[:128], after_ref[:128])
    upper, lower = merge(before_ref[128:192], after_ref[128:192])
    rims = faces_of(pick_ref[...], stacked([first, second, jnp.concatenate([upper, lower], axis=0)]))
    lift = lift_of(lift_ref[...], rim_jumps(near_ref, rims, 6))
    fields = [partial_ref[k] + live * (0.2 * lift[k]) for k in range(6)]
    strain = strains(stiff_ref[0], stiff_ref[1], stacked(fields))
    kernel = kernel_ref[...] + sum(fields[c] * strain[3 + c] for c in range(3))
    k_high, k_low = halves(kernel)
    p_high, p_low = project_ref[0], project_ref[1]
    blocks = dot(jnp.concatenate([p_high, p_high], axis=1), jnp.concatenate([k_high, k_low], axis=0))
    blocks = (blocks + dot(p_low, k_high)) * scale
    for m in range(n_mesh):
        chunk_ref[m, :64] = blocks
        chunk_ref[m, 64:] = wanted_ref[...]
    rim_ref[...] = pack_rim(fields[:3])
    edge_ref[...] = jnp.where(iota((8, 128), 1) < 4, before_ref[192:], after_ref[192:])
    for c in range(3):
        forward_ref[c] = fields[c]
        strain_ref[c] = strain[c]


def dense_kernel(n_event, n_mesh, tile_width, first, parts_ref, edge_ref, before_ref, out_ref):
    rows = 8 * n_event
    row = iota((rows, 128), 0)
    tile = (row % n_event + first) % n_event * (n_mesh * tile_width) + row // n_event - 2
    tile = tile.astype(F32) + (lax.axis_index("mesh") * tile_width).astype(F32)
    left, right = [], []
    for m in range(n_mesh):
        left.append(jnp.concatenate(halves(parts_ref[m, :64]), axis=0))
        wanted = jnp.broadcast_to(parts_ref[m, 64:65], (rows, 128))
        right.append(jnp.where(wanted == tile, 1.0, 0.0).astype(BF16))
    left, right = jnp.concatenate(left, axis=1), jnp.concatenate(right, axis=1)
    both = lax.dot_general(left, right, (((1,), (1,)), ((), ())), preferred_element_type=F32)
    both = both[:64] + both[64:]
    half = 4 * n_event
    both = jnp.concatenate([both[:, :half], both[:, half:]], axis=0).T
    for j in range(4):
        out_ref[pl.ds(j, n_event, stride=5)] = both[n_event * j : n_event * (j + 1)]
    lane, event = iota((n_event, 128), 1), (iota((n_event, 128), 0) + first) % n_event
    apart = event - lax.axis_index("event")
    used = ((apart == 1) & (lane < 4)) | ((apart == -1) & (lane >= 4) & (lane < 8))
    edges = jnp.where(used, jnp.broadcast_to(edge_ref[0:1], (n_event, 128)), 0.0)
    out_ref[pl.ds(4, n_event, stride=5)] = edges


def last_kernel(
    count_ref, field_ref, one_ref, strain_ref, after_ref, before_ref, near_ref, material_ref, pick_ref, lift_ref,
    turned_ref, edge_ref,
    final_ref, table_ref, open_ref,
):
    live = live_mask(count_ref)
    material = jnp.broadcast_to(material_ref[...], (128, 128))
    fields = [one_ref[c] for c in range(3)]
    jumps = own_jumps(near_ref, faces_of(pick_ref[...], stacked(fields)))
    rims = faces_of(pick_ref[...], stacked(list(merge(before_ref[...], after_ref[...]))))
    more = rim_jumps(near_ref, rims, 3)
    lift = lift_of(lift_ref[...], [[a + b for a, b in zip(*pair)] for pair in zip(jumps, more)])
    final = rows_of(final_ref)
    for c in range(3):
        force = 0.5 * lift[c] - material * strain_ref[c]
        out = live * (2.0 * fields[c] - field_ref[c] + 0.4 * force)
        final[NODES * c : NODES * (c + 1)] = out[:NODES]
    mine, parts = lax.axis_index("mesh"), lax.axis_size("mesh")
    tile = iota((8, 128), 0)
    is_open = ((tile == 1) & (mine == 0)) | ((tile == 6) & (mine == parts - 1))
    edge = jnp.where(tile == 6, pltpu.roll(edge_ref[...], 124, 1), edge_ref[...])
    edge = jnp.where(((tile == 1) | (tile == 6)) & ~is_open, edge, 0.0)
    table_ref[...] = jnp.where((tile >= 2) & (tile < 6), pltpu.roll(turned_ref[...], 2, 0), edge)
    open_ref[...] = is_open.astype(F32)


def total_of(parts):
    while len(parts) > 1:
        parts = [sum(parts[i : i + 2][1:], parts[i]) for i in range(0, len(parts), 2)]
    return parts[0]


def smooth_kernel(n_event, x_ref, table_ref, open_ref, o_ref):
    node, tile = iota((8, 128), 1), iota((8, 128), 0)
    span = 40 if n_event % 8 == 0 else 5 * n_event
    total = total_of([x_ref[i : i + span] for i in range(0, 5 * n_event, span)])
    total = total_of([total[i : i + 5] for i in range(0, span, 5)])
    edge = jnp.broadcast_to(total[4:5], (8, 128))
    edge = jnp.where(tile == 6, pltpu.roll(edge, 124, 1), edge)
    table = table_ref[...] + open_ref[...] * edge
    coef = [jnp.broadcast_to(table[:, d : d + 1], (8, 128)) for d in range(4)]
    total = total[:4]
    x = jnp.concatenate([total, pltpu.roll(total, 64, 1)], axis=0)
    for _ in range(2):
        right = jnp.where(tile < 7, pltpu.roll(x, 7, 0), 0.0)
        left = jnp.where(tile > 0, pltpu.roll(x, 1, 0), 0.0)
        out = x + coef[0] * (left + right - 2.0 * x)
        for d, shift in ((1, 4), (2, 2), (3, 0)):
            place, stride = (node >> shift) & 3, 1 << shift
            up = jnp.where(place < 3, pltpu.roll(x, 128 - stride, 1), 0.0)
            down = jnp.where(place > 0, pltpu.roll(x, stride, 1), 0.0)
            out = out + coef[d] * (up + down - 2.0 * x)
        x = out
    o_ref[...] = x[2:6, :64]


def call(kernel, out_shape, n_smem, n_vmem, n_hbm=0, scratch=()):
    many = isinstance(out_shape, tuple)
    return pl.pallas_call(
        kernel,
        out_shape=out_shape,
        in_specs=[SMEM] * n_smem + [VMEM] * n_vmem + [HBM] * n_hbm,
        out_specs=(VMEM,) * len(out_shape) if many else VMEM,
        scratch_shapes=scratch,
        compiler_params=PARAMS,
    )


def per_device(
    forward_start, adjoint_start, stiffness, projection, material, neighbours, destinations, counts, smoothing
):
    elements = forward_start.shape[-1]
    tile_width = smoothing.shape[1]
    n_mesh, n_event = lax.axis_size("mesh"), lax.axis_size("event")
    scale = math.sqrt(tile_width / elements) / STEPS
    forward, adjoint = (x.reshape(3, NODES, 1, 128) for x in (forward_start, adjoint_start))
    up = [(i, (i + 1) % n_mesh) for i in range(n_mesh)]
    down = [(j, i) for i, j in up]
    first_mesh, first_event = 0, n_event // 2
    mesh_group = [(i + first_mesh) % n_mesh for i in range(n_mesh)]
    event_group = [(i + first_event) % n_event for i in range(n_event)]

    near, project = neighbours.reshape(FACES, 1, 128), projection.T
    inputs = (forward, adjoint, smoothing, near, stiffness, material, project, destinations)
    inputs = [pltpu.with_memory_space_constraint(x, pltpu.HBM) for x in inputs]
    rim, fields, smooth_in = call(
        pack_kernel,
        (shape(200, 128), shape(6, 128, 128), shape(4, tile_width)),
        1,
        0,
        3,
        [pltpu.VMEM(x.shape, F32) for x in (forward, adjoint)] + [pltpu.SemaphoreType.DMA((3,))],
    )(counts, *inputs[:3])
    after, before = lax.ppermute(rim, "mesh", down), lax.ppermute(rim, "mesh", up)
    partial, kernel, turned, stiff, pick, lift, project, wanted, near, material = call(
        own_kernel,
        (
            shape(6, 128, 128),
            shape(128, 128),
            shape(8, 128),
            shape(2, 128, 128, dtype=BF16),
            shape(FACES * SHEET, 128, dtype=BF16),
            shape(128, FACES * SHEET, dtype=BF16),
            shape(2, 64, 128, dtype=BF16),
            shape(8, 128),
            shape(FACES, 1, 128, dtype=I32),
            shape(1, 128),
        ),
        1,
        2,
        5,
        [pltpu.VMEM(x.shape, x.dtype) for x in (stiffness, project, destinations)] + [pltpu.SemaphoreType.DMA((5,))],
    )(counts, fields, smooth_in, *inputs[3:])

    def one_step(*refs):
        step_kernel(scale, n_mesh, *refs)

    one, strain, rim_one, edge, chunk = call(
        one_step,
        (shape(3, 128, 128), shape(3, 128, 128), shape(128, 128), shape(8, 128), shape(n_mesh, 72, 128)),
        1,
        10,
    )(counts, partial, kernel, after, before, near, stiff, pick, lift, project, wanted)
    parts = lax.all_to_all(chunk, "mesh", 0, 0, tiled=True, axis_index_groups=[mesh_group])

    before = lax.ppermute(rim_one, "mesh", up)

    def dense(*refs):
        dense_kernel(n_event, n_mesh, tile_width, first_event, *refs)

    partial = call(dense, shape(5 * n_event, 128), 0, 3)(parts, edge, before)
    pieces = lax.all_to_all(partial.reshape(-1, 1, 128), "event", 0, 0, tiled=True, axis_index_groups=[event_group])
    rim_one, _ = lax.optimization_barrier((rim_one, partial))
    after = lax.ppermute(rim_one, "mesh", down)
    final, table, is_open = call(last_kernel, (shape(3, NODES, 1, 128), shape(8, 128), shape(8, 128)), 1, 11)(
        counts, fields, one, strain, after, before, near, material, pick, lift, turned, edge
    )

    def smooth(*refs):
        smooth_kernel(n_event, *refs)

    tiles = call(smooth, shape(tile_width, 64), 0, 3)(pieces.reshape(-1, 128), table, is_open)
    return final.reshape(1, 3, NODES, 128), tiles.T


def solution(mesh):
    in_specs = (
        P("event", None, None, "mesh"),
        P("event", None, None, "mesh"),
        P(),
        P(),
        P("event", "mesh"),
        P("event", None, "mesh"),
        P("event", "mesh"),
        P("event", "mesh"),
        P(None, ("event", "mesh")),
    )
    out_specs = (P("event", None, None, "mesh"), P(None, ("event", "mesh")))
    return jax.shard_map(per_device, mesh=mesh, in_specs=in_specs, out_specs=out_specs, check_vma=False)
```

```python
import math

import jax
import jax.numpy as jnp
from jax import lax
from jax.experimental import pallas as pl
from jax.experimental.pallas import tpu as pltpu
from jax.sharding import PartitionSpec as P

STEPS = 2
NODES = 125
RIM = 32
SHEET = 32
FACES = 6
F32, BF16, I32 = jnp.float32, jnp.bfloat16, jnp.int32
partner_face = (1, 0, 3, 2, 5, 4)

VMEM = pl.BlockSpec(memory_space=pltpu.VMEM)
SMEM = pl.BlockSpec(memory_space=pltpu.SMEM)
HBM = pl.BlockSpec(memory_space=pltpu.HBM)
PARAMS = pltpu.CompilerParams(vmem_limit_bytes=40 * 2**20)


def shape(*dims, dtype=F32):
    return jax.ShapeDtypeStruct(dims, dtype)


def iota(dims, axis):
    return lax.broadcasted_iota(I32, dims, axis)


def halves(x):
    high = x.astype(BF16)
    return high, (x - high.astype(F32)).astype(BF16)


def dot(a, b):
    return lax.dot_general(a, b, (((1,), (0,)), ((), ())), preferred_element_type=F32)


def face_nodes(dims, axis):
    row = iota(dims, axis)
    face, q = row // SHEET, row % SHEET
    a = sum((q >= 5 * i).astype(I32) for i in range(1, 5))
    b = q - 5 * a
    node = jnp.where(face == 0, q, q + 100)
    node = jnp.where(face == 2, 25 * a + b, node)
    node = jnp.where(face == 3, 25 * a + 20 + b, node)
    node = jnp.where(face == 4, 5 * q, node)
    node = jnp.where(face == 5, 5 * q + 4, node)
    return jnp.where(q < 25, node, -1)


def picker():
    dims = (FACES * SHEET, 128)
    return jnp.where(face_nodes(dims, 0) == iota(dims, 1), 1.0, 0.0).astype(BF16)


def lifter():
    dims = (128, FACES * SHEET)
    return jnp.where(face_nodes(dims, 1) == iota(dims, 0), 1.0, 0.0).astype(BF16)


def rows_of(ref):
    return ref.reshape(3 * NODES, 128)


def padded(ref, c):
    rows = rows_of(ref)[NODES * c : NODES * (c + 1)]
    return jnp.concatenate([rows, jnp.zeros((128 - NODES, 128), F32)], axis=0)


def stacked(fields):
    high, low = halves(jnp.concatenate(fields, axis=1))
    return jnp.concatenate([high, low], axis=0)


def pack_rim(fields):
    lane = iota((128, 128), 1)
    out = fields[0]
    for k in range(1, len(fields)):
        out = jnp.where(lane < RIM * k, out, pltpu.roll(fields[k], RIM * k, 1))
    return jnp.where(lane < RIM * len(fields), out, 0.0)


def fold(x):
    return jnp.where(iota((64, 128), 1) < 64, x[:64], pltpu.roll(x[64:], 64, 1))


def live_mask(count_ref):
    return (iota((128, 128), 1) < count_ref[0, 0]).astype(F32)


def edge_row(smooth_ref):
    width = smooth_ref.shape[1]
    last = jnp.broadcast_to(smooth_ref[:, width - 1 : width], (4, 128))
    first = jnp.broadcast_to(smooth_ref[:, 0:1], (4, 128))
    lane, row = iota((4, 128), 1), iota((4, 128), 0)
    spread = jnp.where(lane == row, last, 0.0) + jnp.where(lane == row + 4, first, 0.0)
    return jnp.sum(spread, axis=0, keepdims=True)


def copies_of(sources, targets, sems):
    copies = [pltpu.make_async_copy(a, b, sems.at[i]) for i, (a, b) in enumerate(zip(sources, targets))]
    for copy in copies:
        copy.start()
    return copies


def pack_kernel(count_ref, forward_ref, adjoint_ref, smooth_ref, rim_ref, field_ref, smooth_out_ref, *held):
    copies = copies_of((forward_ref, adjoint_ref, smooth_ref), (*held[:2], smooth_out_ref), held[2])
    live = live_mask(count_ref)
    fields = []
    for ref, copy in zip(held[:2], copies):
        copy.wait()
        fields += [padded(ref, c) * live for c in range(3)]
    rim_ref[:128] = pack_rim(fields[:4])
    rim_ref[128:192] = fold(pack_rim(fields[4:]))
    for k in range(6):
        field_ref[k] = fields[k]
    copies[2].wait()
    rim_ref[192:] = jnp.broadcast_to(edge_row(smooth_out_ref), (8, 128))


def split_stiffness(stiff_ref):
    wide = jnp.concatenate([stiff_ref[...], jnp.zeros((NODES, 128 - NODES), F32)], axis=1)
    return halves(jnp.concatenate([wide, jnp.zeros((128 - NODES, 128), F32)], axis=0))


def columns(x):
    return [x[:, 128 * k : 128 * (k + 1)] for k in range(x.shape[1] // 128)]


def strains(high, low, x):
    return columns(dot(jnp.concatenate([high, high], axis=1), x) + dot(low, x[:128]))


def faces_of(pick, x):
    return columns(dot(jnp.concatenate([pick, pick], axis=1), x))


def take(x, index):
    return jnp.take_along_axis(x, index, axis=1, mode="promise_in_bounds")


def lift_of(lift, jumps):
    high, low = halves(jnp.concatenate([jnp.concatenate(j, axis=0) for j in jumps], axis=1))
    return columns(dot(lift, high) + dot(lift, low))


def own_jumps(near_ref, own):
    jumps = [[] for _ in own]
    for face in range(FACES):
        p = partner_face[face]
        near = jnp.broadcast_to(near_ref[face], (SHEET, 128))
        home = near // 128 == lax.axis_index("mesh")
        slot = near % 128
        for k in range(len(own)):
            here = take(own[k][SHEET * p : SHEET * (p + 1)], slot)
            jumps[k].append(jnp.where(home, here, 0.0) - own[k][SHEET * face : SHEET * (face + 1)])
    return jumps


def rim_jumps(near_ref, rims, n):
    mine, parts = lax.axis_index("mesh"), lax.axis_size("mesh")
    follower = jnp.where(mine + 1 == parts, 0, mine + 1)
    jumps = [[] for _ in range(n)]
    for face in range(FACES):
        p = partner_face[face]
        near = jnp.broadcast_to(near_ref[face], (SHEET, 128))
        target = near // 128
        away = target != mine
        index = near % RIM + jnp.where(target == follower, 64, 0)
        for k in range(n):
            across = take(rims[k // 2][SHEET * p : SHEET * (p + 1)], index + RIM * (k % 2))
            jumps[k].append(jnp.where(away, across, 0.0))
    return jumps


def merge(before, after):
    lane = iota(before.shape, 1)
    first = jnp.where(lane < 64, before, pltpu.roll(after, 64, 1))
    second = jnp.where(lane < 64, pltpu.roll(before, 64, 1), after)
    return first, second


def own_kernel(
    count_ref, field_ref, smooth_ref, near_in, stiff_in, material_in, project_in, destination_in,
    partial_ref, kernel_ref, turned_ref, stiff_out_ref, pick_ref, lift_ref, project_out_ref, wanted_ref, near_ref,
    material_ref, stiff_ref, project_ref, destination_ref, sems,
):
    copies = copies_of(
        (near_in, stiff_in, material_in, project_in, destination_in),
        (near_ref, stiff_ref, material_ref, project_ref, destination_ref),
        sems,
    )
    live = live_mask(count_ref)
    fields = [field_ref[k] for k in range(6)]
    pick, lift = picker(), lifter()
    pick_ref[...] = pick
    lift_ref[...] = lift
    x = stacked(fields)
    faces = faces_of(pick, x)
    copies[0].wait()
    lifted = lift_of(lift, own_jumps(near_ref, faces))
    for copy in copies[1:]:
        copy.wait()
    material = jnp.broadcast_to(material_ref[...], (128, 128))
    high, low = split_stiffness(stiff_ref)
    stiff_out_ref[0] = high
    stiff_out_ref[1] = low
    strain = strains(high, low, x)
    for k in range(6):
        force = 0.5 * lifted[k] - material * strain[k]
        partial_ref[k] = live * (fields[k] + 0.4 * force)
    kernel_ref[...] = sum(fields[c] * strain[3 + c] for c in range(3))
    high, low = halves(jnp.concatenate([project_ref[...], jnp.zeros((64, 128 - NODES), F32)], axis=1))
    project_out_ref[0] = high
    project_out_ref[1] = low
    wanted_ref[...] = jnp.broadcast_to(destination_ref[...].astype(F32), (8, 128))
    width = smooth_ref.shape[1]
    wide = jnp.concatenate([smooth_ref[...], jnp.zeros((4, 128 - width), F32)], axis=1)
    turned_ref[...] = jnp.concatenate([wide, jnp.zeros((124, 128), F32)], axis=0).T[:8]


def step_kernel(
    scale, n_mesh,
    count_ref, partial_ref, kernel_ref, after_ref, before_ref, near_ref, stiff_ref, pick_ref, lift_ref,
    project_ref, wanted_ref,
    forward_ref, strain_ref, rim_ref, edge_ref, chunk_ref,
):
    live = live_mask(count_ref)
    first, second = merge(before_ref[:128], after_ref[:128])
    upper, lower = merge(before_ref[128:192], after_ref[128:192])
    rims = faces_of(pick_ref[...], stacked([first, second, jnp.concatenate([upper, lower], axis=0)]))
    lift = lift_of(lift_ref[...], rim_jumps(near_ref, rims, 6))
    fields = [partial_ref[k] + live * (0.2 * lift[k]) for k in range(6)]
    strain = strains(stiff_ref[0], stiff_ref[1], stacked(fields))
    kernel = kernel_ref[...] + sum(fields[c] * strain[3 + c] for c in range(3))
    k_high, k_low = halves(kernel)
    p_high, p_low = project_ref[0], project_ref[1]
    blocks = dot(jnp.concatenate([p_high, p_high], axis=1), jnp.concatenate([k_high, k_low], axis=0))
    blocks = (blocks + dot(p_low, k_high)) * scale
    for m in range(n_mesh):
        chunk_ref[m, :64] = blocks
        chunk_ref[m, 64:] = wanted_ref[...]
    rim_ref[...] = pack_rim(fields[:3])
    edge_ref[...] = jnp.where(iota((8, 128), 1) < 4, before_ref[192:], after_ref[192:])
    for c in range(3):
        forward_ref[c] = fields[c]
        strain_ref[c] = strain[c]


def dense_kernel(n_event, n_mesh, tile_width, first, parts_ref, edge_ref, after_ref, out_ref):
    rows = 8 * n_event
    row = iota((rows, 128), 0)
    tile = (row % n_event + first) % n_event * (n_mesh * tile_width) + row // n_event - 2
    tile = tile.astype(F32) + (lax.axis_index("mesh") * tile_width).astype(F32)
    left, right = [], []
    for m in range(n_mesh):
        left.append(jnp.concatenate(halves(parts_ref[m, :64]), axis=0))
        wanted = jnp.broadcast_to(parts_ref[m, 64:65], (rows, 128))
        right.append(jnp.where(wanted == tile, 1.0, 0.0).astype(BF16))
    left, right = jnp.concatenate(left, axis=1), jnp.concatenate(right, axis=1)
    both = lax.dot_general(left, right, (((1,), (1,)), ((), ())), preferred_element_type=F32)
    both = both[:64] + both[64:]
    half = 4 * n_event
    both = jnp.concatenate([both[:, :half], both[:, half:]], axis=0).T
    for j in range(4):
        out_ref[pl.ds(j, n_event, stride=5)] = both[n_event * j : n_event * (j + 1)]
    lane, event = iota((n_event, 128), 1), (iota((n_event, 128), 0) + first) % n_event
    apart = event - lax.axis_index("event")
    used = ((apart == 1) & (lane < 4)) | ((apart == -1) & (lane >= 4) & (lane < 8))
    edges = jnp.where(used, jnp.broadcast_to(edge_ref[0:1], (n_event, 128)), 0.0)
    out_ref[pl.ds(4, n_event, stride=5)] = edges


def last_kernel(
    count_ref, field_ref, one_ref, strain_ref, after_ref, before_ref, near_ref, material_ref, pick_ref, lift_ref,
    turned_ref, edge_ref,
    final_ref, table_ref, open_ref,
):
    live = live_mask(count_ref)
    material = jnp.broadcast_to(material_ref[...], (128, 128))
    fields = [one_ref[c] for c in range(3)]
    jumps = own_jumps(near_ref, faces_of(pick_ref[...], stacked(fields)))
    rims = faces_of(pick_ref[...], stacked(list(merge(before_ref[...], after_ref[...]))))
    more = rim_jumps(near_ref, rims, 3)
    lift = lift_of(lift_ref[...], [[a + b for a, b in zip(*pair)] for pair in zip(jumps, more)])
    final = rows_of(final_ref)
    for c in range(3):
        force = 0.5 * lift[c] - material * strain_ref[c]
        out = live * (2.0 * fields[c] - field_ref[c] + 0.4 * force)
        final[NODES * c : NODES * (c + 1)] = out[:NODES]
    mine, parts = lax.axis_index("mesh"), lax.axis_size("mesh")
    tile = iota((8, 128), 0)
    is_open = ((tile == 1) & (mine == 0)) | ((tile == 6) & (mine == parts - 1))
    edge = jnp.where(tile == 6, pltpu.roll(edge_ref[...], 124, 1), edge_ref[...])
    edge = jnp.where(((tile == 1) | (tile == 6)) & ~is_open, edge, 0.0)
    table_ref[...] = jnp.where((tile >= 2) & (tile < 6), pltpu.roll(turned_ref[...], 2, 0), edge)
    open_ref[...] = is_open.astype(F32)


def total_of(parts):
    while len(parts) > 1:
        parts = [sum(parts[i : i + 2][1:], parts[i]) for i in range(0, len(parts), 2)]
    return parts[0]


def smooth_kernel(n_event, x_ref, table_ref, open_ref, o_ref):
    node, tile = iota((8, 128), 1), iota((8, 128), 0)
    span = 40 if n_event % 8 == 0 else 5 * n_event
    total = total_of([x_ref[i : i + span] for i in range(0, 5 * n_event, span)])
    total = total_of([total[i : i + 5] for i in range(0, span, 5)])
    edge = jnp.broadcast_to(total[4:5], (8, 128))
    edge = jnp.where(tile == 6, pltpu.roll(edge, 124, 1), edge)
    table = table_ref[...] + open_ref[...] * edge
    coef = [jnp.broadcast_to(table[:, d : d + 1], (8, 128)) for d in range(4)]
    total = total[:4]
    x = jnp.concatenate([total, pltpu.roll(total, 64, 1)], axis=0)
    for _ in range(2):
        right = jnp.where(tile < 7, pltpu.roll(x, 7, 0), 0.0)
        left = jnp.where(tile > 0, pltpu.roll(x, 1, 0), 0.0)
        out = x + coef[0] * (left + right - 2.0 * x)
        for d, shift in ((1, 4), (2, 2), (3, 0)):
            place, stride = (node >> shift) & 3, 1 << shift
            up = jnp.where(place < 3, pltpu.roll(x, 128 - stride, 1), 0.0)
            down = jnp.where(place > 0, pltpu.roll(x, stride, 1), 0.0)
            out = out + coef[d] * (up + down - 2.0 * x)
        x = out
    o_ref[...] = x[2:6, :64]


def call(kernel, out_shape, n_smem, n_vmem, n_hbm=0, scratch=()):
    many = isinstance(out_shape, tuple)
    return pl.pallas_call(
        kernel,
        out_shape=out_shape,
        in_specs=[SMEM] * n_smem + [VMEM] * n_vmem + [HBM] * n_hbm,
        out_specs=(VMEM,) * len(out_shape) if many else VMEM,
        scratch_shapes=scratch,
        compiler_params=PARAMS,
    )


def per_device(
    forward_start, adjoint_start, stiffness, projection, material, neighbours, destinations, counts, smoothing
):
    elements = forward_start.shape[-1]
    tile_width = smoothing.shape[1]
    n_mesh, n_event = lax.axis_size("mesh"), lax.axis_size("event")
    scale = math.sqrt(tile_width / elements) / STEPS
    forward, adjoint = (x.reshape(3, NODES, 1, 128) for x in (forward_start, adjoint_start))
    up = [(i, (i + 1) % n_mesh) for i in range(n_mesh)]
    down = [(j, i) for i, j in up]
    first_mesh, first_event = 5 * n_mesh // 8, n_event // 2
    mesh_group = [(i + first_mesh) % n_mesh for i in range(n_mesh)]
    event_group = [(i + first_event) % n_event for i in range(n_event)]

    near, project = neighbours.reshape(FACES, 1, 128), projection.T
    inputs = (forward, adjoint, smoothing, near, stiffness, material, project, destinations)
    inputs = [pltpu.with_memory_space_constraint(x, pltpu.HBM) for x in inputs]
    rim, fields, smooth_in = call(
        pack_kernel,
        (shape(200, 128), shape(6, 128, 128), shape(4, tile_width)),
        1,
        0,
        3,
        [pltpu.VMEM(x.shape, F32) for x in (forward, adjoint)] + [pltpu.SemaphoreType.DMA((3,))],
    )(counts, *inputs[:3])
    after, before = lax.ppermute(rim, "mesh", down), lax.ppermute(rim, "mesh", up)
    partial, kernel, turned, stiff, pick, lift, project, wanted, near, material = call(
        own_kernel,
        (
            shape(6, 128, 128),
            shape(128, 128),
            shape(8, 128),
            shape(2, 128, 128, dtype=BF16),
            shape(FACES * SHEET, 128, dtype=BF16),
            shape(128, FACES * SHEET, dtype=BF16),
            shape(2, 64, 128, dtype=BF16),
            shape(8, 128),
            shape(FACES, 1, 128, dtype=I32),
            shape(1, 128),
        ),
        1,
        2,
        5,
        [pltpu.VMEM(x.shape, x.dtype) for x in (stiffness, project, destinations)] + [pltpu.SemaphoreType.DMA((5,))],
    )(counts, fields, smooth_in, *inputs[3:])

    def one_step(*refs):
        step_kernel(scale, n_mesh, *refs)

    one, strain, rim_one, edge, chunk = call(
        one_step,
        (shape(3, 128, 128), shape(3, 128, 128), shape(128, 128), shape(8, 128), shape(n_mesh, 72, 128)),
        1,
        10,
    )(counts, partial, kernel, after, before, near, stiff, pick, lift, project, wanted)
    parts = lax.all_to_all(chunk, "mesh", 0, 0, tiled=True, axis_index_groups=[mesh_group])

    after = lax.ppermute(rim_one, "mesh", down)

    def dense(*refs):
        dense_kernel(n_event, n_mesh, tile_width, first_event, *refs)

    partial = call(dense, shape(5 * n_event, 128), 0, 3)(parts, edge, after)
    pieces = lax.all_to_all(partial.reshape(-1, 1, 128), "event", 0, 0, tiled=True, axis_index_groups=[event_group])
    rim_one, _ = lax.optimization_barrier((rim_one, partial))
    before = lax.ppermute(rim_one, "mesh", up)
    final, table, is_open = call(last_kernel, (shape(3, NODES, 1, 128), shape(8, 128), shape(8, 128)), 1, 11)(
        counts, fields, one, strain, after, before, near, material, pick, lift, turned, edge
    )

    def smooth(*refs):
        smooth_kernel(n_event, *refs)

    tiles = call(smooth, shape(tile_width, 64), 0, 3)(pieces.reshape(-1, 128), table, is_open)
    return final.reshape(1, 3, NODES, 128), tiles.T


def solution(mesh):
    in_specs = (
        P("event", None, None, "mesh"),
        P("event", None, None, "mesh"),
        P(),
        P(),
        P("event", "mesh"),
        P("event", None, "mesh"),
        P("event", "mesh"),
        P("event", "mesh"),
        P(None, ("event", "mesh")),
    )
    out_specs = (P("event", None, None, "mesh"), P(None, ("event", "mesh")))
    return jax.shard_map(per_device, mesh=mesh, in_specs=in_specs, out_specs=out_specs, check_vma=False)
```
